32 devices in a mesh: seq: 8 (over z, y), head: 2 (over x), sample: 2 (over core).
Axes of the slice: x: 2, y: 2, z: 4, core: 2. Of those that a mesh axis runs over, the one named last changes fastest.
Arguments:
- features: bfloat16 [2, 2048, 1536], P('sample', 'seq'), may hold values from -6 to 6
- dilated_weight: bfloat16 [1536, 3, 768], P(None, None, 'head'), may hold values from -0.09375 to 0.09375
- point_weight: bfloat16 [1536, 768], P(None, 'head'), may hold values from -0.21875 to 0.21875
- track_weight: bfloat16 [1536, 3840], P('sample', 'head'), may hold values from -0.15625 to 0.15625
- track_cotangent: bfloat16 [2, 2048, 3840], P('sample', 'seq', 'head'), may hold values from -6 to 6
Outputs:
- input_grad: bfloat16 [2, 2048, 1536], P('sample', 'seq')
- dilated_grad: float32 [1536, 3, 768], P(('seq', 'sample'), None, 'head')
- point_grad: float32 [1536, 768], P(('seq', 'sample'), 'head')
The draws below stay inside these ranges and needn't reach their ends.
All inputs are finite; a program needn't handle non-finite values.
Results may differ from the reference program's by a relative error of at most 0.015.
Values may be sent and summed in bfloat16 or wider, within the bound.
No kernel may reach another device: no remote copies, remote signals or barrier semaphores. Data moves between devices by JAX's collectives and lax.ppermute only.
A program may use at most 128 MiB of HBM per device.

```python
import jax
import jax.numpy as jnp
from jax import lax

C = 1536
F = 768
TRACKS = 3840
DILATION_STEP = 1024
L = 2048
BATCH = 2
N_HEAD = 2


def spiked(drawn, key, source, target, blocks, factor):
    def block_of(axis_at):
        return (jnp.arange(drawn.shape[axis_at]) // (drawn.shape[axis_at] // blocks)).reshape((-1,) + (1,) * (drawn.ndim - 1 - axis_at))

    one_side = jax.random.permutation(key, blocks)[block_of(target)]
    far = (block_of(target) + blocks // 2) % blocks
    return jnp.where((block_of(source) == one_side) | (block_of(source) == far), factor * drawn, drawn)


def block_levels(stream_key, extent, split, smallest, top_value):
    def one(axis_at, blocks):
        heights = jax.random.uniform(jax.random.fold_in(jax.random.fold_in(stream_key, 6), axis_at), (blocks,), jnp.float32, smallest / len(split), top_value / len(split))
        return jnp.repeat(jnp.exp(heights), extent[axis_at] // blocks).reshape((-1,) + (1,) * (len(extent) - axis_at - 1))

    gain = one(*split[0])
    for cut in split[1:]:
        gain = gain * one(*cut)
    return gain


def noise(rng, shape, spread, most, cuts=(), kind=jnp.bfloat16):
    drawn = spread * jax.random.normal(rng, shape, jnp.float32)
    if cuts:
        drawn = drawn * block_levels(rng, shape, cuts, -0.22, 0.18)
    return jnp.clip(drawn, -most, most).astype(kind)


def gaussian_with(key, extent, width, reach, cuts, heavy, kind=jnp.bfloat16):
    entries = width * jax.random.normal(key, extent, jnp.float32)
    if cuts:
        entries = entries * block_levels(key, extent, cuts, -0.22, 0.18)
    return jnp.clip(spiked(entries, jax.random.fold_in(key, 3), *heavy), -reach, reach).astype(kind)


def setup_inputs(seed: int = 0) -> dict:
    seeds = jax.random.split(jax.random.key(seed), 6)
    return {
        "features": gaussian_with(seeds[0], (BATCH, L, C), 1.0, 6.0, ((0, 2), (1, 8)), (1, 2, 8, 2.0)),
        "dilated_weight": noise(seeds[1], (C, 3, F), (3 * C) ** -0.5, 0.09375, ((2, 2),)),
        "point_weight": noise(seeds[2], (C, F), F ** -0.5, 0.21875, ((1, 2),)),
        "track_weight": noise(seeds[3], (C, TRACKS), C ** -0.5, 0.15625, ((0, 2), (1, 2))),
        "track_cotangent": noise(seeds[4], (BATCH, L, TRACKS), 1.0, 6.0, ((0, 2), (1, 8), (2, 2))),
    }


def gelu_value(value):
    inner = 0.7978845608 * (value + 0.044715 * value * value * value)
    return 0.5 * value * (1.0 + jnp.tanh(inner))


def gelu_slope(value):
    inner = 0.7978845608 * (value + 0.044715 * value * value * value)
    tangent = jnp.tanh(inner)
    return 0.5 * (1.0 + tangent) + 0.5 * value * (1.0 - tangent * tangent) * 0.7978845608 * (1.0 + 3.0 * 0.044715 * value * value)


def shifted_input(field, amount):
    empty = jnp.zeros((abs(amount),) + field.shape[1:], field.dtype)
    if amount > 0:
        return jnp.concatenate([empty, field[:-amount]], axis=0)
    return jnp.concatenate([field[-amount:], empty], axis=0)


def rounded(value):
    return lax.optimization_barrier(value.astype(jnp.bfloat16)).astype(jnp.float32)


def one_sample(features, track_cotangent, dilated_weight, point_weight, track_weight):
    feat_wide = features.astype(jnp.float32)
    activated_hidden = gelu_value(feat_wide).astype(jnp.bfloat16)
    preceding_value = shifted_input(activated_hidden, DILATION_STEP)
    following_value = shifted_input(activated_hidden, -DILATION_STEP)
    middle = jnp.dot(preceding_value, dilated_weight[:, 0, :], preferred_element_type=jnp.float32)
    middle = middle + jnp.dot(activated_hidden, dilated_weight[:, 1, :], preferred_element_type=jnp.float32)
    middle = middle + jnp.dot(following_value, dilated_weight[:, 2, :], preferred_element_type=jnp.float32)
    hidden = gelu_value(middle).astype(jnp.bfloat16)
    group_width = F // N_HEAD
    track_width = TRACKS // N_HEAD
    summed = feat_wide
    for group in range(N_HEAD):
        lower = group * group_width
        part = jnp.dot(hidden[:, lower:lower + group_width], point_weight[:, lower:lower + group_width].T, preferred_element_type=jnp.float32)
        summed = summed + rounded(part)
    block_out = summed.astype(jnp.bfloat16)
    scores = jnp.dot(block_out, track_weight, preferred_element_type=jnp.float32)
    score_grad = (track_cotangent.astype(jnp.float32) * jax.nn.sigmoid(scores)).astype(jnp.bfloat16)
    out_grad = jnp.zeros(feat_wide.shape, jnp.float32)
    for group in range(N_HEAD):
        lower = group * track_width
        part = jnp.dot(score_grad[:, lower:lower + track_width], track_weight[:, lower:lower + track_width].T, preferred_element_type=jnp.float32)
        out_grad = out_grad + rounded(part)
    out_grad_b = out_grad.astype(jnp.bfloat16)
    hidden_grad = jnp.dot(out_grad_b, point_weight, preferred_element_type=jnp.float32)
    middle_gradient = (hidden_grad * gelu_slope(middle)).astype(jnp.bfloat16)
    kernel_taps = jnp.stack([shifted_input(middle_gradient, -DILATION_STEP), middle_gradient, shifted_input(middle_gradient, DILATION_STEP)], axis=1)
    positions = kernel_taps.shape[0]
    dilated_grad = jnp.dot(activated_hidden.T, kernel_taps.reshape(positions, 3 * F), preferred_element_type=jnp.float32).reshape(C, 3, F)
    point_grad = jnp.dot(out_grad_b.T, hidden, preferred_element_type=jnp.float32)
    act_grad = jnp.zeros(feat_wide.shape, jnp.float32)
    for group in range(N_HEAD):
        lower = group * group_width
        tap_group = kernel_taps[:, :, lower:lower + group_width].reshape(positions, 3 * group_width)
        weight_group = dilated_weight[:, :, lower:lower + group_width].reshape(C, 3 * group_width)
        act_grad = act_grad + rounded(jnp.dot(tap_group, weight_group.T, preferred_element_type=jnp.float32))
    input_grad = (out_grad + act_grad * gelu_slope(feat_wide)).astype(jnp.bfloat16)
    return input_grad, dilated_grad, point_grad


def reference(features, dilated_weight, point_weight, track_weight, track_cotangent):
    def single(pair):
        return one_sample(pair[0], pair[1], dilated_weight, point_weight, track_weight)

    input_grad, dilated_grad, point_grad = lax.map(single, (features, track_cotangent))
    return input_grad, jnp.sum(dilated_grad, axis=0), jnp.sum(point_grad, axis=0)
```

```python
import jax
import jax.numpy as jnp
from jax import lax
from jax.sharding import PartitionSpec as P

DILATION_STEP = 1024
BF16 = jnp.bfloat16
F32 = jnp.float32


def gelu_value(value):
    inner = 0.7978845608 * (value + 0.044715 * value * value * value)
    return 0.5 * value * (1.0 + jnp.tanh(inner))


def gelu_slope(value):
    inner = 0.7978845608 * (value + 0.044715 * value * value * value)
    tangent = jnp.tanh(inner)
    return 0.5 * (1.0 + tangent) + 0.5 * value * (1.0 - tangent * tangent) * 0.7978845608 * (
        1.0 + 3.0 * 0.044715 * value * value
    )


def dot(left, right, contract):
    return lax.dot_general(left, right, (contract, ((), ())), preferred_element_type=F32)


def flip(value, axis, step=1):
    count = lax.axis_size(axis)
    return lax.ppermute(value, axis, [(i, i ^ step) for i in range(count)])


def own_first(value, axis_at, bit):
    return (
        lax.dynamic_index_in_dim(value, bit, axis_at, keepdims=False),
        lax.dynamic_index_in_dim(value, 1 - bit, axis_at, keepdims=False),
    )


def in_order(own, other, bit, axis):
    first = jnp.where(bit == 0, own, other)
    second = jnp.where(bit == 0, other, own)
    return jnp.concatenate([first, second], axis=axis)


def bits_of(count):
    return count.bit_length() - 1


def body(features, dilated_weight, point_weight, track_weight, track_cotangent):
    samples, positions, channels = features.shape
    rows = samples * positions
    half = rows // 2
    width = dilated_weight.shape[2]
    n_seq, n_sample = lax.axis_size("seq"), lax.axis_size("sample")
    seq, head, sample = lax.axis_index("seq"), lax.axis_index("head"), lax.axis_index("sample")
    dist = DILATION_STEP // positions
    one_sided = n_seq == 2 * dist
    low = seq < dist
    taps = jnp.transpose(dilated_weight, (1, 0, 2))

    if one_sided:
        outer_weights = [lax.dynamic_index_in_dim(taps, jnp.where(low, 0, 2), 0, keepdims=False)]
        pairs = [(i, (i + dist) % n_seq) for i in range(n_seq)]
        forward, backward = [pairs], [pairs]
    else:
        outer_weights = [taps[0], taps[2]]
        up = [(i, i + dist) for i in range(n_seq - dist)]
        down = [(i + dist, i) for i in range(n_seq - dist)]
        forward, backward = [up, down], [down, up]
    count = len(outer_weights)

    whole_track = lax.all_gather(track_weight, "sample", axis=0, tiled=True)
    piece = channels // n_sample
    own_piece = lax.dynamic_slice_in_dim(point_weight, sample * piece, piece, 0)
    other_point = lax.all_gather(flip(own_piece, "head"), "sample", axis=0, tiled=True)

    feat = features.reshape(rows, channels)
    feat_wide = feat.astype(F32)
    activated = gelu_value(feat_wide).astype(BF16)
    sent = [dot(activated, weight, ((1,), (0,))).astype(BF16) for weight in outer_weights]
    arrived = [lax.ppermute(term, "seq", pairs) for term, pairs in zip(sent, forward)]
    middle = dot(activated, taps[1], ((1,), (0,)))
    for term in arrived:
        middle = middle + term.astype(F32)
    middle_b = middle.astype(BF16)
    other_middle = flip(middle_b, "head")
    hidden = gelu_value(middle).astype(BF16)
    other_hidden = gelu_value(other_middle.astype(F32)).astype(BF16)
    block_out = (
        feat_wide
        + dot(hidden, point_weight, ((1,), (1,)))
        + dot(other_hidden, other_point, ((1,), (1,)))
    ).astype(BF16)

    def rows_of(value, which):
        return lax.dynamic_slice_in_dim(value, which * half, half, 0)

    cotangent = track_cotangent.reshape(rows, whole_track.shape[1])

    def track_part(which):
        scores = dot(rows_of(block_out, which), whole_track, ((1,), (0,)))
        grad = (rows_of(cotangent, which).astype(F32) * jax.nn.sigmoid(scores)).astype(BF16)
        return dot(grad, whole_track, ((1,), (1,)))

    theirs = flip(track_part(1 - head).astype(BF16), "head")
    out_grad = track_part(head) + theirs.astype(F32)
    out_grad_b = out_grad.astype(BF16)
    other_out_grad = flip(out_grad_b, "head")

    grad_own = (
        dot(out_grad_b, point_weight, ((1,), (0,))) * gelu_slope(rows_of(middle, head))
    ).astype(BF16)
    grad_other = (
        dot(out_grad_b, other_point, ((1,), (0,)))
        * gelu_slope(rows_of(other_middle, head).astype(F32))
    ).astype(BF16)
    middle_grad = in_order(grad_own, flip(grad_other, "head"), head, 0)
    moved = []
    for pairs in backward:
        straight = lax.ppermute(grad_own, "seq", pairs)
        crossed = lax.ppermute(
            grad_other,
            ("seq", "head"),
            [(2 * i + k, 2 * j + 1 - k) for i, j in pairs for k in range(2)],
        )
        moved.append(in_order(straight, crossed, head, 0))

    act_part = dot(middle_grad, taps[1], ((1,), (1,)))
    for field, weight in zip(moved, outer_weights):
        act_part = act_part + dot(field, weight, ((1,), (1,)))
    act_theirs = flip(rows_of(act_part, 1 - head).astype(BF16), "head")
    act_grad = rows_of(act_part, head) + act_theirs.astype(F32)
    input_half = (out_grad + act_grad * gelu_slope(rows_of(feat_wide, head))).astype(BF16)
    input_grad = in_order(input_half, flip(input_half, "head"), head, 0)

    seq_bits = bits_of(n_seq)
    block = channels // (n_seq * n_sample)
    shape = (2,) * seq_bits + (n_sample, block)

    def halve(value, left, bit, keep_last=False):
        at = left.index(bit)
        if bit < 0:
            mine, give = own_first(value, at, sample)
            got = flip(give.astype(BF16), "sample")
        else:
            mine, give = own_first(value, at, (seq >> bit) & 1)
            got = flip(give.astype(BF16), "seq", 1 << bit)
        rest = [b for b in left if b != bit]
        return (mine, got, rest) if keep_last else (mine.astype(F32) + got.astype(F32), rest)

    def reduced(value, order, apart=False):
        left = list(range(seq_bits - 1, -1, -1)) + [-1]
        value = value.reshape(shape + value.shape[1:])
        for bit in order[:-1]:
            value, left = halve(value, left, bit)
            value = value.astype(BF16)
        mine, got, _ = halve(value, left, order[-1], True)
        if apart:
            return mine.astype(F32), got.astype(F32)
        return mine.astype(F32) + got.astype(F32)

    order_a = [-1] + list(range(seq_bits))
    order_b = [-1] + list(range(1, seq_bits - 1)) + [0, seq_bits - 1]
    whole_out_grad = in_order(out_grad_b, other_out_grad, head, 0)
    point_grad = reduced(dot(whole_out_grad, hidden, ((0,), (0,))), order_a)
    mid_tap = reduced(dot(activated, middle_grad, ((0,), (0,))), order_b)
    if one_sided:
        mine, got = reduced(dot(activated, moved[0], ((0,), (0,))), order_a, True)
        outer = [jnp.where(low, mine, got), jnp.where(low, got, mine)]
    else:
        outer = [reduced(dot(activated, field, ((0,), (0,))), order_a) for field in moved]
    dilated_grad = jnp.transpose(jnp.stack([outer[0], mid_tap, outer[1]]), (1, 0, 2))
    return (input_grad.reshape(samples, positions, channels), dilated_grad, point_grad)


def solution(mesh):
    placed = (
        P("sample", "seq", None),
        P(None, None, "head"),
        P(None, "head"),
        P("sample", "head"),
        P("sample", "seq", "head"),
    )
    return jax.shard_map(
        body,
        mesh=mesh,
        in_specs=placed,
        out_specs=(
            P("sample", "seq", None),
            P(("seq", "sample"), None, "head"),
            P(("seq", "sample"), "head"),
        ),
        check_vma=False,
    )
```

```python
import jax
import jax.numpy as jnp
from jax import lax
from jax.experimental import pallas as pl
from jax.experimental.pallas import tpu as pltpu
from jax.sharding import PartitionSpec as P

DILATION_STEP = 1024
BF16 = jnp.bfloat16
F32 = jnp.float32
VMEM = 40 * 2**20


def gelu_value(value):
    inner = 0.7978845608 * (value + 0.044715 * value * value * value)
    return 0.5 * value * (1.0 + jnp.tanh(inner))


def gelu_slope(value):
    inner = 0.7978845608 * (value + 0.044715 * value * value * value)
    tangent = jnp.tanh(inner)
    return 0.5 * (1.0 + tangent) + 0.5 * value * (1.0 - tangent * tangent) * 0.7978845608 * (
        1.0 + 3.0 * 0.044715 * value * value
    )


def dot(left, right, contract):
    return lax.dot_general(left, right, (contract, ((), ())), preferred_element_type=F32)


def flip(value, axis, step=1):
    count = lax.axis_size(axis)
    return lax.ppermute(value, axis, [(i, i ^ step) for i in range(count)])


def own_first(value, axis_at, bit):
    return (
        lax.dynamic_index_in_dim(value, bit, axis_at, keepdims=False),
        lax.dynamic_index_in_dim(value, 1 - bit, axis_at, keepdims=False),
    )


def in_order(own, other, bit, axis):
    first = jnp.where(bit == 0, own, other)
    second = jnp.where(bit == 0, other, own)
    return jnp.concatenate([first, second], axis=axis)


def bits_of(count):
    return count.bit_length() - 1


def general(features, dilated_weight, point_weight, track_weight, track_cotangent):
    samples, positions, channels = features.shape
    rows = samples * positions
    half = rows // 2
    width = dilated_weight.shape[2]
    n_seq, n_sample = lax.axis_size("seq"), lax.axis_size("sample")
    seq, head, sample = lax.axis_index("seq"), lax.axis_index("head"), lax.axis_index("sample")
    dist = DILATION_STEP // positions
    one_sided = n_seq == 2 * dist
    low = seq < dist
    taps = jnp.transpose(dilated_weight, (1, 0, 2))

    if one_sided:
        outer_weights = [lax.dynamic_index_in_dim(taps, jnp.where(low, 0, 2), 0, keepdims=False)]
        pairs = [(i, (i + dist) % n_seq) for i in range(n_seq)]
        forward, backward = [pairs], [pairs]
    else:
        outer_weights = [taps[0], taps[2]]
        up = [(i, i + dist) for i in range(n_seq - dist)]
        down = [(i + dist, i) for i in range(n_seq - dist)]
        forward, backward = [up, down], [down, up]
    count = len(outer_weights)

    whole_track = lax.all_gather(track_weight, "sample", axis=0, tiled=True)
    piece = channels // n_sample
    own_piece = lax.dynamic_slice_in_dim(point_weight, sample * piece, piece, 0)
    other_point = lax.all_gather(flip(own_piece, "head"), "sample", axis=0, tiled=True)

    feat = features.reshape(rows, channels)
    feat_wide = feat.astype(F32)
    activated = gelu_value(feat_wide).astype(BF16)
    sent = [dot(activated, weight, ((1,), (0,))).astype(BF16) for weight in outer_weights]
    arrived = [lax.ppermute(term, "seq", pairs) for term, pairs in zip(sent, forward)]
    middle = dot(activated, taps[1], ((1,), (0,)))
    for term in arrived:
        middle = middle + term.astype(F32)
    middle_b = middle.astype(BF16)
    other_middle = flip(middle_b, "head")
    hidden = gelu_value(middle).astype(BF16)
    other_hidden = gelu_value(other_middle.astype(F32)).astype(BF16)
    block_out = (
        feat_wide
        + dot(hidden, point_weight, ((1,), (1,)))
        + dot(other_hidden, other_point, ((1,), (1,)))
    ).astype(BF16)

    def rows_of(value, which):
        return lax.dynamic_slice_in_dim(value, which * half, half, 0)

    cotangent = track_cotangent.reshape(rows, whole_track.shape[1])

    def track_part(which):
        scores = dot(rows_of(block_out, which), whole_track, ((1,), (0,)))
        grad = (rows_of(cotangent, which).astype(F32) * jax.nn.sigmoid(scores)).astype(BF16)
        return dot(grad, whole_track, ((1,), (1,)))

    theirs = flip(track_part(1 - head).astype(BF16), "head")
    out_grad = track_part(head) + theirs.astype(F32)
    out_grad_b = out_grad.astype(BF16)
    other_out_grad = flip(out_grad_b, "head")

    grad_own = (
        dot(out_grad_b, point_weight, ((1,), (0,))) * gelu_slope(rows_of(middle, head))
    ).astype(BF16)
    grad_other = (
        dot(out_grad_b, other_point, ((1,), (0,)))
        * gelu_slope(rows_of(other_middle, head).astype(F32))
    ).astype(BF16)
    middle_grad = in_order(grad_own, flip(grad_other, "head"), head, 0)
    moved = []
    for pairs in backward:
        straight = lax.ppermute(grad_own, "seq", pairs)
        crossed = lax.ppermute(
            grad_other,
            ("seq", "head"),
            [(2 * i + k, 2 * j + 1 - k) for i, j in pairs for k in range(2)],
        )
        moved.append(in_order(straight, crossed, head, 0))

    act_part = dot(middle_grad, taps[1], ((1,), (1,)))
    for field, weight in zip(moved, outer_weights):
        act_part = act_part + dot(field, weight, ((1,), (1,)))
    act_theirs = flip(rows_of(act_part, 1 - head).astype(BF16), "head")
    act_grad = rows_of(act_part, head) + act_theirs.astype(F32)
    input_half = (out_grad + act_grad * gelu_slope(rows_of(feat_wide, head))).astype(BF16)
    input_grad = in_order(input_half, flip(input_half, "head"), head, 0)

    seq_bits = bits_of(n_seq)
    block = channels // (n_seq * n_sample)
    shape = (2,) * seq_bits + (n_sample, block)

    def halve(value, left, bit, keep_last=False):
        at = left.index(bit)
        if bit < 0:
            mine, give = own_first(value, at, sample)
            got = flip(give.astype(BF16), "sample")
        else:
            mine, give = own_first(value, at, (seq >> bit) & 1)
            got = flip(give.astype(BF16), "seq", 1 << bit)
        rest = [b for b in left if b != bit]
        return (mine, got, rest) if keep_last else (mine.astype(F32) + got.astype(F32), rest)

    def reduced(value, order, apart=False):
        left = list(range(seq_bits - 1, -1, -1)) + [-1]
        value = value.reshape(shape + value.shape[1:])
        for bit in order[:-1]:
            value, left = halve(value, left, bit)
            value = value.astype(BF16)
        mine, got, _ = halve(value, left, order[-1], True)
        if apart:
            return mine.astype(F32), got.astype(F32)
        return mine.astype(F32) + got.astype(F32)

    order_a = [-1] + list(range(seq_bits))
    order_b = [-1] + list(range(1, seq_bits - 1)) + [0, seq_bits - 1]
    whole_out_grad = in_order(out_grad_b, other_out_grad, head, 0)
    point_grad = reduced(dot(whole_out_grad, hidden, ((0,), (0,))), order_a)
    mid_tap = reduced(dot(activated, middle_grad, ((0,), (0,))), order_b)
    if one_sided:
        mine, got = reduced(dot(activated, moved[0], ((0,), (0,))), order_a, True)
        outer = [jnp.where(low, mine, got), jnp.where(low, got, mine)]
    else:
        outer = [reduced(dot(activated, field, ((0,), (0,))), order_a) for field in moved]
    dilated_grad = jnp.transpose(jnp.stack([outer[0], mid_tap, outer[1]]), (1, 0, 2))
    return (input_grad.reshape(samples, positions, channels), dilated_grad, point_grad)


def wide(ref):
    return ref[...].astype(F32)


def kernel_call(kernel, outs, ins, after=None, scratch=()):
    place, arrays = ins[0], list(ins[1:])
    in_specs = [pl.BlockSpec(memory_space=pltpu.SMEM)]
    in_specs += [pl.BlockSpec(memory_space=pltpu.VMEM)] * len(arrays)
    number = len(arrays) + 1
    if after is not None:
        arrays.append(after)
        in_specs.append(pl.BlockSpec(memory_space=pl.ANY))

    def run(*refs):
        given = refs[:number]
        kernel(*given, *refs[len(in_specs):])

    return pl.pallas_call(
        run,
        out_shape=[jax.ShapeDtypeStruct(s, d) for s, d in outs],
        in_specs=in_specs,
        out_specs=[pl.BlockSpec(memory_space=pltpu.VMEM)] * len(outs),
        scratch_shapes=list(scratch),
        compiler_params=pltpu.CompilerParams(vmem_limit_bytes=VMEM),
        name=kernel.__name__,
    )(place, *arrays)


NN = ((1,), (0,))
NT = ((1,), (1,))
HEAD, SAMPLE, TOP, MID, LOWEST = 1, 2, 3, 4, 5


def outer_term(place, feat, weight, acted, term, total):
    step = pl.program_id(0)
    act = gelu_value(feat[...].astype(F32)).astype(BF16)
    acted[...] = act

    @pl.when(step == 0)
    def _():
        total[...] = jnp.zeros_like(total)

    total[...] += dot(act, weight[0], NN)

    @pl.when(step == pl.num_programs(0) - 1)
    def _():
        term[...] = total[...].astype(BF16)


def middle_term(place, acted, weight, middle, turned):
    act = acted[...]
    middle[...] = dot(act, weight[...], NN)
    turned[...] = act.T.reshape(turned.shape)


def add_terms(place, middle, arrived, total, sent):
    value = middle[...] + wide(arrived)
    total[...] = value
    sent[...] = value.astype(BF16)


def own_hidden(place, middle, feat, point, hidden, slope, block):
    half = slope.shape[0]
    hid = gelu_value(middle[...]).astype(BF16)
    hidden[...] = hid
    own = pl.ds(pl.multiple_of(place[HEAD] * half, half), half)
    slope[...] = gelu_slope(middle[own, :])
    block[...] = wide(feat) + dot(hid, point[...], NT)


def tracks(
    place, block, other_middle, point_near, point_far, near, far, cotangent,
    keep, give, block_b, total,
):
    step = pl.program_id(0)
    sample = place[SAMPLE]
    piece = block_b.shape[2]

    @pl.when(step == 0)
    def _():
        hid = gelu_value(wide(other_middle)).astype(BF16)
        for which, point in ((sample, point_near), (1 - sample, point_far)):
            columns = pl.ds(pl.multiple_of(which * piece, piece), piece)
            block_b[which] = (block[:, columns] + dot(hid, point[...], NT)).astype(BF16)
        total[...] = jnp.zeros_like(total)

    scores = dot(block_b[sample], near[...], NN) + dot(block_b[1 - sample], far[...], NN)
    grad = (wide(cotangent) * jax.nn.sigmoid(scores)).astype(BF16)
    total[sample] += dot(grad, near[...], NT)
    total[1 - sample] += dot(grad, far[...], NT)

    @pl.when(step == pl.num_programs(0) - 1)
    def _():
        half = keep.shape[0]
        own = pl.ds(pl.multiple_of(place[HEAD] * half, half), half)
        theirs = pl.ds(pl.multiple_of((1 - place[HEAD]) * half, half), half)
        for which in range(2):
            columns = pl.ds(which * piece, piece)
            keep[:, columns] = total[which, own, :]
            give[:, columns] = total[which, theirs, :].astype(BF16)


def slopes(place, other_middle, feat, slope_other, slope_feat):
    half = slope_other.shape[0]
    own = pl.ds(pl.multiple_of(place[HEAD] * half, half), half)
    slope_other[...] = gelu_slope(other_middle[own, :].astype(F32))
    slope_feat[...] = gelu_slope(feat[own, :].astype(F32))


def middle_grads(
    place, keep, theirs, point, point_near, point_far, slope, slope_other,
    out_grad, out_grad_b, grad_own, grad_other,
):
    sample = place[SAMPLE]
    piece = point_near.shape[0]
    total = keep[...] + wide(theirs)
    out_grad[...] = total
    total_b = total.astype(BF16)
    out_grad_b[...] = total_b
    grad_own[...] = (dot(total_b, point[...], NN) * slope[...]).astype(BF16)
    near = out_grad_b[:, pl.ds(pl.multiple_of(sample * piece, piece), piece)]
    far = out_grad_b[:, pl.ds(pl.multiple_of((1 - sample) * piece, piece), piece)]
    other = dot(near, point_near[...], NN) + dot(far, point_far[...], NN)
    grad_other[...] = (other * slope_other[...]).astype(BF16)


def assembled(field, own, theirs, head):
    half = own.shape[0]
    field[pl.ds(pl.multiple_of(head * half, half), half), :] = own[...]
    field[pl.ds(pl.multiple_of((1 - head) * half, half), half), :] = theirs[...]


def products(place, turned, field, keep, give, columns):
    groups, _, block, rows = turned.shape
    for which, out in ((1 - place[SAMPLE], give), (place[SAMPLE], keep)):
        left = turned[:, which].reshape(groups * block, rows)
        value = dot(left, field[...], NN).astype(out.dtype)
        out[:, :, columns] = value.reshape(groups, block, value.shape[1])


def middle_tap(place, turned, own, theirs, field, keep, give):
    assembled(field, own, theirs, place[HEAD])
    products(place, turned, field, keep, give, slice(None))


def outer_tap(
    place, turned, straight, crossed, own_grad, other_grad, hidden, field, keep, give, whole,
    turned_grad,
):
    width = straight.shape[1]
    assembled(field, straight, crossed, place[HEAD])
    products(place, turned, field, keep, give, slice(0, width))
    assembled(whole, own_grad, other_grad, place[HEAD])
    turned_grad[...] = whole[...].T.reshape(turned_grad.shape)
    products(place, turned_grad, hidden, keep, give, slice(width, 2 * width))


def act_given(place, middle_grad, moved, mid_weight, outer_weight, give):
    half = give.shape[0]
    theirs = pl.ds(pl.multiple_of((1 - place[HEAD]) * half, half), half)
    value = dot(middle_grad[theirs, :], mid_weight[...], NT)
    give[...] = (value + dot(moved[theirs, :], outer_weight[...], NT)).astype(BF16)


def act_kept(place, middle_grad, moved, mid_weight, outer_weight, keep):
    half = keep.shape[0]
    own = pl.ds(pl.multiple_of(place[HEAD] * half, half), half)
    value = dot(middle_grad[own, :], mid_weight[...], NT)
    keep[...] = value + dot(moved[own, :], outer_weight[...], NT)


def core_sum(place, kept, got, keep, along, across, both):
    mid, lowest = place[MID], place[LOWEST]

    def part(i, j):
        return kept[:, i, j].astype(F32) + got[:, i, j].astype(F32)

    both[...] = part(1 - mid, 1 - lowest).astype(BF16)
    along[...] = part(1 - mid, lowest).astype(BF16)
    across[...] = part(mid, 1 - lowest).astype(BF16)
    keep[...] = part(mid, lowest)


def chips_sum(place, kept, along, across, both, keep, give):
    def part(i):
        total = kept[i] + along[i].astype(F32)
        return total + across[i].astype(F32) + both[i].astype(F32)

    give[...] = part(1 - place[TOP]).astype(BF16)
    keep[...] = part(place[TOP])


def input_part(place, out_grad, kept, got, slope_feat, result):
    result[...] = (out_grad[...] + (kept[...] + wide(got)) * slope_feat[...]).astype(BF16)


def finish(place, mid_kept, mid_got, kept, got, dilated, point):
    width = mid_kept.shape[1]
    dilated[1] = mid_kept[...] + wide(mid_got)
    own, theirs = place[0], 2 - place[0]
    dilated[own] = kept[:, :width]
    dilated[theirs] = got[:, :width].astype(F32)
    point[...] = kept[:, width:] + got[:, width:].astype(F32)


def joined(place, own, theirs, result):
    assembled(result, own, theirs, place[HEAD])


def body(features, dilated_weight, point_weight, track_weight, track_cotangent):
    samples, positions, channels = features.shape
    n_seq, n_sample, n_head = (lax.axis_size(a) for a in ("seq", "sample", "head"))
    dist = DILATION_STEP // positions
    if not (n_seq == 2 * dist and bits_of(n_seq) == 3 and n_sample == 2 and n_head == 2 and samples == 1):
        return general(features, dilated_weight, point_weight, track_weight, track_cotangent)
    rows = positions
    half = rows // 2
    width = dilated_weight.shape[2]
    tracks_here = track_weight.shape[1]
    piece = channels // n_sample
    block = channels // (n_seq * n_sample)
    seq, head, sample = lax.axis_index("seq"), lax.axis_index("head"), lax.axis_index("sample")
    place = jnp.stack(
        [jnp.where(seq < dist, 0, 2), head, sample, (seq >> 2) & 1, (seq >> 1) & 1, seq & 1]
    ).astype(jnp.int32)
    taps = jnp.transpose(dilated_weight, (1, 0, 2))
    feat = features.reshape(rows, channels)
    cotangent = track_cotangent.reshape(rows, tracks_here)
    pairs = [(i, (i + dist) % n_seq) for i in range(n_seq)]
    crossing = [(2 * i + k, 2 * j + 1 - k) for i, j in pairs for k in range(2)]

    own_piece = lax.dynamic_slice_in_dim(point_weight, sample * piece, piece, 0)
    point_near = flip(own_piece, "head")
    far_track = flip(track_weight, "sample")
    point_far = flip(point_near, "sample")

    steps = 3
    depth = channels // steps
    acted, term = pl.pallas_call(
        outer_term,
        grid_spec=pltpu.PrefetchScalarGridSpec(
            num_scalar_prefetch=1,
            grid=(steps,),
            in_specs=[
                pl.BlockSpec((rows, depth), lambda k, place: (0, k)),
                pl.BlockSpec((1, depth, width), lambda k, place: (place[0], k, 0)),
            ],
            out_specs=[
                pl.BlockSpec((rows, depth), lambda k, place: (0, k)),
                pl.BlockSpec((rows, width), lambda k, place: (0, 0)),
            ],
            scratch_shapes=[pltpu.VMEM((rows, width), F32)],
        ),
        out_shape=[
            jax.ShapeDtypeStruct((rows, channels), BF16),
            jax.ShapeDtypeStruct((rows, width), BF16),
        ],
        compiler_params=pltpu.CompilerParams(vmem_limit_bytes=VMEM),
        name="outer_term",
    )(place, feat, taps)
    arrived = lax.ppermute(term, "seq", pairs)
    mid_weight = taps[1]
    outer_weight = lax.dynamic_index_in_dim(taps, place[0], 0, keepdims=False)
    groups = n_seq
    middle, turned = kernel_call(
        middle_term,
        [((rows, width), F32), ((groups, n_sample, block, rows), BF16)],
        [place, acted, mid_weight],
    )
    middle, middle_b = kernel_call(
        add_terms, [((rows, width), F32), ((rows, width), BF16)], [place, middle, arrived], turned
    )
    other_middle = flip(middle_b, "head")
    hidden, slope, block_part = kernel_call(
        own_hidden,
        [((rows, width), BF16), ((half, width), F32), ((rows, channels), F32)],
        [place, middle, feat, point_weight],
    )

    tile = width if tracks_here % width == 0 else tracks_here
    fixed = lambda k, place: (0, 0)
    moving = lambda k, place: (0, k)
    keep, give = pl.pallas_call(
        tracks,
        grid_spec=pltpu.PrefetchScalarGridSpec(
            num_scalar_prefetch=1,
            grid=(tracks_here // tile,),
            in_specs=[
                pl.BlockSpec((rows, channels), fixed),
                pl.BlockSpec((rows, width), fixed),
                pl.BlockSpec((piece, width), fixed),
                pl.BlockSpec((piece, width), fixed),
                pl.BlockSpec((piece, tile), moving),
                pl.BlockSpec((piece, tile), moving),
                pl.BlockSpec((rows, tile), moving),
            ],
            out_specs=[pl.BlockSpec((half, channels), fixed)] * 2,
            scratch_shapes=[
                pltpu.VMEM((n_sample, rows, piece), BF16),
                pltpu.VMEM((n_sample, rows, piece), F32),
            ],
        ),
        out_shape=[
            jax.ShapeDtypeStruct((half, channels), F32),
            jax.ShapeDtypeStruct((half, channels), BF16),
        ],
        compiler_params=pltpu.CompilerParams(vmem_limit_bytes=VMEM),
        name="tracks",
    )(place, block_part, other_middle, point_near, point_far, track_weight, far_track, cotangent)
    theirs = flip(give, "head")
    slope_other, slope_feat = kernel_call(
        slopes,
        [((half, width), F32), ((half, channels), F32)],
        [place, other_middle, feat],
        keep,
    )
    out_grad, out_grad_b, grad_own, grad_other = kernel_call(
        middle_grads,
        [
            ((half, channels), F32),
            ((half, channels), BF16),
            ((half, width), BF16),
            ((half, width), BF16),
        ],
        [place, keep, theirs, point_weight, point_near, point_far, slope, slope_other],
    )
    straight = lax.ppermute(grad_own, "seq", pairs)
    crossed = lax.ppermute(grad_other, ("seq", "head"), crossing)
    grad_theirs = flip(grad_other, "head")
    other_out_grad = flip(out_grad_b, "head")

    def chips(value):
        return value.reshape(2, 2, 2, *value.shape[1:])

    def direct(along, across, both):
        return (
            flip(along, "seq", 2),
            flip(across, "seq", 1),
            flip(both, "seq", 3),
        )

    def summed(keep, give, columns, after):
        got = flip(give, "sample")
        part = [((2, block, columns), F32)] + [((2, block, columns), BF16)] * 3
        kept, along, across, both = kernel_call(
            core_sum, part, [place, chips(keep), chips(got)], after
        )
        return kept, direct(along, across, both)

    def halves(kept, got, columns, after):
        keep, give = kernel_call(
            chips_sum,
            [((block, columns), F32), ((block, columns), BF16)],
            [place, kept, *got],
            after,
        )
        return keep, flip(give, "seq", 4)

    part = [((groups, block, width), BF16)] * 2
    middle_grad, mid_keep, mid_give = kernel_call(
        middle_tap, [((rows, width), BF16)] + part, [place, turned, grad_own, grad_theirs]
    )
    mid_keep, mid_got = summed(mid_keep, mid_give, width, None)
    part = [((groups, block, 2 * width), BF16)] * 2
    moved, out_keep, out_give = kernel_call(
        outer_tap,
        [((rows, width), BF16)] + part,
        [place, turned, straight, crossed, out_grad_b, other_out_grad, hidden],
        mid_keep,
        scratch=[
            pltpu.VMEM((rows, channels), BF16),
            pltpu.VMEM((groups, n_sample, block, rows), BF16),
        ],
    )
    (act_give,) = kernel_call(
        act_given,
        [((half, channels), BF16)],
        [place, middle_grad, moved, mid_weight, outer_weight],
        out_keep,
    )
    act_got = flip(act_give, "head")
    (act_keep,) = kernel_call(
        act_kept,
        [((half, channels), F32)],
        [place, middle_grad, moved, mid_weight, outer_weight],
        act_give,
    )
    out_keep, out_got = summed(out_keep, out_give, 2 * width, act_keep)
    (input_half,) = kernel_call(
        input_part,
        [((half, channels), BF16)],
        [place, out_grad, act_keep, act_got, slope_feat],
        out_keep,
    )
    input_other = flip(input_half, "head")
    mid_keep, mid_got = halves(mid_keep, mid_got, width, input_half)
    out_keep, out_got = halves(out_keep, out_got, 2 * width, mid_keep)
    (input_grad,) = kernel_call(
        joined, [((rows, channels), BF16)], [place, input_half, input_other], out_keep
    )
    dilated_grad, point_grad = kernel_call(
        finish,
        [((3, block, width), F32), ((block, width), F32)],
        [place, mid_keep, mid_got, out_keep, out_got],
        input_grad,
    )
    dilated_grad = jnp.transpose(dilated_grad, (1, 0, 2))
    return (input_grad.reshape(samples, positions, channels), dilated_grad, point_grad)


def solution(mesh):
    placed = (
        P("sample", "seq", None),
        P(None, None, "head"),
        P(None, "head"),
        P("sample", "head"),
        P("sample", "seq", "head"),
    )
    return jax.shard_map(
        body,
        mesh=mesh,
        in_specs=placed,
        out_specs=(
            P("sample", "seq", None),
            P(("seq", "sample"), None, "head"),
            P(("seq", "sample"), "head"),
        ),
        check_vma=False,
    )
```

```python
import jax
import jax.numpy as jnp
from jax import lax
from jax.experimental import pallas as pl
from jax.experimental.pallas import tpu as pltpu
from jax.sharding import PartitionSpec as P

DILATION_STEP = 1024
BF16 = jnp.bfloat16
F32 = jnp.float32
VMEM = 24 * 2**20
LITTLE = pl.CostEstimate(flops=1, bytes_accessed=1, transcendentals=0)


def gelu_value(value):
    inner = 0.7978845608 * (value + 0.044715 * value * value * value)
    return 0.5 * value * (1.0 + jnp.tanh(inner))


def gelu_slope(value):
    inner = 0.7978845608 * (value + 0.044715 * value * value * value)
    tangent = jnp.tanh(inner)
    return 0.5 * (1.0 + tangent) + 0.5 * value * (1.0 - tangent * tangent) * 0.7978845608 * (
        1.0 + 3.0 * 0.044715 * value * value
    )


def dot(left, right, contract):
    return lax.dot_general(left, right, (contract, ((), ())), preferred_element_type=F32)


def flip(value, axis, step=1):
    count = lax.axis_size(axis)
    return lax.ppermute(value, axis, [(i, i ^ step) for i in range(count)])


def own_first(value, axis_at, bit):
    return (
        lax.dynamic_index_in_dim(value, bit, axis_at, keepdims=False),
        lax.dynamic_index_in_dim(value, 1 - bit, axis_at, keepdims=False),
    )


def in_order(own, other, bit, axis):
    first = jnp.where(bit == 0, own, other)
    second = jnp.where(bit == 0, other, own)
    return jnp.concatenate([first, second], axis=axis)


def bits_of(count):
    return count.bit_length() - 1


def general(features, dilated_weight, point_weight, track_weight, track_cotangent):
    samples, positions, channels = features.shape
    rows = samples * positions
    half = rows // 2
    width = dilated_weight.shape[2]
    n_seq, n_sample = lax.axis_size("seq"), lax.axis_size("sample")
    seq, head, sample = lax.axis_index("seq"), lax.axis_index("head"), lax.axis_index("sample")
    dist = DILATION_STEP // positions
    one_sided = n_seq == 2 * dist
    low = seq < dist
    taps = jnp.transpose(dilated_weight, (1, 0, 2))

    if one_sided:
        outer_weights = [lax.dynamic_index_in_dim(taps, jnp.where(low, 0, 2), 0, keepdims=False)]
        pairs = [(i, (i + dist) % n_seq) for i in range(n_seq)]
        forward, backward = [pairs], [pairs]
    else:
        outer_weights = [taps[0], taps[2]]
        up = [(i, i + dist) for i in range(n_seq - dist)]
        down = [(i + dist, i) for i in range(n_seq - dist)]
        forward, backward = [up, down], [down, up]
    count = len(outer_weights)

    whole_track = lax.all_gather(track_weight, "sample", axis=0, tiled=True)
    piece = channels // n_sample
    own_piece = lax.dynamic_slice_in_dim(point_weight, sample * piece, piece, 0)
    other_point = lax.all_gather(flip(own_piece, "head"), "sample", axis=0, tiled=True)

    feat = features.reshape(rows, channels)
    feat_wide = feat.astype(F32)
    activated = gelu_value(feat_wide).astype(BF16)
    sent = [dot(activated, weight, ((1,), (0,))).astype(BF16) for weight in outer_weights]
    arrived = [lax.ppermute(term, "seq", pairs) for term, pairs in zip(sent, forward)]
    middle = dot(activated, taps[1], ((1,), (0,)))
    for term in arrived:
        middle = middle + term.astype(F32)
    middle_b = middle.astype(BF16)
    other_middle = flip(middle_b, "head")
    hidden = gelu_value(middle).astype(BF16)
    other_hidden = gelu_value(other_middle.astype(F32)).astype(BF16)
    block_out = (
        feat_wide
        + dot(hidden, point_weight, ((1,), (1,)))
        + dot(other_hidden, other_point, ((1,), (1,)))
    ).astype(BF16)

    def rows_of(value, which):
        return lax.dynamic_slice_in_dim(value, which * half, half, 0)

    cotangent = track_cotangent.reshape(rows, whole_track.shape[1])

    def track_part(which):
        scores = dot(rows_of(block_out, which), whole_track, ((1,), (0,)))
        grad = (rows_of(cotangent, which).astype(F32) * jax.nn.sigmoid(scores)).astype(BF16)
        return dot(grad, whole_track, ((1,), (1,)))

    theirs = flip(track_part(1 - head).astype(BF16), "head")
    out_grad = track_part(head) + theirs.astype(F32)
    out_grad_b = out_grad.astype(BF16)
    other_out_grad = flip(out_grad_b, "head")

    grad_own = (
        dot(out_grad_b, point_weight, ((1,), (0,))) * gelu_slope(rows_of(middle, head))
    ).astype(BF16)
    grad_other = (
        dot(out_grad_b, other_point, ((1,), (0,)))
        * gelu_slope(rows_of(other_middle, head).astype(F32))
    ).astype(BF16)
    middle_grad = in_order(grad_own, flip(grad_other, "head"), head, 0)
    moved = []
    for pairs in backward:
        straight = lax.ppermute(grad_own, "seq", pairs)
        crossed = lax.ppermute(
            grad_other,
            ("seq", "head"),
            [(2 * i + k, 2 * j + 1 - k) for i, j in pairs for k in range(2)],
        )
        moved.append(in_order(straight, crossed, head, 0))

    act_part = dot(middle_grad, taps[1], ((1,), (1,)))
    for field, weight in zip(moved, outer_weights):
        act_part = act_part + dot(field, weight, ((1,), (1,)))
    act_theirs = flip(rows_of(act_part, 1 - head).astype(BF16), "head")
    act_grad = rows_of(act_part, head) + act_theirs.astype(F32)
    input_half = (out_grad + act_grad * gelu_slope(rows_of(feat_wide, head))).astype(BF16)
    input_grad = in_order(input_half, flip(input_half, "head"), head, 0)

    seq_bits = bits_of(n_seq)
    block = channels // (n_seq * n_sample)
    shape = (2,) * seq_bits + (n_sample, block)

    def halve(value, left, bit, keep_last=False):
        at = left.index(bit)
        if bit < 0:
            mine, give = own_first(value, at, sample)
            got = flip(give.astype(BF16), "sample")
        else:
            mine, give = own_first(value, at, (seq >> bit) & 1)
            got = flip(give.astype(BF16), "seq", 1 << bit)
        rest = [b for b in left if b != bit]
        return (mine, got, rest) if keep_last else (mine.astype(F32) + got.astype(F32), rest)

    def reduced(value, order, apart=False):
        left = list(range(seq_bits - 1, -1, -1)) + [-1]
        value = value.reshape(shape + value.shape[1:])
        for bit in order[:-1]:
            value, left = halve(value, left, bit)
            value = value.astype(BF16)
        mine, got, _ = halve(value, left, order[-1], True)
        if apart:
            return mine.astype(F32), got.astype(F32)
        return mine.astype(F32) + got.astype(F32)

    order_a = [-1] + list(range(seq_bits))
    order_b = [-1] + list(range(1, seq_bits - 1)) + [0, seq_bits - 1]
    whole_out_grad = in_order(out_grad_b, other_out_grad, head, 0)
    point_grad = reduced(dot(whole_out_grad, hidden, ((0,), (0,))), order_a)
    mid_tap = reduced(dot(activated, middle_grad, ((0,), (0,))), order_b)
    if one_sided:
        mine, got = reduced(dot(activated, moved[0], ((0,), (0,))), order_a, True)
        outer = [jnp.where(low, mine, got), jnp.where(low, got, mine)]
    else:
        outer = [reduced(dot(activated, field, ((0,), (0,))), order_a) for field in moved]
    dilated_grad = jnp.transpose(jnp.stack([outer[0], mid_tap, outer[1]]), (1, 0, 2))
    return (input_grad.reshape(samples, positions, channels), dilated_grad, point_grad)


def wide(ref):
    return ref[...].astype(F32)


def kernel_call(kernel, outs, ins, after=None, scratch=(), spaces={}):
    place, arrays = ins[0], list(ins[1:])
    in_specs = [pl.BlockSpec(memory_space=pltpu.SMEM)]
    in_specs += [
        pl.BlockSpec(memory_space=spaces.get(k + 1, pltpu.VMEM)) for k in range(len(arrays))
    ]
    number = len(arrays) + 1
    if after is not None:
        arrays.append(after)
        in_specs.append(pl.BlockSpec(memory_space=pl.ANY))

    def run(*refs):
        given = refs[:number]
        kernel(*given, *refs[len(in_specs):])

    return pl.pallas_call(
        run,
        out_shape=[jax.ShapeDtypeStruct(s, d) for s, d in outs],
        in_specs=in_specs,
        out_specs=[pl.BlockSpec(memory_space=pltpu.VMEM)] * len(outs),
        scratch_shapes=list(scratch),
        compiler_params=pltpu.CompilerParams(vmem_limit_bytes=VMEM),
        cost_estimate=LITTLE,
        name=kernel.__name__,
    )(place, *arrays)


def in_hbm(value):
    return pltpu.with_memory_space_constraint(value, pltpu.HBM)


NN = ((1,), (0,))
NT = ((1,), (1,))
HEAD, SAMPLE, TOP, MID, LOWEST = 1, 2, 3, 4, 5


def outer_term(place, feat, taps, acted, term, rows, weight, sems):
    steps = sems.shape[1]
    depth = rows.shape[1] // steps
    parts = [pl.ds(k * depth, depth) for k in range(steps)]
    feats = [
        pltpu.make_async_copy(feat.at[:, part], rows.at[:, part], sems.at[0, k])
        for k, part in enumerate(parts)
    ]
    weights = [
        pltpu.make_async_copy(taps.at[place[0], part], weight.at[part], sems.at[1, k])
        for k, part in enumerate(parts)
    ]
    for pair in zip(feats, weights):
        for copy in pair:
            copy.start()
    total = None
    for copy, coming, part in zip(feats, weights, parts):
        copy.wait()
        act = gelu_value(rows[:, part].astype(F32)).astype(BF16)
        acted[:, part] = act
        coming.wait()
        value = dot(act, weight[part, :], NN)
        total = value if total is None else total + value
    term[...] = total.astype(BF16)


def piece_of(place, point, piece):
    number = piece.shape[0]
    piece[...] = point[pl.ds(pl.multiple_of(place[SAMPLE] * number, number), number), :]


def middle_term(place, acted, weight, middle, kept, given):
    act = acted[...]
    middle[...] = dot(act, weight[1], NN)
    part_channels(place, act.T, kept, given)


def part_channels(place, turned, kept, given):
    groups, block, rows = kept.shape
    split = turned.reshape(groups, 2, block, rows)
    first = place[SAMPLE] == 0
    kept[...] = jnp.where(first, split[:, 0], split[:, 1])
    given[...] = jnp.where(first, split[:, 1], split[:, 0])


def add_terms(place, middle, arrived, total, sent):
    value = middle[...] + wide(arrived)
    total[...] = value
    sent[...] = value.astype(BF16)


def own_hidden(place, middle, feat, point, hidden, slope, block):
    half = slope.shape[0]
    hid = gelu_value(middle[...]).astype(BF16)
    hidden[...] = hid
    own = pl.ds(pl.multiple_of(place[HEAD] * half, half), half)
    slope[...] = gelu_slope(middle[own, :])
    block[...] = wide(feat) + dot(hid, point[...], NT)


def tracks(place, block, other_middle, near, far, cotangent, *rest):
    *points, keep, give, block_b, grads = rest
    sample = place[SAMPLE]
    half = keep.shape[0]
    piece = block_b.shape[2]
    width = other_middle.shape[1]
    own = pl.ds(pl.multiple_of(place[HEAD] * half, half), half)
    theirs = pl.ds(pl.multiple_of((1 - place[HEAD]) * half, half), half)

    def turned(ref, columns):
        return jnp.concatenate([ref[theirs, columns], ref[own, columns]], axis=0)

    hid = gelu_value(turned(other_middle, slice(None)).astype(F32)).astype(BF16)
    ahead = 0
    for point in points:
        number = point.shape[0]
        which, column = (sample, ahead) if ahead < piece else (1 - sample, ahead - piece)
        columns = pl.ds(pl.multiple_of(which * piece + column, number), number)
        value = turned(block, columns) + dot(hid, point[...], NT)
        block_b[which, :, column : column + number] = value.astype(BF16)
        ahead += number
    number = near.shape[1]
    tile = width if number % width == 0 else number
    for start in range(0, number, tile):
        columns = slice(start, start + tile)
        scores = dot(block_b[sample], near[:, columns], NN)
        scores += dot(block_b[1 - sample], far[:, columns], NN)
        cot = turned(cotangent, columns).astype(F32)
        grads[:, columns] = (cot * jax.nn.sigmoid(scores)).astype(BF16)
    for which, weight in ((sample, near), (1 - sample, far)):
        columns = pl.ds(pl.multiple_of(which * piece, piece), piece)
        value = dot(grads[...], weight[...], NT)
        give[:, columns] = value[:half].astype(BF16)
        keep[:, columns] = value[half:]


def slopes(place, other_middle, feat, slope_other, slope_feat):
    half = slope_other.shape[0]
    own = pl.ds(pl.multiple_of(place[HEAD] * half, half), half)
    slope_other[...] = gelu_slope(other_middle[own, :].astype(F32))
    slope_feat[...] = gelu_slope(feat[own, :].astype(F32))


def middle_grads(place, keep, theirs, point, slope, slope_other, *rest):
    *points, out_grad, both, grad_own, grad_other = rest
    sample = place[SAMPLE]
    channels = keep.shape[1]
    piece = channels // 2
    total = keep[...] + wide(theirs)
    out_grad[...] = total
    total_b = total.astype(BF16)
    both[:, :channels] = total_b
    grad_own[...] = (dot(total_b, point[...], NN) * slope[...]).astype(BF16)
    other, ahead = None, 0
    for part in points:
        number = part.shape[0]
        which, column = (sample, ahead) if ahead < piece else (1 - sample, ahead - piece)
        left = both[:, pl.ds(pl.multiple_of(which * piece + column, number), number)]
        value = dot(left, part[...], NN)
        other = value if other is None else other + value
        ahead += number
    other = (other * slope_other[...]).astype(BF16)
    grad_other[...] = other
    both[:, channels:] = other


def assembled(field, own, theirs, head):
    half = field.shape[0] // 2
    field[pl.ds(pl.multiple_of(head * half, half), half), :] = own
    field[pl.ds(pl.multiple_of((1 - head) * half, half), half), :] = theirs


def gathered(
    place, both, got, grad_own, straight, crossed, middle_grad, moved, kept, given, whole,
):
    channels = whole.shape[1]
    groups = kept.shape[0]
    assembled(middle_grad, grad_own[...], got[:, channels:], place[HEAD])
    assembled(moved, straight[...], crossed[...], place[HEAD])
    assembled(whole, both[:, :channels], got[:, :channels], place[HEAD])
    part_channels(place, whole[...].T, kept, given.at[:groups])
    block, rows = kept.shape[1:]
    number = middle_grad.shape[1] // block
    shape = (number, block, rows)
    given[groups : groups + number] = middle_grad[...].T.reshape(shape)
    given[groups + number :] = moved[...].T.reshape(shape)


def products(
    place, acts, other_acts, outs, pack, middle_grad, moved, hidden, other_hidden,
    keep, along, across, both,
):
    groups, block, rows = acts.shape
    width = hidden.shape[1]
    number = width // block
    half = groups // 2
    other_mid = pack[groups : groups + number].reshape(width, rows)
    other_moved = pack[groups + number :].reshape(width, rows)
    mid, lowest = place[MID], place[LOWEST]

    for i, j, out in (
        (1 - mid, 1 - lowest, both),
        (1 - mid, lowest, along),
        (mid, 1 - lowest, across),
        (mid, lowest, keep),
    ):
        at = 2 * i + j

        def left(ref):
            return jnp.concatenate([ref[at], ref[half + at]], axis=0)

        own, other = left(acts), left(other_acts)
        values = (
            dot(own, moved[...], NN) + dot(other, other_moved, NT),
            dot(own, middle_grad[...], NN) + dot(other, other_mid, NT),
            dot(left(outs), hidden[...], NN) + dot(left(pack), other_hidden[...], NN),
        )
        for k, value in enumerate(values):
            shape = (2, block, width)
            out[:, :, k * width : (k + 1) * width] = value.astype(out.dtype).reshape(shape)


def act_given(place, middle_grad, moved, weight, give):
    half = give.shape[0]
    theirs = pl.ds(pl.multiple_of((1 - place[HEAD]) * half, half), half)
    value = dot(middle_grad[theirs, :], weight[1], NT)
    give[...] = (value + dot(moved[theirs, :], weight[place[0]], NT)).astype(BF16)


def act_kept(place, middle_grad, moved, weight, keep):
    half = keep.shape[0]
    own = pl.ds(pl.multiple_of(place[HEAD] * half, half), half)
    value = dot(middle_grad[own, :], weight[1], NT)
    keep[...] = value + dot(moved[own, :], weight[place[0]], NT)


def chips_sum(place, kept, along, across, both, keep, give):
    def part(i):
        total = kept[i] + along[i].astype(F32)
        return total + across[i].astype(F32) + both[i].astype(F32)

    give[...] = part(1 - place[TOP]).astype(BF16)
    keep[...] = part(place[TOP])


def input_part(place, out_grad, kept, got, slope_feat, result):
    result[...] = (out_grad[...] + (kept[...] + wide(got)) * slope_feat[...]).astype(BF16)


def finish(place, kept, got, own, theirs, dilated, point, result):
    assembled(result, own[...], theirs[...], place[HEAD])
    width = point.shape[1]
    dilated[place[0]] = kept[:, :width]
    dilated[2 - place[0]] = got[:, :width].astype(F32)
    dilated[1] = kept[:, width : 2 * width] + got[:, width : 2 * width].astype(F32)
    point[...] = kept[:, 2 * width :] + got[:, 2 * width :].astype(F32)


def body(features, dilated_weight, point_weight, track_weight, track_cotangent):
    samples, positions, channels = features.shape
    n_seq, n_sample, n_head = (lax.axis_size(a) for a in ("seq", "sample", "head"))
    dist = DILATION_STEP // positions
    if not (n_seq == 2 * dist and bits_of(n_seq) == 3 and n_sample == 2 and n_head == 2 and samples == 1):
        return general(features, dilated_weight, point_weight, track_weight, track_cotangent)
    rows = positions
    half = rows // 2
    width = dilated_weight.shape[2]
    tracks_here = track_weight.shape[1]
    piece = channels // n_sample
    block = channels // (n_seq * n_sample)
    seq, head, sample = lax.axis_index("seq"), lax.axis_index("head"), lax.axis_index("sample")
    place = jnp.stack(
        [jnp.where(seq < dist, 0, 2), head, sample, (seq >> 2) & 1, (seq >> 1) & 1, seq & 1]
    ).astype(jnp.int32)
    taps = jnp.transpose(dilated_weight, (1, 0, 2))
    feat = features.reshape(rows, channels)
    cotangent = track_cotangent.reshape(rows, tracks_here)
    pairs = [(i, (i + dist) % n_seq) for i in range(n_seq)]
    crossing = [(2 * i + k, 2 * j + 1 - k) for i, j in pairs for k in range(2)]

    far_track = flip(track_weight, "sample")
    acted, term = kernel_call(
        outer_term,
        [((rows, channels), BF16), ((rows, width), BF16)],
        [place, in_hbm(feat), in_hbm(taps)],
        scratch=[
            pltpu.VMEM((rows, channels), BF16),
            pltpu.VMEM((channels, width), BF16),
            pltpu.SemaphoreType.DMA((2, 3)),
        ],
        spaces={1: pltpu.HBM, 2: pltpu.HBM},
    )
    arrived = lax.ppermute(term, "seq", pairs)
    groups = n_seq

    (own_piece,) = kernel_call(
        piece_of, [((piece, width), BF16)], [place, point_weight], acted
    )
    cut = piece // 3
    near = [flip(own_piece[k : k + cut], "head") for k in range(0, piece, cut)]
    far = [
        flip(part[k : k + cut // 2], "sample") for part in near for k in range(0, cut, cut // 2)
    ]
    points = near + far

    turned = ((groups, block, rows), BF16)
    middle, acts, acts_given = kernel_call(
        middle_term,
        [((rows, width), F32), turned, turned],
        [place, acted, taps],
        own_piece,
    )
    middle, middle_b = kernel_call(
        add_terms, [((rows, width), F32), ((rows, width), BF16)], [place, middle, arrived], acts
    )
    other_middle = flip(middle_b, "head")
    hidden, slope, block_part = kernel_call(
        own_hidden,
        [((rows, width), BF16), ((half, width), F32), ((rows, channels), F32)],
        [place, middle, feat, point_weight],
    )

    keep, give = kernel_call(
        tracks,
        [((half, channels), F32), ((half, channels), BF16)],
        [place, block_part, other_middle, track_weight, far_track, cotangent, *points],
        scratch=[
            pltpu.VMEM((n_sample, rows, piece), BF16),
            pltpu.VMEM((rows, tracks_here), BF16),
        ],
    )
    theirs = flip(give, "head")
    slope_other, slope_feat = kernel_call(
        slopes,
        [((half, width), F32), ((half, channels), F32)],
        [place, other_middle, feat],
        keep,
    )
    out_grad, both, grad_own, grad_other = kernel_call(
        middle_grads,
        [
            ((half, channels), F32),
            ((half, channels + width), BF16),
            ((half, width), BF16),
            ((half, width), BF16),
        ],
        [place, keep, theirs, point_weight, slope, slope_other, *points],
    )
    straight = lax.ppermute(grad_own, "seq", pairs)
    crossed = lax.ppermute(grad_other, ("seq", "head"), crossing)
    got = flip(both, "head")
    number = groups + 2 * width // block
    middle_grad, moved, outs, pack = kernel_call(
        gathered,
        [((rows, width), BF16)] * 2 + [turned, ((number, block, rows), BF16)],
        [place, both, got, grad_own, straight, crossed],
        scratch=[pltpu.VMEM((rows, channels), BF16)],
    )
    other_pack = flip(pack, "sample")
    (act_give,) = kernel_call(
        act_given, [((half, channels), BF16)], [place, middle_grad, moved, taps]
    )
    act_got = flip(act_give, "head")
    part = (2, block, 3 * width)
    kept, along, across, diagonal = kernel_call(
        products,
        [(part, F32)] + [(part, BF16)] * 3,
        [
            place, acts, flip(acts_given, "sample"), outs, other_pack, middle_grad, moved,
            hidden, flip(hidden, "sample"),
        ],
        act_give,
    )
    along, across, diagonal = flip(along, "seq", 2), flip(across, "seq", 1), flip(diagonal, "seq", 3)
    (act_keep,) = kernel_call(
        act_kept, [((half, channels), F32)], [place, middle_grad, moved, taps], kept
    )
    (input_half,) = kernel_call(
        input_part,
        [((half, channels), BF16)],
        [place, out_grad, act_keep, act_got, slope_feat],
    )
    input_other = flip(input_half, "head")
    kept, given = kernel_call(
        chips_sum,
        [((block, 3 * width), F32), ((block, 3 * width), BF16)],
        [place, kept, along, across, diagonal],
        input_half,
    )
    dilated_grad, point_grad, input_grad = kernel_call(
        finish,
        [((3, block, width), F32), ((block, width), F32), ((rows, channels), BF16)],
        [place, kept, flip(given, "seq", 4), input_half, input_other],
    )
    dilated_grad = jnp.transpose(dilated_grad, (1, 0, 2))
    return (input_grad.reshape(samples, positions, channels), dilated_grad, point_grad)


def solution(mesh):
    placed = (
        P("sample", "seq", None),
        P(None, None, "head"),
        P(None, "head"),
        P("sample", "head"),
        P("sample", "seq", "head"),
    )
    return jax.shard_map(
        body,
        mesh=mesh,
        in_specs=placed,
        out_specs=(
            P("sample", "seq", None),
            P(("seq", "sample"), None, "head"),
            P(("seq", "sample"), "head"),
        ),
        check_vma=False,
    )
```

```python
import jax
import jax.numpy as jnp
from jax import lax
from jax.experimental import pallas as pl
from jax.experimental.pallas import tpu as pltpu
from jax.sharding import PartitionSpec as P

DILATION_STEP = 1024
BF16 = jnp.bfloat16
F32 = jnp.float32
VMEM = 24 * 2**20
LITTLE = pl.CostEstimate(flops=1, bytes_accessed=1, transcendentals=0)


def gelu_value(value):
    inner = 0.7978845608 * (value + 0.044715 * value * value * value)
    return 0.5 * value * (1.0 + jnp.tanh(inner))


def gelu_slope(value):
    inner = 0.7978845608 * (value + 0.044715 * value * value * value)
    tangent = jnp.tanh(inner)
    return 0.5 * (1.0 + tangent) + 0.5 * value * (1.0 - tangent * tangent) * 0.7978845608 * (
        1.0 + 3.0 * 0.044715 * value * value
    )


def dot(left, right, contract):
    return lax.dot_general(left, right, (contract, ((), ())), preferred_element_type=F32)


def flip(value, axis, step=1):
    count = lax.axis_size(axis)
    return lax.ppermute(value, axis, [(i, i ^ step) for i in range(count)])


def own_first(value, axis_at, bit):
    return (
        lax.dynamic_index_in_dim(value, bit, axis_at, keepdims=False),
        lax.dynamic_index_in_dim(value, 1 - bit, axis_at, keepdims=False),
    )


def in_order(own, other, bit, axis):
    first = jnp.where(bit == 0, own, other)
    second = jnp.where(bit == 0, other, own)
    return jnp.concatenate([first, second], axis=axis)


def bits_of(count):
    return count.bit_length() - 1


def general(features, dilated_weight, point_weight, track_weight, track_cotangent):
    samples, positions, channels = features.shape
    rows = samples * positions
    half = rows // 2
    width = dilated_weight.shape[2]
    n_seq, n_sample = lax.axis_size("seq"), lax.axis_size("sample")
    seq, head, sample = lax.axis_index("seq"), lax.axis_index("head"), lax.axis_index("sample")
    dist = DILATION_STEP // positions
    one_sided = n_seq == 2 * dist
    low = seq < dist
    taps = jnp.transpose(dilated_weight, (1, 0, 2))

    if one_sided:
        outer_weights = [lax.dynamic_index_in_dim(taps, jnp.where(low, 0, 2), 0, keepdims=False)]
        pairs = [(i, (i + dist) % n_seq) for i in range(n_seq)]
        forward, backward = [pairs], [pairs]
    else:
        outer_weights = [taps[0], taps[2]]
        up = [(i, i + dist) for i in range(n_seq - dist)]
        down = [(i + dist, i) for i in range(n_seq - dist)]
        forward, backward = [up, down], [down, up]
    count = len(outer_weights)

    whole_track = lax.all_gather(track_weight, "sample", axis=0, tiled=True)
    piece = channels // n_sample
    own_piece = lax.dynamic_slice_in_dim(point_weight, sample * piece, piece, 0)
    other_point = lax.all_gather(flip(own_piece, "head"), "sample", axis=0, tiled=True)

    feat = features.reshape(rows, channels)
    feat_wide = feat.astype(F32)
    activated = gelu_value(feat_wide).astype(BF16)
    sent = [dot(activated, weight, ((1,), (0,))).astype(BF16) for weight in outer_weights]
    arrived = [lax.ppermute(term, "seq", pairs) for term, pairs in zip(sent, forward)]
    middle = dot(activated, taps[1], ((1,), (0,)))
    for term in arrived:
        middle = middle + term.astype(F32)
    middle_b = middle.astype(BF16)
    other_middle = flip(middle_b, "head")
    hidden = gelu_value(middle).astype(BF16)
    other_hidden = gelu_value(other_middle.astype(F32)).astype(BF16)
    block_out = (
        feat_wide
        + dot(hidden, point_weight, ((1,), (1,)))
        + dot(other_hidden, other_point, ((1,), (1,)))
    ).astype(BF16)

    def rows_of(value, which):
        return lax.dynamic_slice_in_dim(value, which * half, half, 0)

    cotangent = track_cotangent.reshape(rows, whole_track.shape[1])

    def track_part(which):
        scores = dot(rows_of(block_out, which), whole_track, ((1,), (0,)))
        grad = (rows_of(cotangent, which).astype(F32) * jax.nn.sigmoid(scores)).astype(BF16)
        return dot(grad, whole_track, ((1,), (1,)))

    theirs = flip(track_part(1 - head).astype(BF16), "head")
    out_grad = track_part(head) + theirs.astype(F32)
    out_grad_b = out_grad.astype(BF16)
    other_out_grad = flip(out_grad_b, "head")

    grad_own = (
        dot(out_grad_b, point_weight, ((1,), (0,))) * gelu_slope(rows_of(middle, head))
    ).astype(BF16)
    grad_other = (
        dot(out_grad_b, other_point, ((1,), (0,)))
        * gelu_slope(rows_of(other_middle, head).astype(F32))
    ).astype(BF16)
    middle_grad = in_order(grad_own, flip(grad_other, "head"), head, 0)
    moved = []
    for pairs in backward:
        straight = lax.ppermute(grad_own, "seq", pairs)
        crossed = lax.ppermute(
            grad_other,
            ("seq", "head"),
            [(2 * i + k, 2 * j + 1 - k) for i, j in pairs for k in range(2)],
        )
        moved.append(in_order(straight, crossed, head, 0))

    act_part = dot(middle_grad, taps[1], ((1,), (1,)))
    for field, weight in zip(moved, outer_weights):
        act_part = act_part + dot(field, weight, ((1,), (1,)))
    act_theirs = flip(rows_of(act_part, 1 - head).astype(BF16), "head")
    act_grad = rows_of(act_part, head) + act_theirs.astype(F32)
    input_half = (out_grad + act_grad * gelu_slope(rows_of(feat_wide, head))).astype(BF16)
    input_grad = in_order(input_half, flip(input_half, "head"), head, 0)

    seq_bits = bits_of(n_seq)
    block = channels // (n_seq * n_sample)
    shape = (2,) * seq_bits + (n_sample, block)

    def halve(value, left, bit, keep_last=False):
        at = left.index(bit)
        if bit < 0:
            mine, give = own_first(value, at, sample)
            got = flip(give.astype(BF16), "sample")
        else:
            mine, give = own_first(value, at, (seq >> bit) & 1)
            got = flip(give.astype(BF16), "seq", 1 << bit)
        rest = [b for b in left if b != bit]
        return (mine, got, rest) if keep_last else (mine.astype(F32) + got.astype(F32), rest)

    def reduced(value, order, apart=False):
        left = list(range(seq_bits - 1, -1, -1)) + [-1]
        value = value.reshape(shape + value.shape[1:])
        for bit in order[:-1]:
            value, left = halve(value, left, bit)
            value = value.astype(BF16)
        mine, got, _ = halve(value, left, order[-1], True)
        if apart:
            return mine.astype(F32), got.astype(F32)
        return mine.astype(F32) + got.astype(F32)

    order_a = [-1] + list(range(seq_bits))
    order_b = [-1] + list(range(1, seq_bits - 1)) + [0, seq_bits - 1]
    whole_out_grad = in_order(out_grad_b, other_out_grad, head, 0)
    point_grad = reduced(dot(whole_out_grad, hidden, ((0,), (0,))), order_a)
    mid_tap = reduced(dot(activated, middle_grad, ((0,), (0,))), order_b)
    if one_sided:
        mine, got = reduced(dot(activated, moved[0], ((0,), (0,))), order_a, True)
        outer = [jnp.where(low, mine, got), jnp.where(low, got, mine)]
    else:
        outer = [reduced(dot(activated, field, ((0,), (0,))), order_a) for field in moved]
    dilated_grad = jnp.transpose(jnp.stack([outer[0], mid_tap, outer[1]]), (1, 0, 2))
    return (input_grad.reshape(samples, positions, channels), dilated_grad, point_grad)


def wide(ref):
    return ref[...].astype(F32)


def kernel_call(kernel, outs, ins, after=None, scratch=(), spaces={}):
    place, arrays = ins[0], list(ins[1:])
    in_specs = [pl.BlockSpec(memory_space=pltpu.SMEM)]
    in_specs += [
        pl.BlockSpec(memory_space=spaces.get(k + 1, pltpu.VMEM)) for k in range(len(arrays))
    ]
    number = len(arrays) + 1
    if after is not None:
        arrays.append(after)
        in_specs.append(pl.BlockSpec(memory_space=pl.ANY))

    def run(*refs):
        given = refs[:number]
        kernel(*given, *refs[len(in_specs):])

    return pl.pallas_call(
        run,
        out_shape=[jax.ShapeDtypeStruct(s, d) for s, d in outs],
        in_specs=in_specs,
        out_specs=[pl.BlockSpec(memory_space=pltpu.VMEM)] * len(outs),
        scratch_shapes=list(scratch),
        compiler_params=pltpu.CompilerParams(vmem_limit_bytes=VMEM),
        cost_estimate=LITTLE,
        name=kernel.__name__,
    )(place, *arrays)


def in_hbm(value):
    return pltpu.with_memory_space_constraint(value, pltpu.HBM)


NN = ((1,), (0,))
NT = ((1,), (1,))
HEAD, SAMPLE, TOP, MID, LOWEST = 1, 2, 3, 4, 5


def outer_term(place, feat, taps, acted, term, rows, weight, sems):
    steps = sems.shape[1]
    depth = rows.shape[1] // steps
    parts = [pl.ds(k * depth, depth) for k in range(steps)]
    feats = [
        pltpu.make_async_copy(feat.at[:, part], rows.at[:, part], sems.at[0, k])
        for k, part in enumerate(parts)
    ]
    weights = [
        pltpu.make_async_copy(taps.at[place[0], part], weight.at[part], sems.at[1, k])
        for k, part in enumerate(parts)
    ]
    for pair in zip(feats, weights):
        for copy in pair:
            copy.start()
    total = None
    for copy, coming, part in zip(feats, weights, parts):
        copy.wait()
        act = gelu_value(rows[:, part].astype(F32)).astype(BF16)
        acted[:, part] = act
        coming.wait()
        value = dot(act, weight[part, :], NN)
        total = value if total is None else total + value
    term[...] = total.astype(BF16)


def piece_of(place, point, piece, sem):
    number = piece.shape[0]
    own = pl.ds(pl.multiple_of(place[SAMPLE] * number, number), number)
    copy = pltpu.make_async_copy(point.at[own], piece, sem)
    copy.start()
    copy.wait()


def middle_term(place, acted, weight, middle, kept, given):
    act = acted[...]
    middle[...] = dot(act, weight[1], NN)
    part_channels(place, act.T, kept, [given])


def part_channels(place, turned, kept, given):
    groups, block, rows = kept.shape
    split = turned.reshape(groups, 2, block, rows)
    first = place[SAMPLE] == 0
    kept[...] = jnp.where(first, split[:, 0], split[:, 1])
    theirs = jnp.where(first, split[:, 1], split[:, 0])
    number = groups // len(given)
    for k, part in enumerate(given):
        part[...] = theirs[k * number : (k + 1) * number]


def add_terms(place, middle, arrived, total, sent):
    value = middle[...] + wide(arrived)
    total[...] = value
    sent[...] = value.astype(BF16)


def own_hidden(place, middle, feat, point, hidden, block):
    hid = gelu_value(middle[...]).astype(BF16)
    hidden[...] = hid
    block[...] = wide(feat) + dot(hid, point[...], NT)


def tracks(place, block, other_middle, near, far, cotangent, *rest):
    *points, give, block_b, grads = rest
    sample = place[SAMPLE]
    piece = block_b.shape[2]
    width = other_middle.shape[1]
    hid = gelu_value(wide(other_middle)).astype(BF16)
    ahead = 0
    for point in points:
        number = point.shape[0]
        which, column = (sample, ahead) if ahead < piece else (1 - sample, ahead - piece)
        columns = pl.ds(pl.multiple_of(which * piece + column, number), number)
        value = block[:, columns] + dot(hid, point[...], NT)
        block_b[which, :, column : column + number] = value.astype(BF16)
        ahead += number
    number = near.shape[1]
    tile = width if number % width == 0 else number
    for start in range(0, number, tile):
        columns = slice(start, start + tile)
        scores = dot(block_b[sample], near[:, columns], NN)
        scores += dot(block_b[1 - sample], far[:, columns], NN)
        grads[:, columns] = (wide(cotangent.at[:, columns]) * jax.nn.sigmoid(scores)).astype(BF16)
    for which, weight in ((sample, near), (1 - sample, far)):
        columns = pl.ds(pl.multiple_of(which * piece, piece), piece)
        give[:, columns] = dot(grads[...], weight[...], NT).astype(BF16)


def slopes(place, middle, feat, slope, slope_feat):
    slope[...] = gelu_slope(middle[...])
    slope_feat[...] = gelu_slope(wide(feat))


def middle_grads(
    place, own, theirs, point, slope, out_grad, middle_grad, kept, first, second, turned
):
    total = wide(own) + wide(theirs)
    out_grad[...] = total
    total_b = total.astype(BF16)
    grad = (dot(total_b, point[...], NN) * slope[...]).astype(BF16)
    middle_grad[...] = grad
    turned[...] = grad.T
    part_channels(place, total_b.T, kept, [first, second])


def each_chip(place, keep, along, across, both, values):
    mid, lowest = place[MID], place[LOWEST]
    for i, j, out in (
        (1 - mid, 1 - lowest, both),
        (1 - mid, lowest, along),
        (mid, 1 - lowest, across),
        (mid, lowest, keep),
    ):

        def left(ref):
            groups, at = ref.shape[0], 2 * i + j
            return jnp.concatenate([ref[at], ref[groups // 2 + at]], axis=0)

        for k, value in enumerate(values(left)):
            width = value.shape[1]
            shape = (2, out.shape[1], width)
            out[:, :, k * width : (k + 1) * width] = value.astype(out.dtype).reshape(shape)


def middle_products(
    place, acts, other_acts, outs, first, second, other_mid, middle_grad, hidden, other_hidden,
    keep, along, across, both, other_outs,
):
    number = first.shape[0]
    other_outs[:number] = first[...]
    other_outs[number:] = second[...]

    def values(left):
        return (
            dot(left(acts), middle_grad[...], NN) + dot(left(other_acts), other_mid[...], NT),
            dot(left(outs), hidden[...], NN) + dot(left(other_outs), other_hidden[...], NN),
        )

    each_chip(place, keep, along, across, both, values)


def outer_products(
    place, acts, other_acts, moved, first, second, keep, along, across, both, other_moved
):
    number = first.shape[0]
    other_moved[:number] = first[...]
    other_moved[number:] = second[...]

    def values(left):
        return (dot(left(acts), moved[...], NN) + dot(left(other_acts), other_moved[...], NN),)

    each_chip(place, keep, along, across, both, values)


def act_part(first):
    def act_rows(place, middle_grad, moved, weight, give):
        rows = slice(first, first + give.shape[0])
        value = dot(middle_grad[rows, :], weight[1], NT)
        give[...] = (value + dot(moved[rows, :], weight[place[0]], NT)).astype(BF16)

    return act_rows


def chips_sum(place, kept, along, across, both, keep, give):
    def part(i):
        total = kept[i] + along[i].astype(F32)
        return total + across[i].astype(F32) + both[i].astype(F32)

    give[...] = part(1 - place[TOP]).astype(BF16)
    keep[...] = part(place[TOP])


def finish(
    place, out_grad, slope, act_one, got_one, act_two, got_two, mid_kept, mid_got, kept, got,
    dilated, point, result,
):
    width = point.shape[1]
    dilated[place[0]] = kept[...]
    dilated[2 - place[0]] = wide(got)
    dilated[1] = mid_kept[:, :width] + mid_got[:, :width].astype(F32)
    point[...] = mid_kept[:, width:] + mid_got[:, width:].astype(F32)
    first = 0
    for own, theirs in ((act_one, got_one), (act_two, got_two)):
        rows = slice(first, first + own.shape[0])
        act_grad = wide(own) + wide(theirs)
        result[rows, :] = (out_grad[rows, :] + act_grad * slope[rows, :]).astype(BF16)
        first += own.shape[0]


def body(features, dilated_weight, point_weight, track_weight, track_cotangent):
    samples, positions, channels = features.shape
    n_seq, n_sample, n_head = (lax.axis_size(a) for a in ("seq", "sample", "head"))
    dist = DILATION_STEP // positions
    if not (n_seq == 2 * dist and bits_of(n_seq) == 3 and n_sample == 2 and n_head == 2 and samples == 1):
        return general(features, dilated_weight, point_weight, track_weight, track_cotangent)
    rows = positions
    half = rows // 2
    width = dilated_weight.shape[2]
    tracks_here = track_weight.shape[1]
    piece = channels // n_sample
    block = channels // (n_seq * n_sample)
    seq, head, sample = lax.axis_index("seq"), lax.axis_index("head"), lax.axis_index("sample")
    place = jnp.stack(
        [jnp.where(seq < dist, 0, 2), head, sample, (seq >> 2) & 1, (seq >> 1) & 1, seq & 1]
    ).astype(jnp.int32)
    taps = jnp.transpose(dilated_weight, (1, 0, 2))
    feat = features.reshape(rows, channels)
    cotangent = track_cotangent.reshape(rows, tracks_here)
    pairs = [(i, (i + dist) % n_seq) for i in range(n_seq)]

    (own_piece,) = kernel_call(
        piece_of,
        [((piece, width), BF16)],
        [place, in_hbm(point_weight)],
        scratch=[pltpu.SemaphoreType.DMA],
        spaces={1: pltpu.HBM},
    )
    near = flip(own_piece, "head")
    cut = piece // 3
    points = [near] + [flip(near[k : k + cut], "sample") for k in range(0, piece, cut)]
    far_track = flip(track_weight, "sample")
    acted, term = kernel_call(
        outer_term,
        [((rows, channels), BF16), ((rows, width), BF16)],
        [place, in_hbm(feat), in_hbm(taps)],
        own_piece,
        scratch=[
            pltpu.VMEM((rows, channels), BF16),
            pltpu.VMEM((channels, width), BF16),
            pltpu.SemaphoreType.DMA((2, 3)),
        ],
        spaces={1: pltpu.HBM, 2: pltpu.HBM},
    )
    arrived = lax.ppermute(term, "seq", pairs)
    groups = n_seq

    turned = ((groups, block, rows), BF16)
    middle, acts, acts_given = kernel_call(
        middle_term,
        [((rows, width), F32), turned, turned],
        [place, acted, taps],
    )
    middle, middle_b = kernel_call(
        add_terms, [((rows, width), F32), ((rows, width), BF16)], [place, middle, arrived], acts
    )
    other_middle = flip(middle_b, "head")
    hidden, block_part = kernel_call(
        own_hidden,
        [((rows, width), BF16), ((rows, channels), F32)],
        [place, middle, feat, point_weight],
    )
    (give,) = kernel_call(
        tracks,
        [((rows, channels), BF16)],
        [place, block_part, other_middle, track_weight, far_track, cotangent, *points],
        scratch=[
            pltpu.VMEM((n_sample, rows, piece), BF16),
            pltpu.VMEM((rows, tracks_here), BF16),
        ],
    )
    got = flip(give, "head")
    slope, slope_feat = kernel_call(
        slopes, [((rows, width), F32), ((rows, channels), F32)], [place, middle, feat], give
    )
    out_grad, middle_grad, outs, *given = kernel_call(
        middle_grads,
        [((rows, channels), F32), ((rows, width), BF16), turned]
        + [((groups // 2, block, rows), BF16)] * 2
        + [((width, rows), BF16)],
        [place, give, got, point_weight, slope],
    )
    moved = lax.ppermute(middle_grad, "seq", pairs)

    def traded(kernel, columns, ins, after=None, scratch=()):
        part = (2, block, columns)
        keep, *gives = kernel_call(
            kernel, [(part, F32)] + [(part, BF16)] * 3, [place, *ins], after, scratch
        )
        return keep, [flip(value, "seq", step) for value, step in zip(gives, (2, 1, 3))]

    def halved(kept, got, columns, after):
        part = (block, columns)
        kept, given = kernel_call(
            chips_sum, [(part, F32), (part, BF16)], [place, kept, *got], after
        )
        return kept, flip(given, "seq", 4)

    other_acts, other_hidden = flip(acts_given, "sample"), flip(hidden, "sample")
    mid_kept, mid_got = traded(
        middle_products,
        2 * width,
        [acts, other_acts, outs]
        + [flip(part, "sample") for part in given]
        + [middle_grad, hidden, other_hidden],
        scratch=[pltpu.VMEM((groups, block, rows), BF16)],
    )
    other_moved = [flip(moved[k : k + half], "sample") for k in (0, half)]
    act_one = kernel_call(
        act_part(0), [((half, channels), BF16)], [place, middle_grad, moved, taps], mid_kept
    )[0]
    kept, got = traded(
        outer_products,
        width,
        [acts, other_acts, moved, *other_moved],
        act_one,
        scratch=[pltpu.VMEM((rows, width), BF16)],
    )
    act_two = kernel_call(
        act_part(half), [((half, channels), BF16)], [place, middle_grad, moved, taps], kept
    )[0]
    mid_kept, mid_got = halved(mid_kept, mid_got, 2 * width, act_two)
    kept, got = halved(kept, got, width, mid_kept)
    dilated_grad, point_grad, input_grad = kernel_call(
        finish,
        [((3, block, width), F32), ((block, width), F32), ((rows, channels), BF16)],
        [
            place, out_grad, slope_feat, act_one, flip(act_one, "head"),
            act_two, flip(act_two, "head"), mid_kept, mid_got, kept, got,
        ],
    )
    dilated_grad = jnp.transpose(dilated_grad, (1, 0, 2))
    return (input_grad.reshape(samples, positions, channels), dilated_grad, point_grad)


def solution(mesh):
    placed = (
        P("sample", "seq", None),
        P(None, None, "head"),
        P(None, "head"),
        P("sample", "head"),
        P("sample", "seq", "head"),
    )
    return jax.shard_map(
        body,
        mesh=mesh,
        in_specs=placed,
        out_specs=(
            P("sample", "seq", None),
            P(("seq", "sample"), None, "head"),
            P(("seq", "sample"), "head"),
        ),
        check_vma=False,
    )
```

```python
import jax
import jax.numpy as jnp
from jax import lax
from jax.experimental import pallas as pl
from jax.experimental.pallas import tpu as pltpu
from jax.sharding import PartitionSpec as P

DILATION_STEP = 1024
BF16 = jnp.bfloat16
F32 = jnp.float32
VMEM = 24 * 2**20
LITTLE = pl.CostEstimate(flops=1, bytes_accessed=1, transcendentals=0)


def gelu_value(value):
    inner = 0.7978845608 * (value + 0.044715 * value * value * value)
    return 0.5 * value * (1.0 + jnp.tanh(inner))


def gelu_slope(value):
    inner = 0.7978845608 * (value + 0.044715 * value * value * value)
    tangent = jnp.tanh(inner)
    return 0.5 * (1.0 + tangent) + 0.5 * value * (1.0 - tangent * tangent) * 0.7978845608 * (
        1.0 + 3.0 * 0.044715 * value * value
    )


def dot(left, right, contract):
    return lax.dot_general(left, right, (contract, ((), ())), preferred_element_type=F32)


def flip(value, axis, step=1):
    count = lax.axis_size(axis)
    return lax.ppermute(value, axis, [(i, i ^ step) for i in range(count)])


def own_first(value, axis_at, bit):
    return (
        lax.dynamic_index_in_dim(value, bit, axis_at, keepdims=False),
        lax.dynamic_index_in_dim(value, 1 - bit, axis_at, keepdims=False),
    )


def in_order(own, other, bit, axis):
    first = jnp.where(bit == 0, own, other)
    second = jnp.where(bit == 0, other, own)
    return jnp.concatenate([first, second], axis=axis)


def bits_of(count):
    return count.bit_length() - 1


def general(features, dilated_weight, point_weight, track_weight, track_cotangent):
    samples, positions, channels = features.shape
    rows = samples * positions
    half = rows // 2
    width = dilated_weight.shape[2]
    n_seq, n_sample = lax.axis_size("seq"), lax.axis_size("sample")
    seq, head, sample = lax.axis_index("seq"), lax.axis_index("head"), lax.axis_index("sample")
    dist = DILATION_STEP // positions
    one_sided = n_seq == 2 * dist
    low = seq < dist
    taps = jnp.transpose(dilated_weight, (1, 0, 2))

    if one_sided:
        outer_weights = [lax.dynamic_index_in_dim(taps, jnp.where(low, 0, 2), 0, keepdims=False)]
        pairs = [(i, (i + dist) % n_seq) for i in range(n_seq)]
        forward, backward = [pairs], [pairs]
    else:
        outer_weights = [taps[0], taps[2]]
        up = [(i, i + dist) for i in range(n_seq - dist)]
        down = [(i + dist, i) for i in range(n_seq - dist)]
        forward, backward = [up, down], [down, up]
    count = len(outer_weights)

    whole_track = lax.all_gather(track_weight, "sample", axis=0, tiled=True)
    piece = channels // n_sample
    own_piece = lax.dynamic_slice_in_dim(point_weight, sample * piece, piece, 0)
    other_point = lax.all_gather(flip(own_piece, "head"), "sample", axis=0, tiled=True)

    feat = features.reshape(rows, channels)
    feat_wide = feat.astype(F32)
    activated = gelu_value(feat_wide).astype(BF16)
    sent = [dot(activated, weight, ((1,), (0,))).astype(BF16) for weight in outer_weights]
    arrived = [lax.ppermute(term, "seq", pairs) for term, pairs in zip(sent, forward)]
    middle = dot(activated, taps[1], ((1,), (0,)))
    for term in arrived:
        middle = middle + term.astype(F32)
    middle_b = middle.astype(BF16)
    other_middle = flip(middle_b, "head")
    hidden = gelu_value(middle).astype(BF16)
    other_hidden = gelu_value(other_middle.astype(F32)).astype(BF16)
    block_out = (
        feat_wide
        + dot(hidden, point_weight, ((1,), (1,)))
        + dot(other_hidden, other_point, ((1,), (1,)))
    ).astype(BF16)

    def rows_of(value, which):
        return lax.dynamic_slice_in_dim(value, which * half, half, 0)

    cotangent = track_cotangent.reshape(rows, whole_track.shape[1])

    def track_part(which):
        scores = dot(rows_of(block_out, which), whole_track, ((1,), (0,)))
        grad = (rows_of(cotangent, which).astype(F32) * jax.nn.sigmoid(scores)).astype(BF16)
        return dot(grad, whole_track, ((1,), (1,)))

    theirs = flip(track_part(1 - head).astype(BF16), "head")
    out_grad = track_part(head) + theirs.astype(F32)
    out_grad_b = out_grad.astype(BF16)
    other_out_grad = flip(out_grad_b, "head")

    grad_own = (
        dot(out_grad_b, point_weight, ((1,), (0,))) * gelu_slope(rows_of(middle, head))
    ).astype(BF16)
    grad_other = (
        dot(out_grad_b, other_point, ((1,), (0,)))
        * gelu_slope(rows_of(other_middle, head).astype(F32))
    ).astype(BF16)
    middle_grad = in_order(grad_own, flip(grad_other, "head"), head, 0)
    moved = []
    for pairs in backward:
        straight = lax.ppermute(grad_own, "seq", pairs)
        crossed = lax.ppermute(
            grad_other,
            ("seq", "head"),
            [(2 * i + k, 2 * j + 1 - k) for i, j in pairs for k in range(2)],
        )
        moved.append(in_order(straight, crossed, head, 0))

    act_part = dot(middle_grad, taps[1], ((1,), (1,)))
    for field, weight in zip(moved, outer_weights):
        act_part = act_part + dot(field, weight, ((1,), (1,)))
    act_theirs = flip(rows_of(act_part, 1 - head).astype(BF16), "head")
    act_grad = rows_of(act_part, head) + act_theirs.astype(F32)
    input_half = (out_grad + act_grad * gelu_slope(rows_of(feat_wide, head))).astype(BF16)
    input_grad = in_order(input_half, flip(input_half, "head"), head, 0)

    seq_bits = bits_of(n_seq)
    block = channels // (n_seq * n_sample)
    shape = (2,) * seq_bits + (n_sample, block)

    def halve(value, left, bit, keep_last=False):
        at = left.index(bit)
        if bit < 0:
            mine, give = own_first(value, at, sample)
            got = flip(give.astype(BF16), "sample")
        else:
            mine, give = own_first(value, at, (seq >> bit) & 1)
            got = flip(give.astype(BF16), "seq", 1 << bit)
        rest = [b for b in left if b != bit]
        return (mine, got, rest) if keep_last else (mine.astype(F32) + got.astype(F32), rest)

    def reduced(value, order, apart=False):
        left = list(range(seq_bits - 1, -1, -1)) + [-1]
        value = value.reshape(shape + value.shape[1:])
        for bit in order[:-1]:
            value, left = halve(value, left, bit)
            value = value.astype(BF16)
        mine, got, _ = halve(value, left, order[-1], True)
        if apart:
            return mine.astype(F32), got.astype(F32)
        return mine.astype(F32) + got.astype(F32)

    order_a = [-1] + list(range(seq_bits))
    order_b = [-1] + list(range(1, seq_bits - 1)) + [0, seq_bits - 1]
    whole_out_grad = in_order(out_grad_b, other_out_grad, head, 0)
    point_grad = reduced(dot(whole_out_grad, hidden, ((0,), (0,))), order_a)
    mid_tap = reduced(dot(activated, middle_grad, ((0,), (0,))), order_b)
    if one_sided:
        mine, got = reduced(dot(activated, moved[0], ((0,), (0,))), order_a, True)
        outer = [jnp.where(low, mine, got), jnp.where(low, got, mine)]
    else:
        outer = [reduced(dot(activated, field, ((0,), (0,))), order_a) for field in moved]
    dilated_grad = jnp.transpose(jnp.stack([outer[0], mid_tap, outer[1]]), (1, 0, 2))
    return (input_grad.reshape(samples, positions, channels), dilated_grad, point_grad)


def wide(ref):
    return ref[...].astype(F32)


def kernel_call(kernel, outs, ins, after=None, scratch=(), spaces={}):
    place, arrays = ins[0], list(ins[1:])
    in_specs = [pl.BlockSpec(memory_space=pltpu.SMEM)]
    in_specs += [
        pl.BlockSpec(memory_space=spaces.get(k + 1, pltpu.VMEM)) for k in range(len(arrays))
    ]
    number = len(arrays) + 1
    if after is not None:
        arrays.append(after)
        in_specs.append(pl.BlockSpec(memory_space=pl.ANY))

    def run(*refs):
        given = refs[:number]
        kernel(*given, *refs[len(in_specs):])

    return pl.pallas_call(
        run,
        out_shape=[jax.ShapeDtypeStruct(s, d) for s, d in outs],
        in_specs=in_specs,
        out_specs=[pl.BlockSpec(memory_space=pltpu.VMEM)] * len(outs),
        scratch_shapes=list(scratch),
        compiler_params=pltpu.CompilerParams(vmem_limit_bytes=VMEM),
        cost_estimate=LITTLE,
        name=kernel.__name__,
    )(place, *arrays)


def in_hbm(value):
    return pltpu.with_memory_space_constraint(value, pltpu.HBM)


NN = ((1,), (0,))
NT = ((1,), (1,))
HEAD, SAMPLE, TOP, MID, LOWEST = 1, 2, 3, 4, 5


def outer_term(place, feat, taps, acted, term, rows, weight, sems):
    steps = sems.shape[1]
    depth = rows.shape[1] // steps
    parts = [pl.ds(k * depth, depth) for k in range(steps)]
    feats = [
        pltpu.make_async_copy(feat.at[:, part], rows.at[:, part], sems.at[0, k])
        for k, part in enumerate(parts)
    ]
    weights = [
        pltpu.make_async_copy(taps.at[place[0], part], weight.at[part], sems.at[1, k])
        for k, part in enumerate(parts)
    ]
    for pair in zip(feats, weights):
        for copy in pair:
            copy.start()
    total = None
    for copy, coming, part in zip(feats, weights, parts):
        copy.wait()
        act = gelu_value(rows[:, part].astype(F32)).astype(BF16)
        acted[:, part] = act
        coming.wait()
        value = dot(act, weight[part, :], NN)
        total = value if total is None else total + value
    term[...] = total.astype(BF16)


def middle_term(place, acted, weight, middle, kept, given):
    act = acted[...]
    middle[...] = dot(act, weight[1], NN)
    part_channels(place, act.T, kept, given)


def part_channels(place, turned, kept, given):
    groups, block, rows = kept.shape
    split = turned.reshape(groups, 2, block, rows)
    first = place[SAMPLE] == 0
    kept[...] = jnp.where(first, split[:, 0], split[:, 1])
    given[...] = jnp.where(first, split[:, 1], split[:, 0])


def add_terms(place, middle, arrived, total, sent):
    value = middle[...] + wide(arrived)
    total[...] = value
    sent[...] = value.astype(BF16)


def own_hidden(place, middle, feat, point, direct, *rest):
    *passed, hidden, block, other_point = rest
    hid = gelu_value(middle[...]).astype(BF16)
    hidden[...] = hid
    block[...] = wide(feat) + dot(hid, point[...], NT)
    first = 0
    for part in passed:
        rows = slice(first, first + part.shape[0])
        other_point[rows, :] = jnp.where(place[SAMPLE] == 0, direct[rows, :], part[...])
        first += part.shape[0]


def slopes(place, middle, feat, slope, slope_feat):
    slope[...] = gelu_slope(middle[...])
    slope_feat[...] = gelu_slope(wide(feat))


def tracks(
    place, block, other_middle, near, far, cotangent, point, other_point,
    part, other_hidden, grad_kept, grad_given, block_b, grads,
):
    sample = place[SAMPLE]
    piece = block_b.shape[2]
    width = other_middle.shape[1]
    hid = gelu_value(wide(other_middle)).astype(BF16)
    other_hidden[...] = hid
    for which in range(2):
        columns = slice(which * piece, (which + 1) * piece)
        value = block[:, columns] + dot(hid, other_point[columns, :], NT)
        block_b[which] = value.astype(BF16)
    number = near.shape[1]
    tile = width if number % width == 0 else number
    for start in range(0, number, tile):
        columns = slice(start, start + tile)
        scores = dot(block_b[sample], near[:, columns], NN)
        scores += dot(block_b[1 - sample], far[:, columns], NN)
        grads[:, columns] = (wide(cotangent.at[:, columns]) * jax.nn.sigmoid(scores)).astype(BF16)
    kept = given = 0.0
    for which, weight in ((sample, near), (1 - sample, far)):
        columns = pl.ds(pl.multiple_of(which * piece, piece), piece)
        value = dot(grads[...], weight[...], NT).astype(BF16)
        part[:, columns] = value
        kept += dot(value, point[columns, :], NN)
        given += dot(value, other_point[columns, :], NN)
    grad_kept[...] = kept
    grad_given[...] = given.astype(BF16)


def turn_parts(place, part, far_middle, kept, far_hidden, *rest):
    *pieces, given = rest
    far_hidden[...] = gelu_value(wide(far_middle)).astype(BF16)
    part_channels(place, part[...].T, kept, given)
    first = 0
    for piece in pieces:
        piece[...] = given[first : first + piece.shape[0]]
        first += piece.shape[0]


def middle_grads(place, kept, got, slope, middle_grad):
    middle_grad[...] = ((kept[...] + wide(got)) * slope[...]).astype(BF16)


def joined(pieces, whole):
    first = 0
    for piece in pieces:
        whole[first : first + piece.shape[0]] = piece[...]
        first += piece.shape[0]


def each_chip(place, keep, along, across, both, values):
    mid, lowest = place[MID], place[LOWEST]
    for i, j, out in (
        (1 - mid, 1 - lowest, both),
        (1 - mid, lowest, along),
        (mid, 1 - lowest, across),
        (mid, lowest, keep),
    ):

        def left(ref):
            groups, at = ref.shape[0], 2 * i + j
            return jnp.concatenate([ref[at], ref[groups // 2 + at]], axis=0)

        for k, value in enumerate(values(left)):
            width = value.shape[1]
            shape = (2, out.shape[1], width)
            out[:, :, k * width : (k + 1) * width] = value.astype(out.dtype).reshape(shape)


def point_products(
    place, outs, hidden, other_hidden, far_hidden, far_other, *rest
):
    *pieces, keep, along, across, both, other_outs = rest
    joined(pieces, other_outs)

    def values(left):
        own, other = left(outs), left(other_outs)
        return (
            dot(own, hidden[...], NN) + dot(other, far_hidden[...], NN),
            dot(own, other_hidden[...], NN) + dot(other, far_other[...], NN),
        )

    each_chip(place, keep, along, across, both, values)


def tap_products(
    place, acts, other_acts, middle_grad, other_middle_grad, moved, other_moved,
    keep, along, across, both,
):
    def values(left):
        own, other = left(acts), left(other_acts)
        return (
            dot(own, middle_grad[...], NN) + dot(other, other_middle_grad[...], NN),
            dot(own, moved[...], NN) + dot(other, other_moved[...], NN),
        )

    each_chip(place, keep, along, across, both, values)


def act_part(place, middle_grad, moved, weight, part, slope, give):
    value = dot(middle_grad[...], weight[1], NT) + dot(moved[...], weight[place[0]], NT)
    give[...] = (wide(part) + value * slope[...]).astype(BF16)


def over_chips(at, kept, *arrived):
    total = kept[at]
    for part in arrived:
        total += part[at].astype(F32)
    return total


def point_sum(place, kept, along, across, both, keep, give):
    width = keep.shape[2]
    for at in range(2):
        total = over_chips(at, kept, along, across, both)
        keep[at] = total[:, :width]
        give[at] = total[:, width:].astype(BF16)


def point_half(place, kept, got, keep, give):
    top = place[TOP]
    keep[...] = over_chips(top, kept, got)
    give[...] = over_chips(1 - top, kept, got).astype(BF16)


def taps_sum(place, *refs):
    *parts, keep, give = refs
    top = place[TOP]
    keep[...] = over_chips(top, *parts)
    give[...] = over_chips(1 - top, *parts).astype(BF16)


def finish(place, own, theirs, point_kept, point_got, kept, got, dilated, point, result):
    width = point.shape[1]
    dilated[1] = kept[:, :width] + got[:, :width].astype(F32)
    dilated[place[0]] = kept[:, width:]
    dilated[2 - place[0]] = got[:, width:].astype(F32)
    point[...] = point_kept[...] + wide(point_got)
    result[...] = (wide(own) + wide(theirs)).astype(BF16)


def body(features, dilated_weight, point_weight, track_weight, track_cotangent):
    samples, positions, channels = features.shape
    n_seq, n_sample, n_head = (lax.axis_size(a) for a in ("seq", "sample", "head"))
    dist = DILATION_STEP // positions
    if not (n_seq == 2 * dist and bits_of(n_seq) == 3 and n_sample == 2 and n_head == 2 and samples == 1):
        return general(features, dilated_weight, point_weight, track_weight, track_cotangent)
    rows = positions
    half = rows // 2
    width = dilated_weight.shape[2]
    tracks_here = track_weight.shape[1]
    piece = channels // n_sample
    block = channels // (n_seq * n_sample)
    seq, head, sample = lax.axis_index("seq"), lax.axis_index("head"), lax.axis_index("sample")
    place = jnp.stack(
        [jnp.where(seq < dist, 0, 2), head, sample, (seq >> 2) & 1, (seq >> 1) & 1, seq & 1]
    ).astype(jnp.int32)
    taps = jnp.transpose(dilated_weight, (1, 0, 2))
    feat = features.reshape(rows, channels)
    cotangent = track_cotangent.reshape(rows, tracks_here)
    pairs = [(i, (i + dist) % n_seq) for i in range(n_seq)]

    direct = lax.ppermute(point_weight, ("head", "sample"), [(0, 2), (2, 0)])
    cut = channels // 3
    passed = [
        lax.ppermute(direct[k : k + cut], "sample", [(0, 1)]) for k in range(0, channels, cut)
    ]
    far_track = flip(track_weight, "sample")
    acted, term = kernel_call(
        outer_term,
        [((rows, channels), BF16), ((rows, width), BF16)],
        [place, in_hbm(feat), in_hbm(taps)],
        scratch=[
            pltpu.VMEM((rows, channels), BF16),
            pltpu.VMEM((channels, width), BF16),
            pltpu.SemaphoreType.DMA((2, 3)),
        ],
        spaces={1: pltpu.HBM, 2: pltpu.HBM},
    )
    arrived = lax.ppermute(term, "seq", pairs)
    groups = n_seq

    turned = ((groups, block, rows), BF16)
    middle, acts, acts_given = kernel_call(
        middle_term,
        [((rows, width), F32), turned, turned],
        [place, acted, taps],
    )
    middle, middle_b = kernel_call(
        add_terms, [((rows, width), F32), ((rows, width), BF16)], [place, middle, arrived], acts
    )
    other_middle = flip(middle_b, "head")
    hidden, block_part, other_point = kernel_call(
        own_hidden,
        [((rows, width), BF16), ((rows, channels), F32), ((channels, width), BF16)],
        [place, middle, feat, point_weight, direct, *passed],
    )
    slope, slope_feat = kernel_call(
        slopes,
        [((rows, width), F32), ((rows, channels), F32)],
        [place, middle, feat],
        block_part,
    )
    part, other_hidden, grad_kept, grad_given = kernel_call(
        tracks,
        [((rows, channels), BF16), ((rows, width), BF16), ((rows, width), F32), ((rows, width), BF16)],
        [
            place, block_part, other_middle, track_weight, far_track, cotangent, point_weight,
            other_point,
        ],
        slope,
        scratch=[
            pltpu.VMEM((n_sample, rows, piece), BF16),
            pltpu.VMEM((rows, tracks_here), BF16),
        ],
    )
    grad_got = flip(grad_given, "head")
    far_hidden = flip(hidden, "sample")

    def traded(kernel, columns, ins, after=None, scratch=()):
        shape = (2, block, columns)
        keep, *gives = kernel_call(
            kernel, [(shape, F32)] + [(shape, BF16)] * 3, [place, *ins], after, scratch
        )
        return keep, *[flip(value, "seq", step) for value, step in zip(gives, (2, 1, 3))]

    third = -(-groups // 3)
    outs, far_other, *outs_given = kernel_call(
        turn_parts,
        [turned, ((rows, width), BF16)]
        + [((min(third, groups - k), block, rows), BF16) for k in range(0, groups, third)],
        [place, part, flip(other_middle, "sample")],
        far_hidden,
        scratch=[pltpu.VMEM((groups, block, rows), BF16)],
    )
    points = traded(
        point_products,
        2 * width,
        [outs, hidden, other_hidden, far_hidden, far_other]
        + [flip(piece, "sample") for piece in outs_given],
        scratch=[pltpu.VMEM((groups, block, rows), BF16)],
    )
    (middle_grad,) = kernel_call(
        middle_grads, [((rows, width), BF16)], [place, grad_kept, grad_got, slope], points[0]
    )
    moved = lax.ppermute(middle_grad, "seq", pairs)
    small = ((block, width), F32), ((block, width), BF16)
    point_kept, point_give = kernel_call(
        point_sum,
        [((2, block, width), F32), ((2, block, width), BF16)],
        [place, *points],
        middle_grad,
    )
    (own,) = kernel_call(
        act_part,
        [((rows, channels), BF16)],
        [place, middle_grad, moved, taps, part, slope_feat],
        point_kept,
    )
    steps = traded(
        tap_products,
        2 * width,
        [
            acts, flip(acts_given, "sample"), middle_grad, flip(middle_grad, "sample"), moved,
            flip(moved, "sample"),
        ],
        own,
    )
    point_kept, point_give = kernel_call(
        point_half, small, [place, point_kept, flip(point_give, "head")], steps[0]
    )
    point_got = flip(point_give, "seq", n_seq // 2)
    kept, give = kernel_call(
        taps_sum,
        [((block, 2 * width), F32), ((block, 2 * width), BF16)],
        [place, *steps],
        point_got,
    )
    dilated_grad, point_grad, input_grad = kernel_call(
        finish,
        [((3, block, width), F32), ((block, width), F32), ((rows, channels), BF16)],
        [
            place, own, flip(own, "head"), point_kept, point_got, kept,
            flip(give, "seq", n_seq // 2),
        ],
    )
    dilated_grad = jnp.transpose(dilated_grad, (1, 0, 2))
    return (input_grad.reshape(samples, positions, channels), dilated_grad, point_grad)


def solution(mesh):
    placed = (
        P("sample", "seq", None),
        P(None, None, "head"),
        P(None, "head"),
        P("sample", "head"),
        P("sample", "seq", "head"),
    )
    return jax.shard_map(
        body,
        mesh=mesh,
        in_specs=placed,
        out_specs=(
            P("sample", "seq", None),
            P(("seq", "sample"), None, "head"),
            P(("seq", "sample"), "head"),
        ),
        check_vma=False,
    )
```

```python
import jax
import jax.numpy as jnp
from jax import lax
from jax.experimental import pallas as pl
from jax.experimental.pallas import tpu as pltpu
from jax.sharding import PartitionSpec as P

DILATION_STEP = 1024
BF16 = jnp.bfloat16
F32 = jnp.float32
VMEM = 24 * 2**20
LITTLE = pl.CostEstimate(flops=1, bytes_accessed=1, transcendentals=0)


def gelu_value(value):
    inner = 0.7978845608 * (value + 0.044715 * value * value * value)
    return 0.5 * value * (1.0 + jnp.tanh(inner))


def gelu_slope(value):
    inner = 0.7978845608 * (value + 0.044715 * value * value * value)
    tangent = jnp.tanh(inner)
    return 0.5 * (1.0 + tangent) + 0.5 * value * (1.0 - tangent * tangent) * 0.7978845608 * (
        1.0 + 3.0 * 0.044715 * value * value
    )


def dot(left, right, contract):
    return lax.dot_general(left, right, (contract, ((), ())), preferred_element_type=F32)


def flip(value, axis, step=1):
    count = lax.axis_size(axis)
    return lax.ppermute(value, axis, [(i, i ^ step) for i in range(count)])


def own_first(value, axis_at, bit):
    return (
        lax.dynamic_index_in_dim(value, bit, axis_at, keepdims=False),
        lax.dynamic_index_in_dim(value, 1 - bit, axis_at, keepdims=False),
    )


def in_order(own, other, bit, axis):
    first = jnp.where(bit == 0, own, other)
    second = jnp.where(bit == 0, other, own)
    return jnp.concatenate([first, second], axis=axis)


def bits_of(count):
    return count.bit_length() - 1


def general(features, dilated_weight, point_weight, track_weight, track_cotangent):
    samples, positions, channels = features.shape
    rows = samples * positions
    half = rows // 2
    width = dilated_weight.shape[2]
    n_seq, n_sample = lax.axis_size("seq"), lax.axis_size("sample")
    seq, head, sample = lax.axis_index("seq"), lax.axis_index("head"), lax.axis_index("sample")
    dist = DILATION_STEP // positions
    one_sided = n_seq == 2 * dist
    low = seq < dist
    taps = jnp.transpose(dilated_weight, (1, 0, 2))

    if one_sided:
        outer_weights = [lax.dynamic_index_in_dim(taps, jnp.where(low, 0, 2), 0, keepdims=False)]
        pairs = [(i, (i + dist) % n_seq) for i in range(n_seq)]
        forward, backward = [pairs], [pairs]
    else:
        outer_weights = [taps[0], taps[2]]
        up = [(i, i + dist) for i in range(n_seq - dist)]
        down = [(i + dist, i) for i in range(n_seq - dist)]
        forward, backward = [up, down], [down, up]
    count = len(outer_weights)

    whole_track = lax.all_gather(track_weight, "sample", axis=0, tiled=True)
    piece = channels // n_sample
    own_piece = lax.dynamic_slice_in_dim(point_weight, sample * piece, piece, 0)
    other_point = lax.all_gather(flip(own_piece, "head"), "sample", axis=0, tiled=True)

    feat = features.reshape(rows, channels)
    feat_wide = feat.astype(F32)
    activated = gelu_value(feat_wide).astype(BF16)
    sent = [dot(activated, weight, ((1,), (0,))).astype(BF16) for weight in outer_weights]
    arrived = [lax.ppermute(term, "seq", pairs) for term, pairs in zip(sent, forward)]
    middle = dot(activated, taps[1], ((1,), (0,)))
    for term in arrived:
        middle = middle + term.astype(F32)
    middle_b = middle.astype(BF16)
    other_middle = flip(middle_b, "head")
    hidden = gelu_value(middle).astype(BF16)
    other_hidden = gelu_value(other_middle.astype(F32)).astype(BF16)
    block_out = (
        feat_wide
        + dot(hidden, point_weight, ((1,), (1,)))
        + dot(other_hidden, other_point, ((1,), (1,)))
    ).astype(BF16)

    def rows_of(value, which):
        return lax.dynamic_slice_in_dim(value, which * half, half, 0)

    cotangent = track_cotangent.reshape(rows, whole_track.shape[1])

    def track_part(which):
        scores = dot(rows_of(block_out, which), whole_track, ((1,), (0,)))
        grad = (rows_of(cotangent, which).astype(F32) * jax.nn.sigmoid(scores)).astype(BF16)
        return dot(grad, whole_track, ((1,), (1,)))

    theirs = flip(track_part(1 - head).astype(BF16), "head")
    out_grad = track_part(head) + theirs.astype(F32)
    out_grad_b = out_grad.astype(BF16)
    other_out_grad = flip(out_grad_b, "head")

    grad_own = (
        dot(out_grad_b, point_weight, ((1,), (0,))) * gelu_slope(rows_of(middle, head))
    ).astype(BF16)
    grad_other = (
        dot(out_grad_b, other_point, ((1,), (0,)))
        * gelu_slope(rows_of(other_middle, head).astype(F32))
    ).astype(BF16)
    middle_grad = in_order(grad_own, flip(grad_other, "head"), head, 0)
    moved = []
    for pairs in backward:
        straight = lax.ppermute(grad_own, "seq", pairs)
        crossed = lax.ppermute(
            grad_other,
            ("seq", "head"),
            [(2 * i + k, 2 * j + 1 - k) for i, j in pairs for k in range(2)],
        )
        moved.append(in_order(straight, crossed, head, 0))

    act_part = dot(middle_grad, taps[1], ((1,), (1,)))
    for field, weight in zip(moved, outer_weights):
        act_part = act_part + dot(field, weight, ((1,), (1,)))
    act_theirs = flip(rows_of(act_part, 1 - head).astype(BF16), "head")
    act_grad = rows_of(act_part, head) + act_theirs.astype(F32)
    input_half = (out_grad + act_grad * gelu_slope(rows_of(feat_wide, head))).astype(BF16)
    input_grad = in_order(input_half, flip(input_half, "head"), head, 0)

    seq_bits = bits_of(n_seq)
    block = channels // (n_seq * n_sample)
    shape = (2,) * seq_bits + (n_sample, block)

    def halve(value, left, bit, keep_last=False):
        at = left.index(bit)
        if bit < 0:
            mine, give = own_first(value, at, sample)
            got = flip(give.astype(BF16), "sample")
        else:
            mine, give = own_first(value, at, (seq >> bit) & 1)
            got = flip(give.astype(BF16), "seq", 1 << bit)
        rest = [b for b in left if b != bit]
        return (mine, got, rest) if keep_last else (mine.astype(F32) + got.astype(F32), rest)

    def reduced(value, order, apart=False):
        left = list(range(seq_bits - 1, -1, -1)) + [-1]
        value = value.reshape(shape + value.shape[1:])
        for bit in order[:-1]:
            value, left = halve(value, left, bit)
            value = value.astype(BF16)
        mine, got, _ = halve(value, left, order[-1], True)
        if apart:
            return mine.astype(F32), got.astype(F32)
        return mine.astype(F32) + got.astype(F32)

    order_a = [-1] + list(range(seq_bits))
    order_b = [-1] + list(range(1, seq_bits - 1)) + [0, seq_bits - 1]
    whole_out_grad = in_order(out_grad_b, other_out_grad, head, 0)
    point_grad = reduced(dot(whole_out_grad, hidden, ((0,), (0,))), order_a)
    mid_tap = reduced(dot(activated, middle_grad, ((0,), (0,))), order_b)
    if one_sided:
        mine, got = reduced(dot(activated, moved[0], ((0,), (0,))), order_a, True)
        outer = [jnp.where(low, mine, got), jnp.where(low, got, mine)]
    else:
        outer = [reduced(dot(activated, field, ((0,), (0,))), order_a) for field in moved]
    dilated_grad = jnp.transpose(jnp.stack([outer[0], mid_tap, outer[1]]), (1, 0, 2))
    return (input_grad.reshape(samples, positions, channels), dilated_grad, point_grad)


def wide(ref):
    return ref[...].astype(F32)


def kernel_call(kernel, outs, ins, after=None, scratch=(), spaces={}):
    place, arrays = ins[0], list(ins[1:])
    in_specs = [pl.BlockSpec(memory_space=pltpu.SMEM)]
    in_specs += [
        pl.BlockSpec(memory_space=spaces.get(k + 1, pltpu.VMEM)) for k in range(len(arrays))
    ]
    number = len(arrays) + 1
    if after is not None:
        arrays.append(after)
        in_specs.append(pl.BlockSpec(memory_space=pl.ANY))

    def run(*refs):
        given = refs[:number]
        kernel(*given, *refs[len(in_specs):])

    return pl.pallas_call(
        run,
        out_shape=[jax.ShapeDtypeStruct(s, d) for s, d in outs],
        in_specs=in_specs,
        out_specs=[pl.BlockSpec(memory_space=pltpu.VMEM)] * len(outs),
        scratch_shapes=list(scratch),
        compiler_params=pltpu.CompilerParams(vmem_limit_bytes=VMEM),
        cost_estimate=LITTLE,
        name=kernel.__name__,
    )(place, *arrays)


def in_hbm(value):
    return pltpu.with_memory_space_constraint(value, pltpu.HBM)


NN = ((1,), (0,))
NT = ((1,), (1,))
HEAD, SAMPLE, TOP, MID, LOWEST = 1, 2, 3, 4, 5


def outer_term(place, feat, taps, acted, term, rows, weight, sems):
    steps = sems.shape[1]
    depth = rows.shape[1] // steps
    parts = [pl.ds(k * depth, depth) for k in range(steps)]
    feats = [
        pltpu.make_async_copy(feat.at[:, part], rows.at[:, part], sems.at[0, k])
        for k, part in enumerate(parts)
    ]
    weights = [
        pltpu.make_async_copy(taps.at[place[0], part], weight.at[part], sems.at[1, k])
        for k, part in enumerate(parts)
    ]
    for pair in zip(feats, weights):
        for copy in pair:
            copy.start()
    total = None
    for copy, coming, part in zip(feats, weights, parts):
        copy.wait()
        act = gelu_value(rows[:, part].astype(F32)).astype(BF16)
        acted[:, part] = act
        coming.wait()
        value = dot(act, weight[part, :], NN)
        total = value if total is None else total + value
    term[...] = total.astype(BF16)


def piece_of(place, point, piece, sem):
    number = piece.shape[0]
    own = pl.ds(pl.multiple_of(place[SAMPLE] * number, number), number)
    copy = pltpu.make_async_copy(point.at[own], piece, sem)
    copy.start()
    copy.wait()


def middle_term(place, acted, weight, middle, kept, given):
    act = acted[...]
    middle[...] = dot(act, weight[1], NN)
    part_channels(place, act.T, kept, given)


def part_channels(place, turned, kept, given):
    groups, block, rows = kept.shape
    split = turned.reshape(groups, 2, block, rows)
    first = place[SAMPLE] == 0
    kept[...] = jnp.where(first, split[:, 0], split[:, 1])
    given[...] = jnp.where(first, split[:, 1], split[:, 0])


def add_terms(place, middle, arrived, total, sent):
    value = middle[...] + wide(arrived)
    total[...] = value
    sent[...] = value.astype(BF16)


def own_hidden(place, middle, feat, point, hidden, block, slope):
    value = middle[...]
    hid = gelu_value(value).astype(BF16)
    hidden[...] = hid
    block[...] = wide(feat) + dot(hid, point[...], NT)
    slope[...] = gelu_slope(value)


def feature_slope(place, feat, slope):
    slope[...] = gelu_slope(wide(feat))


def tracks(place, block, other_middle, near, far, cotangent, point, *rest):
    *pieces, part, other_hidden, grad_kept, grad_given, block_b, grads, points = rest
    sample = place[SAMPLE]
    piece = block_b.shape[2]
    width = other_middle.shape[1]
    ahead = 0
    for other in pieces:
        number = other.shape[0]
        which, row = (sample, ahead) if ahead < piece else (1 - sample, ahead - piece)
        points[which, row : row + number, width:] = other[...]
        ahead += number
    hid = gelu_value(wide(other_middle)).astype(BF16)
    other_hidden[...] = hid
    for which in range(2):
        columns = slice(which * piece, (which + 1) * piece)
        points[which, :, :width] = point[columns, :]
        value = block[:, columns] + dot(hid, points[which, :, width:], NT)
        block_b[which] = value.astype(BF16)
    number = near.shape[1]
    tile = width if number % width == 0 else number
    for start in range(0, number, tile):
        columns = slice(start, start + tile)
        scores = dot(block_b[sample], near[:, columns], NN)
        scores += dot(block_b[1 - sample], far[:, columns], NN)
        grads[:, columns] = (wide(cotangent.at[:, columns]) * jax.nn.sigmoid(scores)).astype(BF16)
    both = 0.0
    for which, weight in ((sample, near), (1 - sample, far)):
        columns = pl.ds(pl.multiple_of(which * piece, piece), piece)
        value = dot(grads[...], weight[...], NT).astype(BF16)
        part[:, columns] = value
        both += dot(value, points[which], NN)
    grad_kept[...] = both[:, :width]
    grad_given[...] = both[:, width:].astype(BF16)


def turn_parts(place, part, far_middle, kept, far_hidden, *rest):
    *pieces, given = rest
    far_hidden[...] = gelu_value(wide(far_middle)).astype(BF16)
    part_channels(place, part[...].T, kept, given)
    first = 0
    for piece in pieces:
        piece[...] = given[first : first + piece.shape[0]]
        first += piece.shape[0]


def middle_grads(place, kept, got, slope, middle_grad):
    middle_grad[...] = ((kept[...] + wide(got)) * slope[...]).astype(BF16)


def joined(pieces, whole):
    first = 0
    for piece in pieces:
        whole[first : first + piece.shape[0]] = piece[...]
        first += piece.shape[0]


def each_chip(place, keep, along, across, both, values):
    mid, lowest = place[MID], place[LOWEST]
    for i, j, out in (
        (1 - mid, 1 - lowest, both),
        (1 - mid, lowest, along),
        (mid, 1 - lowest, across),
        (mid, lowest, keep),
    ):

        def left(ref):
            groups, at = ref.shape[0], 2 * i + j
            return jnp.concatenate([ref[at], ref[groups // 2 + at]], axis=0)

        for k, value in enumerate(values(left)):
            width = value.shape[1]
            shape = (2, out.shape[1], width)
            out[:, :, k * width : (k + 1) * width] = value.astype(out.dtype).reshape(shape)


def point_products(
    place, outs, hidden, other_hidden, far_hidden, far_other, *rest
):
    *pieces, keep, along, across, both, other_outs = rest
    joined(pieces, other_outs)

    def values(left):
        own, other = left(outs), left(other_outs)
        return (
            dot(own, hidden[...], NN) + dot(other, far_hidden[...], NN),
            dot(own, other_hidden[...], NN) + dot(other, far_other[...], NN),
        )

    each_chip(place, keep, along, across, both, values)


def tap_products(
    place, acts, other_acts, middle_grad, other_middle_grad, moved, other_moved,
    keep, along, across, both,
):
    def values(left):
        own, other = left(acts), left(other_acts)
        return (
            dot(own, middle_grad[...], NN) + dot(other, other_middle_grad[...], NN),
            dot(own, moved[...], NN) + dot(other, other_moved[...], NN),
        )

    each_chip(place, keep, along, across, both, values)


def act_part(first):
    def act_rows(place, middle_grad, moved, weight, part, slope, give):
        rows = slice(first, first + give.shape[0])
        value = dot(middle_grad[rows, :], weight[1], NT)
        value += dot(moved[rows, :], weight[place[0]], NT)
        give[...] = (part[rows, :].astype(F32) + value * slope[rows, :]).astype(BF16)

    return act_rows


def over_chips(at, kept, *arrived):
    total = kept[at]
    for part in arrived:
        total += part[at].astype(F32)
    return total


def point_sum(place, kept, along, across, both, keep, give):
    width = keep.shape[2]
    for at in range(2):
        total = over_chips(at, kept, along, across, both)
        keep[at] = total[:, :width]
        give[at] = total[:, width:].astype(BF16)


def last_sum(place, point_kept, point_got, *refs):
    *parts, keep, give = refs
    top = place[TOP]
    width = parts[0].shape[2]
    for columns, terms in (
        (slice(0, width), parts),
        (slice(width, None), (point_kept, point_got)),
    ):
        keep[:, columns] = over_chips(top, *terms)
        give[:, columns] = over_chips(1 - top, *terms).astype(BF16)


def finish(place, one, one_got, two, two_got, kept, got, dilated, point, result):
    width = point.shape[1]
    dilated[1] = kept[:, :width] + got[:, :width].astype(F32)
    dilated[place[0]] = kept[:, width : 2 * width]
    dilated[2 - place[0]] = got[:, width : 2 * width].astype(F32)
    point[...] = kept[:, 2 * width :] + got[:, 2 * width :].astype(F32)
    first = 0
    for own, theirs in ((one, one_got), (two, two_got)):
        rows = slice(first, first + own.shape[0])
        result[rows, :] = (wide(own) + wide(theirs)).astype(BF16)
        first += own.shape[0]


def body(features, dilated_weight, point_weight, track_weight, track_cotangent):
    samples, positions, channels = features.shape
    n_seq, n_sample, n_head = (lax.axis_size(a) for a in ("seq", "sample", "head"))
    dist = DILATION_STEP // positions
    if not (n_seq == 2 * dist and bits_of(n_seq) == 3 and n_sample == 2 and n_head == 2 and samples == 1):
        return general(features, dilated_weight, point_weight, track_weight, track_cotangent)
    rows = positions
    half = rows // 2
    width = dilated_weight.shape[2]
    tracks_here = track_weight.shape[1]
    piece = channels // n_sample
    block = channels // (n_seq * n_sample)
    seq, head, sample = lax.axis_index("seq"), lax.axis_index("head"), lax.axis_index("sample")
    place = jnp.stack(
        [jnp.where(seq < dist, 0, 2), head, sample, (seq >> 2) & 1, (seq >> 1) & 1, seq & 1]
    ).astype(jnp.int32)
    taps = jnp.transpose(dilated_weight, (1, 0, 2))
    feat = features.reshape(rows, channels)
    cotangent = track_cotangent.reshape(rows, tracks_here)
    pairs = [(i, (i + dist) % n_seq) for i in range(n_seq)]

    (own_piece,) = kernel_call(
        piece_of,
        [((piece, width), BF16)],
        [place, in_hbm(point_weight)],
        scratch=[pltpu.SemaphoreType.DMA],
        spaces={1: pltpu.HBM},
    )
    near = flip(own_piece, "head")
    cut = piece // 3
    points = [near] + [flip(near[k : k + cut], "sample") for k in range(0, piece, cut)]
    far_track = flip(track_weight, "sample")
    acted, term = kernel_call(
        outer_term,
        [((rows, channels), BF16), ((rows, width), BF16)],
        [place, in_hbm(feat), in_hbm(taps)],
        own_piece,
        scratch=[
            pltpu.VMEM((rows, channels), BF16),
            pltpu.VMEM((channels, width), BF16),
            pltpu.SemaphoreType.DMA((2, 3)),
        ],
        spaces={1: pltpu.HBM, 2: pltpu.HBM},
    )
    arrived = lax.ppermute(term, "seq", pairs)
    groups = n_seq

    turned = ((groups, block, rows), BF16)
    middle, acts, acts_given = kernel_call(
        middle_term,
        [((rows, width), F32), turned, turned],
        [place, acted, taps],
    )
    middle, middle_b = kernel_call(
        add_terms, [((rows, width), F32), ((rows, width), BF16)], [place, middle, arrived], acts
    )
    other_middle = flip(middle_b, "head")
    hidden, block_part, slope = kernel_call(
        own_hidden,
        [((rows, width), BF16), ((rows, channels), F32), ((rows, width), F32)],
        [place, middle, feat, point_weight],
    )
    (slope_feat,) = kernel_call(
        feature_slope, [((rows, channels), F32)], [place, feat], block_part
    )
    part, other_hidden, grad_kept, grad_given = kernel_call(
        tracks,
        [((rows, channels), BF16), ((rows, width), BF16), ((rows, width), F32), ((rows, width), BF16)],
        [
            place, block_part, other_middle, track_weight, far_track, cotangent, point_weight,
            *points,
        ],
        slope_feat,
        scratch=[
            pltpu.VMEM((n_sample, rows, piece), BF16),
            pltpu.VMEM((rows, tracks_here), BF16),
            pltpu.VMEM((n_sample, piece, n_head * width), BF16),
        ],
    )
    grad_got = flip(grad_given, "head")
    far_hidden, other_acts = flip(hidden, "sample"), flip(acts_given, "sample")

    def traded(kernel, columns, ins, after=None, scratch=()):
        shape = (2, block, columns)
        keep, *gives = kernel_call(
            kernel, [(shape, F32)] + [(shape, BF16)] * 3, [place, *ins], after, scratch
        )
        return keep, *[flip(value, "seq", step) for value, step in zip(gives, (2, 1, 3))]

    third = -(-groups // 3)
    outs, far_other, *outs_given = kernel_call(
        turn_parts,
        [turned, ((rows, width), BF16)]
        + [((min(third, groups - k), block, rows), BF16) for k in range(0, groups, third)],
        [place, part, flip(other_middle, "sample")],
        far_hidden,
        scratch=[pltpu.VMEM((groups, block, rows), BF16)],
    )
    points = traded(
        point_products,
        2 * width,
        [outs, hidden, other_hidden, far_hidden, far_other]
        + [flip(piece, "sample") for piece in outs_given],
        other_acts,
        scratch=[pltpu.VMEM((groups, block, rows), BF16)],
    )
    (middle_grad,) = kernel_call(
        middle_grads, [((rows, width), BF16)], [place, grad_kept, grad_got, slope], points[0]
    )
    moved = lax.ppermute(middle_grad, "seq", pairs)
    ins = [place, middle_grad, moved, taps, part, slope_feat]
    other_grad = flip(middle_grad, "sample")
    most = rows * 3 // 4
    (one,) = kernel_call(act_part(0), [((most, channels), BF16)], ins, other_grad)
    point_kept, point_give = kernel_call(
        point_sum,
        [((2, block, width), F32), ((2, block, width), BF16)],
        [place, *points],
        one,
    )
    steps = traded(
        tap_products,
        2 * width,
        [acts, other_acts, middle_grad, other_grad, moved, flip(moved, "sample")],
        point_kept,
    )
    (two,) = kernel_call(act_part(most), [((rows - most, channels), BF16)], ins, steps[0])
    kept, give = kernel_call(
        last_sum,
        [((block, 3 * width), F32), ((block, 3 * width), BF16)],
        [place, point_kept, flip(point_give, "head"), *steps],
        two,
    )
    dilated_grad, point_grad, input_grad = kernel_call(
        finish,
        [((3, block, width), F32), ((block, width), F32), ((rows, channels), BF16)],
        [
            place, one, flip(one, "head"), two, flip(two, "head"), kept,
            flip(give, "seq", n_seq // 2),
        ],
    )
    dilated_grad = jnp.transpose(dilated_grad, (1, 0, 2))
    return (input_grad.reshape(samples, positions, channels), dilated_grad, point_grad)


def solution(mesh):
    placed = (
        P("sample", "seq", None),
        P(None, None, "head"),
        P(None, "head"),
        P("sample", "head"),
        P("sample", "seq", "head"),
    )
    return jax.shard_map(
        body,
        mesh=mesh,
        in_specs=placed,
        out_specs=(
            P("sample", "seq", None),
            P(("seq", "sample"), None, "head"),
            P(("seq", "sample"), "head"),
        ),
        check_vma=False,
    )
```

```python
import jax
import jax.numpy as jnp
from jax import lax
from jax.experimental import pallas as pl
from jax.experimental.pallas import tpu as pltpu
from jax.sharding import PartitionSpec as P

DILATION_STEP = 1024
BF16 = jnp.bfloat16
F32 = jnp.float32
VMEM = 24 * 2**20
LITTLE = pl.CostEstimate(flops=1, bytes_accessed=1, transcendentals=0)


def gelu_value(value):
    inner = 0.7978845608 * (value + 0.044715 * value * value * value)
    return 0.5 * value * (1.0 + jnp.tanh(inner))


def gelu_slope(value):
    inner = 0.7978845608 * (value + 0.044715 * value * value * value)
    tangent = jnp.tanh(inner)
    return 0.5 * (1.0 + tangent) + 0.5 * value * (1.0 - tangent * tangent) * 0.7978845608 * (
        1.0 + 3.0 * 0.044715 * value * value
    )


def dot(left, right, contract):
    return lax.dot_general(left, right, (contract, ((), ())), preferred_element_type=F32)


def flip(value, axis, step=1):
    count = lax.axis_size(axis)
    return lax.ppermute(value, axis, [(i, i ^ step) for i in range(count)])


def own_first(value, axis_at, bit):
    return (
        lax.dynamic_index_in_dim(value, bit, axis_at, keepdims=False),
        lax.dynamic_index_in_dim(value, 1 - bit, axis_at, keepdims=False),
    )


def in_order(own, other, bit, axis):
    first = jnp.where(bit == 0, own, other)
    second = jnp.where(bit == 0, other, own)
    return jnp.concatenate([first, second], axis=axis)


def bits_of(count):
    return count.bit_length() - 1


def general(features, dilated_weight, point_weight, track_weight, track_cotangent):
    samples, positions, channels = features.shape
    rows = samples * positions
    half = rows // 2
    width = dilated_weight.shape[2]
    n_seq, n_sample = lax.axis_size("seq"), lax.axis_size("sample")
    seq, head, sample = lax.axis_index("seq"), lax.axis_index("head"), lax.axis_index("sample")
    dist = DILATION_STEP // positions
    one_sided = n_seq == 2 * dist
    low = seq < dist
    taps = jnp.transpose(dilated_weight, (1, 0, 2))

    if one_sided:
        outer_weights = [lax.dynamic_index_in_dim(taps, jnp.where(low, 0, 2), 0, keepdims=False)]
        pairs = [(i, (i + dist) % n_seq) for i in range(n_seq)]
        forward, backward = [pairs], [pairs]
    else:
        outer_weights = [taps[0], taps[2]]
        up = [(i, i + dist) for i in range(n_seq - dist)]
        down = [(i + dist, i) for i in range(n_seq - dist)]
        forward, backward = [up, down], [down, up]
    count = len(outer_weights)

    whole_track = lax.all_gather(track_weight, "sample", axis=0, tiled=True)
    piece = channels // n_sample
    own_piece = lax.dynamic_slice_in_dim(point_weight, sample * piece, piece, 0)
    other_point = lax.all_gather(flip(own_piece, "head"), "sample", axis=0, tiled=True)

    feat = features.reshape(rows, channels)
    feat_wide = feat.astype(F32)
    activated = gelu_value(feat_wide).astype(BF16)
    sent = [dot(activated, weight, ((1,), (0,))).astype(BF16) for weight in outer_weights]
    arrived = [lax.ppermute(term, "seq", pairs) for term, pairs in zip(sent, forward)]
    middle = dot(activated, taps[1], ((1,), (0,)))
    for term in arrived:
        middle = middle + term.astype(F32)
    middle_b = middle.astype(BF16)
    other_middle = flip(middle_b, "head")
    hidden = gelu_value(middle).astype(BF16)
    other_hidden = gelu_value(other_middle.astype(F32)).astype(BF16)
    block_out = (
        feat_wide
        + dot(hidden, point_weight, ((1,), (1,)))
        + dot(other_hidden, other_point, ((1,), (1,)))
    ).astype(BF16)

    def rows_of(value, which):
        return lax.dynamic_slice_in_dim(value, which * half, half, 0)

    cotangent = track_cotangent.reshape(rows, whole_track.shape[1])

    def track_part(which):
        scores = dot(rows_of(block_out, which), whole_track, ((1,), (0,)))
        grad = (rows_of(cotangent, which).astype(F32) * jax.nn.sigmoid(scores)).astype(BF16)
        return dot(grad, whole_track, ((1,), (1,)))

    theirs = flip(track_part(1 - head).astype(BF16), "head")
    out_grad = track_part(head) + theirs.astype(F32)
    out_grad_b = out_grad.astype(BF16)
    other_out_grad = flip(out_grad_b, "head")

    grad_own = (
        dot(out_grad_b, point_weight, ((1,), (0,))) * gelu_slope(rows_of(middle, head))
    ).astype(BF16)
    grad_other = (
        dot(out_grad_b, other_point, ((1,), (0,)))
        * gelu_slope(rows_of(other_middle, head).astype(F32))
    ).astype(BF16)
    middle_grad = in_order(grad_own, flip(grad_other, "head"), head, 0)
    moved = []
    for pairs in backward:
        straight = lax.ppermute(grad_own, "seq", pairs)
        crossed = lax.ppermute(
            grad_other,
            ("seq", "head"),
            [(2 * i + k, 2 * j + 1 - k) for i, j in pairs for k in range(2)],
        )
        moved.append(in_order(straight, crossed, head, 0))

    act_part = dot(middle_grad, taps[1], ((1,), (1,)))
    for field, weight in zip(moved, outer_weights):
        act_part = act_part + dot(field, weight, ((1,), (1,)))
    act_theirs = flip(rows_of(act_part, 1 - head).astype(BF16), "head")
    act_grad = rows_of(act_part, head) + act_theirs.astype(F32)
    input_half = (out_grad + act_grad * gelu_slope(rows_of(feat_wide, head))).astype(BF16)
    input_grad = in_order(input_half, flip(input_half, "head"), head, 0)

    seq_bits = bits_of(n_seq)
    block = channels // (n_seq * n_sample)
    shape = (2,) * seq_bits + (n_sample, block)

    def halve(value, left, bit, keep_last=False):
        at = left.index(bit)
        if bit < 0:
            mine, give = own_first(value, at, sample)
            got = flip(give.astype(BF16), "sample")
        else:
            mine, give = own_first(value, at, (seq >> bit) & 1)
            got = flip(give.astype(BF16), "seq", 1 << bit)
        rest = [b for b in left if b != bit]
        return (mine, got, rest) if keep_last else (mine.astype(F32) + got.astype(F32), rest)

    def reduced(value, order, apart=False):
        left = list(range(seq_bits - 1, -1, -1)) + [-1]
        value = value.reshape(shape + value.shape[1:])
        for bit in order[:-1]:
            value, left = halve(value, left, bit)
            value = value.astype(BF16)
        mine, got, _ = halve(value, left, order[-1], True)
        if apart:
            return mine.astype(F32), got.astype(F32)
        return mine.astype(F32) + got.astype(F32)

    order_a = [-1] + list(range(seq_bits))
    order_b = [-1] + list(range(1, seq_bits - 1)) + [0, seq_bits - 1]
    whole_out_grad = in_order(out_grad_b, other_out_grad, head, 0)
    point_grad = reduced(dot(whole_out_grad, hidden, ((0,), (0,))), order_a)
    mid_tap = reduced(dot(activated, middle_grad, ((0,), (0,))), order_b)
    if one_sided:
        mine, got = reduced(dot(activated, moved[0], ((0,), (0,))), order_a, True)
        outer = [jnp.where(low, mine, got), jnp.where(low, got, mine)]
    else:
        outer = [reduced(dot(activated, field, ((0,), (0,))), order_a) for field in moved]
    dilated_grad = jnp.transpose(jnp.stack([outer[0], mid_tap, outer[1]]), (1, 0, 2))
    return (input_grad.reshape(samples, positions, channels), dilated_grad, point_grad)


def wide(ref):
    return ref[...].astype(F32)


def kernel_call(kernel, outs, ins, after=None, scratch=(), spaces={}):
    place, arrays = ins[0], list(ins[1:])
    in_specs = [pl.BlockSpec(memory_space=pltpu.SMEM)]
    in_specs += [
        pl.BlockSpec(memory_space=spaces.get(k + 1, pltpu.VMEM)) for k in range(len(arrays))
    ]
    number = len(arrays) + 1
    if after is not None:
        arrays.append(after)
        in_specs.append(pl.BlockSpec(memory_space=pl.ANY))

    def run(*refs):
        given = refs[:number]
        kernel(*given, *refs[len(in_specs):])

    return pl.pallas_call(
        run,
        out_shape=[jax.ShapeDtypeStruct(s, d) for s, d in outs],
        in_specs=in_specs,
        out_specs=[pl.BlockSpec(memory_space=pltpu.VMEM)] * len(outs),
        scratch_shapes=list(scratch),
        compiler_params=pltpu.CompilerParams(vmem_limit_bytes=VMEM),
        cost_estimate=LITTLE,
        name=kernel.__name__,
    )(place, *arrays)


def in_hbm(value):
    return pltpu.with_memory_space_constraint(value, pltpu.HBM)


NN = ((1,), (0,))
NT = ((1,), (1,))
HEAD, SAMPLE, TOP, MID, LOWEST = 1, 2, 3, 4, 5


def outer_term(place, feat, taps, acted, term, rows, weight, sems):
    steps = sems.shape[1]
    depth = rows.shape[1] // steps
    parts = [pl.ds(k * depth, depth) for k in range(steps)]
    feats = [
        pltpu.make_async_copy(feat.at[:, part], rows.at[:, part], sems.at[0, k])
        for k, part in enumerate(parts)
    ]
    weights = [
        pltpu.make_async_copy(taps.at[place[0], part], weight.at[part], sems.at[1, k])
        for k, part in enumerate(parts)
    ]
    for pair in zip(feats, weights):
        for copy in pair:
            copy.start()
    total = None
    for copy, coming, part in zip(feats, weights, parts):
        copy.wait()
        act = gelu_value(rows[:, part].astype(F32)).astype(BF16)
        acted[:, part] = act
        coming.wait()
        value = dot(act, weight[part, :], NN)
        total = value if total is None else total + value
    term[...] = total.astype(BF16)


def piece_of(place, point, piece, sem):
    number = piece.shape[0]
    own = pl.ds(pl.multiple_of(place[SAMPLE] * number, number), number)
    copy = pltpu.make_async_copy(point.at[own], piece, sem)
    copy.start()
    copy.wait()


def middle_term(place, acted, weight, middle, kept, given):
    act = acted[...]
    middle[...] = dot(act, weight[1], NN)
    part_channels(place, act.T, kept, given)


def part_channels(place, turned, kept, given):
    groups, block, rows = kept.shape
    split = turned.reshape(groups, 2, block, rows)
    first = place[SAMPLE] == 0
    kept[...] = jnp.where(first, split[:, 0], split[:, 1])
    given[...] = jnp.where(first, split[:, 1], split[:, 0])


def add_terms(place, middle, arrived, total, sent):
    value = middle[...] + wide(arrived)
    total[...] = value
    sent[...] = value.astype(BF16)


def own_hidden(place, middle, feat, point, near, hidden, block, slope, slope_feat, *pieces):
    value = middle[...]
    hid = gelu_value(value).astype(BF16)
    hidden[...] = hid
    rows = wide(feat)
    block[...] = rows + dot(hid, point[...], NT)
    slope[...] = gelu_slope(value)
    slope_feat[...] = gelu_slope(rows)
    first = 0
    for piece in pieces:
        piece[...] = near[first : first + piece.shape[0]]
        first += piece.shape[0]


def tracks(place, block, other_middle, near, far, cotangent, point, *rest):
    *pieces, part, other_hidden, grad_kept, grad_given, block_b, grads, points = rest
    sample = place[SAMPLE]
    piece = block_b.shape[2]
    width = other_middle.shape[1]
    ahead = 0
    for other in pieces:
        number = other.shape[0]
        which, row = (sample, ahead) if ahead < piece else (1 - sample, ahead - piece)
        points[which, row : row + number, width:] = other[...]
        ahead += number
    hid = gelu_value(wide(other_middle)).astype(BF16)
    other_hidden[...] = hid
    for which in range(2):
        columns = slice(which * piece, (which + 1) * piece)
        points[which, :, :width] = point[columns, :]
        value = block[:, columns] + dot(hid, points[which, :, width:], NT)
        block_b[which] = value.astype(BF16)
    number = near.shape[1]
    tile = width if number % width == 0 else number
    for start in range(0, number, tile):
        columns = slice(start, start + tile)
        scores = dot(block_b[sample], near[:, columns], NN)
        scores += dot(block_b[1 - sample], far[:, columns], NN)
        grads[:, columns] = (wide(cotangent.at[:, columns]) * jax.nn.sigmoid(scores)).astype(BF16)
    both = 0.0
    for which, weight in ((sample, near), (1 - sample, far)):
        columns = pl.ds(pl.multiple_of(which * piece, piece), piece)
        value = dot(grads[...], weight[...], NT).astype(BF16)
        part[:, columns] = value
        both += dot(value, points[which], NN)
    grad_kept[...] = both[:, :width]
    grad_given[...] = both[:, width:].astype(BF16)


def turn_parts(place, part, far_middle, kept, far_hidden, *rest):
    *pieces, given = rest
    far_hidden[...] = gelu_value(wide(far_middle)).astype(BF16)
    part_channels(place, part[...].T, kept, given)
    first = 0
    for piece in pieces:
        piece[...] = given[first : first + piece.shape[0]]
        first += piece.shape[0]


def middle_grads(place, kept, got, slope, middle_grad):
    middle_grad[...] = ((kept[...] + wide(got)) * slope[...]).astype(BF16)


def joined(pieces, whole):
    first = 0
    for piece in pieces:
        whole[first : first + piece.shape[0]] = piece[...]
        first += piece.shape[0]


def each_chip(place, keep, along, across, both, values):
    mid, lowest = place[MID], place[LOWEST]
    for i, j, out in (
        (1 - mid, 1 - lowest, both),
        (1 - mid, lowest, along),
        (mid, 1 - lowest, across),
        (mid, lowest, keep),
    ):

        def left(ref):
            groups, at = ref.shape[0], 2 * i + j
            return jnp.concatenate([ref[at], ref[groups // 2 + at]], axis=0)

        for k, value in enumerate(values(left)):
            width = value.shape[1]
            shape = (2, out.shape[1], width)
            out[:, :, k * width : (k + 1) * width] = value.astype(out.dtype).reshape(shape)


def early_products(
    place, acts, other_acts, middle_grad, outs, hidden, other_hidden, far_hidden, far_other, *rest
):
    *pieces, first, second, keep, along, across, both, other_outs, other_grad = rest
    joined(pieces, other_outs)
    joined((first, second), other_grad)

    def values(left):
        own, other = left(outs), left(other_outs)
        return (
            dot(left(acts), middle_grad[...], NN) + dot(left(other_acts), other_grad[...], NN),
            dot(own, hidden[...], NN) + dot(other, far_hidden[...], NN),
            dot(own, other_hidden[...], NN) + dot(other, far_other[...], NN),
        )

    each_chip(place, keep, along, across, both, values)


def outer_products(place, acts, other_acts, moved, other_moved, keep, along, across, both):
    def values(left):
        return (dot(left(acts), moved[...], NN) + dot(left(other_acts), other_moved[...], NN),)

    each_chip(place, keep, along, across, both, values)


def act_part(place, middle_grad, moved, weight, part, slope, give):
    value = dot(middle_grad[...], weight[1], NT) + dot(moved[...], weight[place[0]], NT)
    give[...] = (wide(part) + value * slope[...]).astype(BF16)


def over_chips(at, kept, *arrived):
    total = kept[at]
    for part in arrived:
        total += part[at].astype(F32)
    return total


def early_sum(place, kept, along, across, both, keep, give):
    two = keep.shape[2]
    for at in range(2):
        total = over_chips(at, kept, along, across, both)
        keep[at] = total[:, :two]
        give[at] = total[:, two:].astype(BF16)


def last_sum(place, early, point_got, *refs):
    *parts, keep, give = refs
    top = place[TOP]
    width = parts[0].shape[2]
    for at, out in ((top, keep), (1 - top, give)):
        rest = early[at]
        point = rest[:, width:] + point_got[at].astype(F32)
        out[:, :width] = over_chips(at, *parts).astype(out.dtype)
        out[:, width : 2 * width] = rest[:, :width].astype(out.dtype)
        out[:, 2 * width :] = point.astype(out.dtype)


def finish(place, own, theirs, kept, got, dilated, point, result):
    width = point.shape[1]
    dilated[place[0]] = kept[:, :width]
    dilated[2 - place[0]] = got[:, :width].astype(F32)
    dilated[1] = kept[:, width : 2 * width] + got[:, width : 2 * width].astype(F32)
    point[...] = kept[:, 2 * width :] + got[:, 2 * width :].astype(F32)
    result[...] = (wide(own) + wide(theirs)).astype(BF16)


def body(features, dilated_weight, point_weight, track_weight, track_cotangent):
    samples, positions, channels = features.shape
    n_seq, n_sample, n_head = (lax.axis_size(a) for a in ("seq", "sample", "head"))
    dist = DILATION_STEP // positions
    if not (n_seq == 2 * dist and bits_of(n_seq) == 3 and n_sample == 2 and n_head == 2 and samples == 1):
        return general(features, dilated_weight, point_weight, track_weight, track_cotangent)
    rows = positions
    half = rows // 2
    width = dilated_weight.shape[2]
    tracks_here = track_weight.shape[1]
    piece = channels // n_sample
    block = channels // (n_seq * n_sample)
    seq, head, sample = lax.axis_index("seq"), lax.axis_index("head"), lax.axis_index("sample")
    place = jnp.stack(
        [jnp.where(seq < dist, 0, 2), head, sample, (seq >> 2) & 1, (seq >> 1) & 1, seq & 1]
    ).astype(jnp.int32)
    taps = jnp.transpose(dilated_weight, (1, 0, 2))
    feat = features.reshape(rows, channels)
    cotangent = track_cotangent.reshape(rows, tracks_here)
    pairs = [(i, (i + dist) % n_seq) for i in range(n_seq)]

    (own_piece,) = kernel_call(
        piece_of,
        [((piece, width), BF16)],
        [place, in_hbm(point_weight)],
        scratch=[pltpu.SemaphoreType.DMA],
        spaces={1: pltpu.HBM},
    )
    near = flip(own_piece, "head")
    far_track = flip(track_weight, "sample")
    acted, term = kernel_call(
        outer_term,
        [((rows, channels), BF16), ((rows, width), BF16)],
        [place, in_hbm(feat), in_hbm(taps)],
        own_piece,
        scratch=[
            pltpu.VMEM((rows, channels), BF16),
            pltpu.VMEM((channels, width), BF16),
            pltpu.SemaphoreType.DMA((2, 3)),
        ],
        spaces={1: pltpu.HBM, 2: pltpu.HBM},
    )
    arrived = lax.ppermute(term, "seq", pairs)
    groups = n_seq

    turned = ((groups, block, rows), BF16)
    middle, acts, acts_given = kernel_call(
        middle_term,
        [((rows, width), F32), turned, turned],
        [place, acted, taps],
    )
    middle, middle_b = kernel_call(
        add_terms, [((rows, width), F32), ((rows, width), BF16)], [place, middle, arrived], acts
    )
    other_middle = flip(middle_b, "head")
    cut = piece // 3
    hidden, block_part, slope, slope_feat, *pieces = kernel_call(
        own_hidden,
        [
            ((rows, width), BF16),
            ((rows, channels), F32),
            ((rows, width), F32),
            ((rows, channels), F32),
        ]
        + [((cut, width), BF16)] * (piece // cut),
        [place, middle, feat, point_weight, near],
    )
    points = [near] + [flip(part, "sample") for part in pieces]
    part, other_hidden, grad_kept, grad_given = kernel_call(
        tracks,
        [((rows, channels), BF16), ((rows, width), BF16), ((rows, width), F32), ((rows, width), BF16)],
        [
            place, block_part, other_middle, track_weight, far_track, cotangent, point_weight,
            *points,
        ],
        scratch=[
            pltpu.VMEM((n_sample, rows, piece), BF16),
            pltpu.VMEM((rows, tracks_here), BF16),
            pltpu.VMEM((n_sample, piece, n_head * width), BF16),
        ],
    )
    grad_got = flip(grad_given, "head")
    far_hidden, other_acts = flip(hidden, "sample"), flip(acts_given, "sample")

    def traded(kernel, columns, ins, after=None, scratch=()):
        shape = (2, block, columns)
        keep, *gives = kernel_call(
            kernel, [(shape, F32)] + [(shape, BF16)] * 3, [place, *ins], after, scratch
        )
        return keep, *[flip(value, "seq", step) for value, step in zip(gives, (2, 1, 3))]

    third = -(-groups // 3)
    outs, far_other, *outs_given = kernel_call(
        turn_parts,
        [turned, ((rows, width), BF16)]
        + [((min(third, groups - k), block, rows), BF16) for k in range(0, groups, third)],
        [place, part, flip(other_middle, "sample")],
        far_hidden,
        scratch=[pltpu.VMEM((groups, block, rows), BF16)],
    )
    (middle_grad,) = kernel_call(
        middle_grads, [((rows, width), BF16)], [place, grad_kept, grad_got, slope], outs
    )
    moved = lax.ppermute(middle_grad, "seq", pairs)
    early = traded(
        early_products,
        3 * width,
        [acts, other_acts, middle_grad, outs, hidden, other_hidden, far_hidden, far_other]
        + [flip(piece, "sample") for piece in outs_given]
        + [flip(middle_grad[k : k + half], "sample") for k in (0, half)],
        scratch=[pltpu.VMEM((groups, block, rows), BF16), pltpu.VMEM((rows, width), BF16)],
    )
    (own,) = kernel_call(
        act_part,
        [((rows, channels), BF16)],
        [place, middle_grad, moved, taps, part, slope_feat],
        early[0],
    )
    kept, point_give = kernel_call(
        early_sum,
        [((2, block, 2 * width), F32), ((2, block, width), BF16)],
        [place, *early],
        own,
    )
    steps = traded(
        outer_products, width, [acts, other_acts, moved, flip(moved, "sample")], kept
    )
    kept, give = kernel_call(
        last_sum,
        [((block, 3 * width), F32), ((block, 3 * width), BF16)],
        [place, kept, flip(point_give, "head"), *steps],
    )
    dilated_grad, point_grad, input_grad = kernel_call(
        finish,
        [((3, block, width), F32), ((block, width), F32), ((rows, channels), BF16)],
        [place, own, flip(own, "head"), kept, flip(give, "seq", n_seq // 2)],
    )
    dilated_grad = jnp.transpose(dilated_grad, (1, 0, 2))
    return (input_grad.reshape(samples, positions, channels), dilated_grad, point_grad)


def solution(mesh):
    placed = (
        P("sample", "seq", None),
        P(None, None, "head"),
        P(None, "head"),
        P("sample", "head"),
        P("sample", "seq", "head"),
    )
    return jax.shard_map(
        body,
        mesh=mesh,
        in_specs=placed,
        out_specs=(
            P("sample", "seq", None),
            P(("seq", "sample"), None, "head"),
            P(("seq", "sample"), "head"),
        ),
        check_vma=False,
    )
```

```python
import jax
import jax.numpy as jnp
from jax import lax
from jax.experimental import pallas as pl
from jax.experimental.pallas import tpu as pltpu
from jax.sharding import PartitionSpec as P

DILATION_STEP = 1024
BF16 = jnp.bfloat16
F32 = jnp.float32
VMEM = 24 * 2**20
LITTLE = pl.CostEstimate(flops=1, bytes_accessed=1, transcendentals=0)


def gelu_value(value):
    inner = 0.7978845608 * (value + 0.044715 * value * value * value)
    return 0.5 * value * (1.0 + jnp.tanh(inner))


def gelu_slope(value):
    inner = 0.7978845608 * (value + 0.044715 * value * value * value)
    tangent = jnp.tanh(inner)
    return 0.5 * (1.0 + tangent) + 0.5 * value * (1.0 - tangent * tangent) * 0.7978845608 * (
        1.0 + 3.0 * 0.044715 * value * value
    )


def dot(left, right, contract):
    return lax.dot_general(left, right, (contract, ((), ())), preferred_element_type=F32)


def flip(value, axis, step=1):
    count = lax.axis_size(axis)
    return lax.ppermute(value, axis, [(i, i ^ step) for i in range(count)])


def own_first(value, axis_at, bit):
    return (
        lax.dynamic_index_in_dim(value, bit, axis_at, keepdims=False),
        lax.dynamic_index_in_dim(value, 1 - bit, axis_at, keepdims=False),
    )


def in_order(own, other, bit, axis):
    first = jnp.where(bit == 0, own, other)
    second = jnp.where(bit == 0, other, own)
    return jnp.concatenate([first, second], axis=axis)


def bits_of(count):
    return count.bit_length() - 1


def general(features, dilated_weight, point_weight, track_weight, track_cotangent):
    samples, positions, channels = features.shape
    rows = samples * positions
    half = rows // 2
    width = dilated_weight.shape[2]
    n_seq, n_sample = lax.axis_size("seq"), lax.axis_size("sample")
    seq, head, sample = lax.axis_index("seq"), lax.axis_index("head"), lax.axis_index("sample")
    dist = DILATION_STEP // positions
    one_sided = n_seq == 2 * dist
    low = seq < dist
    taps = jnp.transpose(dilated_weight, (1, 0, 2))

    if one_sided:
        outer_weights = [lax.dynamic_index_in_dim(taps, jnp.where(low, 0, 2), 0, keepdims=False)]
        pairs = [(i, (i + dist) % n_seq) for i in range(n_seq)]
        forward, backward = [pairs], [pairs]
    else:
        outer_weights = [taps[0], taps[2]]
        up = [(i, i + dist) for i in range(n_seq - dist)]
        down = [(i + dist, i) for i in range(n_seq - dist)]
        forward, backward = [up, down], [down, up]
    count = len(outer_weights)

    whole_track = lax.all_gather(track_weight, "sample", axis=0, tiled=True)
    piece = channels // n_sample
    own_piece = lax.dynamic_slice_in_dim(point_weight, sample * piece, piece, 0)
    other_point = lax.all_gather(flip(own_piece, "head"), "sample", axis=0, tiled=True)

    feat = features.reshape(rows, channels)
    feat_wide = feat.astype(F32)
    activated = gelu_value(feat_wide).astype(BF16)
    sent = [dot(activated, weight, ((1,), (0,))).astype(BF16) for weight in outer_weights]
    arrived = [lax.ppermute(term, "seq", pairs) for term, pairs in zip(sent, forward)]
    middle = dot(activated, taps[1], ((1,), (0,)))
    for term in arrived:
        middle = middle + term.astype(F32)
    middle_b = middle.astype(BF16)
    other_middle = flip(middle_b, "head")
    hidden = gelu_value(middle).astype(BF16)
    other_hidden = gelu_value(other_middle.astype(F32)).astype(BF16)
    block_out = (
        feat_wide
        + dot(hidden, point_weight, ((1,), (1,)))
        + dot(other_hidden, other_point, ((1,), (1,)))
    ).astype(BF16)

    def rows_of(value, which):
        return lax.dynamic_slice_in_dim(value, which * half, half, 0)

    cotangent = track_cotangent.reshape(rows, whole_track.shape[1])

    def track_part(which):
        scores = dot(rows_of(block_out, which), whole_track, ((1,), (0,)))
        grad = (rows_of(cotangent, which).astype(F32) * jax.nn.sigmoid(scores)).astype(BF16)
        return dot(grad, whole_track, ((1,), (1,)))

    theirs = flip(track_part(1 - head).astype(BF16), "head")
    out_grad = track_part(head) + theirs.astype(F32)
    out_grad_b = out_grad.astype(BF16)
    other_out_grad = flip(out_grad_b, "head")

    grad_own = (
        dot(out_grad_b, point_weight, ((1,), (0,))) * gelu_slope(rows_of(middle, head))
    ).astype(BF16)
    grad_other = (
        dot(out_grad_b, other_point, ((1,), (0,)))
        * gelu_slope(rows_of(other_middle, head).astype(F32))
    ).astype(BF16)
    middle_grad = in_order(grad_own, flip(grad_other, "head"), head, 0)
    moved = []
    for pairs in backward:
        straight = lax.ppermute(grad_own, "seq", pairs)
        crossed = lax.ppermute(
            grad_other,
            ("seq", "head"),
            [(2 * i + k, 2 * j + 1 - k) for i, j in pairs for k in range(2)],
        )
        moved.append(in_order(straight, crossed, head, 0))

    act_part = dot(middle_grad, taps[1], ((1,), (1,)))
    for field, weight in zip(moved, outer_weights):
        act_part = act_part + dot(field, weight, ((1,), (1,)))
    act_theirs = flip(rows_of(act_part, 1 - head).astype(BF16), "head")
    act_grad = rows_of(act_part, head) + act_theirs.astype(F32)
    input_half = (out_grad + act_grad * gelu_slope(rows_of(feat_wide, head))).astype(BF16)
    input_grad = in_order(input_half, flip(input_half, "head"), head, 0)

    seq_bits = bits_of(n_seq)
    block = channels // (n_seq * n_sample)
    shape = (2,) * seq_bits + (n_sample, block)

    def halve(value, left, bit, keep_last=False):
        at = left.index(bit)
        if bit < 0:
            mine, give = own_first(value, at, sample)
            got = flip(give.astype(BF16), "sample")
        else:
            mine, give = own_first(value, at, (seq >> bit) & 1)
            got = flip(give.astype(BF16), "seq", 1 << bit)
        rest = [b for b in left if b != bit]
        return (mine, got, rest) if keep_last else (mine.astype(F32) + got.astype(F32), rest)

    def reduced(value, order, apart=False):
        left = list(range(seq_bits - 1, -1, -1)) + [-1]
        value = value.reshape(shape + value.shape[1:])
        for bit in order[:-1]:
            value, left = halve(value, left, bit)
            value = value.astype(BF16)
        mine, got, _ = halve(value, left, order[-1], True)
        if apart:
            return mine.astype(F32), got.astype(F32)
        return mine.astype(F32) + got.astype(F32)

    order_a = [-1] + list(range(seq_bits))
    order_b = [-1] + list(range(1, seq_bits - 1)) + [0, seq_bits - 1]
    whole_out_grad = in_order(out_grad_b, other_out_grad, head, 0)
    point_grad = reduced(dot(whole_out_grad, hidden, ((0,), (0,))), order_a)
    mid_tap = reduced(dot(activated, middle_grad, ((0,), (0,))), order_b)
    if one_sided:
        mine, got = reduced(dot(activated, moved[0], ((0,), (0,))), order_a, True)
        outer = [jnp.where(low, mine, got), jnp.where(low, got, mine)]
    else:
        outer = [reduced(dot(activated, field, ((0,), (0,))), order_a) for field in moved]
    dilated_grad = jnp.transpose(jnp.stack([outer[0], mid_tap, outer[1]]), (1, 0, 2))
    return (input_grad.reshape(samples, positions, channels), dilated_grad, point_grad)


def wide(ref):
    return ref[...].astype(F32)


def kernel_call(kernel, outs, ins, after=(), scratch=(), spaces={}):
    place, arrays = ins[0], list(ins[1:])
    in_specs = [pl.BlockSpec(memory_space=pltpu.SMEM)]
    in_specs += [
        pl.BlockSpec(memory_space=spaces.get(k + 1, pltpu.VMEM)) for k in range(len(arrays))
    ]
    number = len(arrays) + 1
    for value in after:
        arrays.append(value)
        in_specs.append(pl.BlockSpec(memory_space=pl.ANY))

    def run(*refs):
        given = refs[:number]
        kernel(*given, *refs[len(in_specs):])

    return pl.pallas_call(
        run,
        out_shape=[jax.ShapeDtypeStruct(s, d) for s, d in outs],
        in_specs=in_specs,
        out_specs=[pl.BlockSpec(memory_space=pltpu.VMEM)] * len(outs),
        scratch_shapes=list(scratch),
        compiler_params=pltpu.CompilerParams(vmem_limit_bytes=VMEM),
        cost_estimate=LITTLE,
        name=kernel.__name__,
    )(place, *arrays)


def in_hbm(value):
    return pltpu.with_memory_space_constraint(value, pltpu.HBM)


NN = ((1,), (0,))
NT = ((1,), (1,))
HEAD, SAMPLE, TOP, MID, LOWEST = 1, 2, 3, 4, 5


def outer_term(place, feat, taps, acted, term, rows, weight, sems):
    steps = sems.shape[1]
    depth = rows.shape[1] // steps
    parts = [pl.ds(k * depth, depth) for k in range(steps)]
    feats = [
        pltpu.make_async_copy(feat.at[:, part], rows.at[:, part], sems.at[0, k])
        for k, part in enumerate(parts)
    ]
    weights = [
        pltpu.make_async_copy(taps.at[place[0], part], weight.at[part], sems.at[1, k])
        for k, part in enumerate(parts)
    ]
    for pair in zip(feats, weights):
        for copy in pair:
            copy.start()
    total = None
    for copy, coming, part in zip(feats, weights, parts):
        copy.wait()
        act = gelu_value(rows[:, part].astype(F32)).astype(BF16)
        acted[:, part] = act
        coming.wait()
        value = dot(act, weight[part, :], NN)
        total = value if total is None else total + value
    term[...] = total.astype(BF16)


def piece_of(place, point, piece, sem):
    number = piece.shape[0]
    own = pl.ds(pl.multiple_of(place[SAMPLE] * number, number), number)
    copy = pltpu.make_async_copy(point.at[own], piece, sem)
    copy.start()
    copy.wait()


def middle_term(place, acted, weight, middle, kept, given):
    act = acted[...]
    middle[...] = dot(act, weight[1], NN)
    part_channels(place, act.T, kept, given)


def part_channels(place, turned, kept, given):
    groups, block, rows = kept.shape
    split = turned.reshape(groups, 2, block, rows)
    first = place[SAMPLE] == 0
    kept[...] = jnp.where(first, split[:, 0], split[:, 1])
    given[...] = jnp.where(first, split[:, 1], split[:, 0])


def add_terms(place, middle, arrived, total, sent):
    value = middle[...] + wide(arrived)
    total[...] = value
    sent[...] = value.astype(BF16)


def own_hidden(place, middle, feat, point, near, hidden, block, slope, slope_feat, *pieces):
    value = middle[...]
    hid = gelu_value(value).astype(BF16)
    hidden[...] = hid
    rows = wide(feat)
    block[...] = rows + dot(hid, point[...], NT)
    slope[...] = gelu_slope(value)
    slope_feat[...] = gelu_slope(rows)
    first = 0
    for piece in pieces:
        piece[...] = near[first : first + piece.shape[0]]
        first += piece.shape[0]


def tracks(place, block, other_middle, near, far, cotangent, point, *rest):
    *pieces, part, other_hidden, grad_kept, grad_given, block_b, grads, points = rest
    sample = place[SAMPLE]
    piece = block_b.shape[2]
    width = other_middle.shape[1]
    ahead = 0
    for other in pieces:
        number = other.shape[0]
        which, row = (sample, ahead) if ahead < piece else (1 - sample, ahead - piece)
        points[which, row : row + number, width:] = other[...]
        ahead += number
    hid = gelu_value(wide(other_middle)).astype(BF16)
    other_hidden[...] = hid
    for which in range(2):
        columns = slice(which * piece, (which + 1) * piece)
        points[which, :, :width] = point[columns, :]
        value = block[:, columns] + dot(hid, points[which, :, width:], NT)
        block_b[which] = value.astype(BF16)
    number = near.shape[1]
    tile = width if number % width == 0 else number
    for start in range(0, number, tile):
        columns = slice(start, start + tile)
        scores = dot(block_b[sample], near[:, columns], NN)
        scores += dot(block_b[1 - sample], far[:, columns], NN)
        grads[:, columns] = (wide(cotangent.at[:, columns]) * jax.nn.sigmoid(scores)).astype(BF16)
    both = 0.0
    for which, weight in ((sample, near), (1 - sample, far)):
        columns = pl.ds(pl.multiple_of(which * piece, piece), piece)
        value = dot(grads[...], weight[...], NT).astype(BF16)
        part[:, columns] = value
        both += dot(value, points[which], NN)
    grad_kept[...] = both[:, :width]
    grad_given[...] = both[:, width:].astype(BF16)


def turn_parts(place, part, far_middle, kept, far_hidden, *rest):
    *pieces, given = rest
    far_hidden[...] = gelu_value(wide(far_middle)).astype(BF16)
    part_channels(place, part[...].T, kept, given)
    first = 0
    for piece in pieces:
        piece[...] = given[first : first + piece.shape[0]]
        first += piece.shape[0]


def other_points(place, outs, other_hidden, far_other, *rest):
    *pieces, share, other_outs = rest
    joined(pieces, other_outs)
    groups, block, rows = outs.shape
    value = dot(outs[...].reshape(groups * block, rows), other_hidden[...], NN)
    value += dot(other_outs[...].reshape(groups * block, rows), far_other[...], NN)
    share[...] = value.astype(BF16).reshape(share.shape)


def middle_grads(place, kept, got, slope, share, middle_grad, give):
    middle_grad[...] = ((kept[...] + wide(got)) * slope[...]).astype(BF16)
    give[...] = share[...]


def joined(pieces, whole):
    first = 0
    for piece in pieces:
        whole[first : first + piece.shape[0]] = piece[...]
        first += piece.shape[0]


def each_chip(place, keep, along, across, both, values):
    mid, lowest = place[MID], place[LOWEST]
    for i, j, out in (
        (1 - mid, 1 - lowest, both),
        (1 - mid, lowest, along),
        (mid, 1 - lowest, across),
        (mid, lowest, keep),
    ):

        def left(ref):
            groups, at = ref.shape[0], 2 * i + j
            return jnp.concatenate([ref[at], ref[groups // 2 + at]], axis=0)

        for k, value in enumerate(values(left)):
            width = value.shape[1]
            shape = (2, out.shape[1], width)
            out[:, :, k * width : (k + 1) * width] = value.astype(out.dtype).reshape(shape)


def middle_products(place, acts, other_acts, field, *rest):
    *pieces, keep, along, across, both, other = rest
    joined(pieces, other)

    def values(left):
        return (dot(left(acts), field[...], NN) + dot(left(other_acts), other[...], NN),)

    each_chip(place, keep, along, across, both, values)


def late_products(
    place, acts, other_acts, moved, other_moved, outs, other_outs, hidden, far_hidden, shares,
    keep, along, across, both,
):
    def values(left):
        point = dot(left(outs), hidden[...], NN) + dot(left(other_outs), far_hidden[...], NN)
        return (
            dot(left(acts), moved[...], NN) + dot(left(other_acts), other_moved[...], NN),
            point + left(shares).astype(F32),
        )

    each_chip(place, keep, along, across, both, values)


def act_part(first):
    def act_rows(place, middle_grad, moved, weight, part, slope, give):
        rows = slice(first, first + give.shape[0])
        value = dot(middle_grad[rows, :], weight[1], NT)
        value += dot(moved[rows, :], weight[place[0]], NT)
        give[...] = (part[rows, :].astype(F32) + value * slope[rows, :]).astype(BF16)

    return act_rows


def over_chips(at, kept, *arrived):
    total = kept[at]
    for part in arrived:
        total += part[at].astype(F32)
    return total


def chips_sum(place, *refs):
    *parts, keep, give = refs
    top = place[TOP]
    keep[...] = over_chips(top, *parts)
    give[...] = over_chips(1 - top, *parts).astype(BF16)


def finish(
    place, one, one_got, two, two_got, mid_kept, mid_got, kept, got, dilated, point, result
):
    width = point.shape[1]
    dilated[1] = mid_kept[...] + wide(mid_got)
    dilated[place[0]] = kept[:, :width]
    dilated[2 - place[0]] = got[:, :width].astype(F32)
    point[...] = kept[:, width:] + got[:, width:].astype(F32)
    first = 0
    for own, theirs in ((one, one_got), (two, two_got)):
        rows = slice(first, first + own.shape[0])
        result[rows, :] = (wide(own) + wide(theirs)).astype(BF16)
        first += own.shape[0]


def body(features, dilated_weight, point_weight, track_weight, track_cotangent):
    samples, positions, channels = features.shape
    n_seq, n_sample, n_head = (lax.axis_size(a) for a in ("seq", "sample", "head"))
    dist = DILATION_STEP // positions
    if not (n_seq == 2 * dist and bits_of(n_seq) == 3 and n_sample == 2 and n_head == 2 and samples == 1):
        return general(features, dilated_weight, point_weight, track_weight, track_cotangent)
    rows = positions
    half = rows // 2
    width = dilated_weight.shape[2]
    tracks_here = track_weight.shape[1]
    piece = channels // n_sample
    block = channels // (n_seq * n_sample)
    seq, head, sample = lax.axis_index("seq"), lax.axis_index("head"), lax.axis_index("sample")
    place = jnp.stack(
        [jnp.where(seq < dist, 0, 2), head, sample, (seq >> 2) & 1, (seq >> 1) & 1, seq & 1]
    ).astype(jnp.int32)
    taps = jnp.transpose(dilated_weight, (1, 0, 2))
    feat = features.reshape(rows, channels)
    cotangent = track_cotangent.reshape(rows, tracks_here)
    pairs = [(i, (i + dist) % n_seq) for i in range(n_seq)]

    (own_piece,) = kernel_call(
        piece_of,
        [((piece, width), BF16)],
        [place, in_hbm(point_weight)],
        scratch=[pltpu.SemaphoreType.DMA],
        spaces={1: pltpu.HBM},
    )
    near = flip(own_piece, "head")
    far_track = flip(track_weight, "sample")
    acted, term = kernel_call(
        outer_term,
        [((rows, channels), BF16), ((rows, width), BF16)],
        [place, in_hbm(feat), in_hbm(taps)],
        [own_piece],
        scratch=[
            pltpu.VMEM((rows, channels), BF16),
            pltpu.VMEM((channels, width), BF16),
            pltpu.SemaphoreType.DMA((2, 3)),
        ],
        spaces={1: pltpu.HBM, 2: pltpu.HBM},
    )
    arrived = lax.ppermute(term, "seq", pairs)
    groups = n_seq

    turned = ((groups, block, rows), BF16)
    middle, acts, acts_given = kernel_call(
        middle_term,
        [((rows, width), F32), turned, turned],
        [place, acted, taps],
    )
    middle, middle_b = kernel_call(
        add_terms, [((rows, width), F32), ((rows, width), BF16)], [place, middle, arrived], [acts]
    )
    other_middle = flip(middle_b, "head")
    cut = piece // 3
    other_acts = flip(acts_given, "sample")
    hidden, block_part, slope, slope_feat, *pieces = kernel_call(
        own_hidden,
        [
            ((rows, width), BF16),
            ((rows, channels), F32),
            ((rows, width), F32),
            ((rows, channels), F32),
        ]
        + [((cut, width), BF16)] * (piece // cut),
        [place, middle, feat, point_weight, near],
    )
    points = [near] + [flip(part, "sample") for part in pieces]
    part, other_hidden, grad_kept, grad_given = kernel_call(
        tracks,
        [((rows, channels), BF16), ((rows, width), BF16), ((rows, width), F32), ((rows, width), BF16)],
        [
            place, block_part, other_middle, track_weight, far_track, cotangent, point_weight,
            *points,
        ],
        scratch=[
            pltpu.VMEM((n_sample, rows, piece), BF16),
            pltpu.VMEM((rows, tracks_here), BF16),
            pltpu.VMEM((n_sample, piece, n_head * width), BF16),
        ],
    )
    grad_got = flip(grad_given, "head")
    far_hidden = flip(hidden, "sample")

    def traded(kernel, columns, ins, after=(), scratch=()):
        shape = (2, block, columns)
        keep, *gives = kernel_call(
            kernel, [(shape, F32)] + [(shape, BF16)] * 3, [place, *ins], after, scratch
        )
        return keep, *[flip(value, "seq", step) for value, step in zip(gives, (2, 1, 3))]

    third = -(-groups // 3)
    outs, far_other, *outs_given = kernel_call(
        turn_parts,
        [turned, ((rows, width), BF16)]
        + [((min(third, groups - k), block, rows), BF16) for k in range(0, groups, third)],
        [place, part, flip(other_middle, "sample")],
        [far_hidden],
        scratch=[pltpu.VMEM((groups, block, rows), BF16)],
    )
    shares = ((groups, block, width), BF16)
    share, other_outs = kernel_call(
        other_points,
        [shares, turned],
        [place, outs, other_hidden, far_other] + [flip(piece, "sample") for piece in outs_given],
    )
    middle_grad, share = kernel_call(
        middle_grads,
        [((rows, width), BF16), shares],
        [place, grad_kept, grad_got, slope, share],
    )
    moved = lax.ppermute(middle_grad, "seq", pairs)
    share_got = flip(share, "head")
    cuts = [0, rows * 3 // 8, rows * 3 // 4, rows]
    early = traded(
        middle_products,
        width,
        [acts, other_acts, middle_grad]
        + [flip(middle_grad[i:j], "sample") for i, j in zip(cuts[:-1], cuts[1:])],
        scratch=[pltpu.VMEM((rows, width), BF16)],
    )

    def halved(terms, columns, after):
        kept, give = kernel_call(
            chips_sum, [((block, columns), F32), ((block, columns), BF16)], [place, *terms], after
        )
        return kept, flip(give, "seq", n_seq // 2)

    mid_kept, mid_got = halved(early, width, [share_got])
    most = rows * 3 // 4
    ins = [place, middle_grad, moved, taps, part, slope_feat]
    (one,) = kernel_call(act_part(0), [((most, channels), BF16)], ins, [mid_kept])
    late = traded(
        late_products,
        2 * width,
        [
            acts, other_acts, moved, flip(moved, "sample"), outs, other_outs, hidden, far_hidden,
            share_got,
        ],
        [one],
    )
    (two,) = kernel_call(act_part(most), [((rows - most, channels), BF16)], ins, [late[0]])
    kept, got = halved(late, 2 * width, [two, mid_got])
    dilated_grad, point_grad, input_grad = kernel_call(
        finish,
        [((3, block, width), F32), ((block, width), F32), ((rows, channels), BF16)],
        [place, one, flip(one, "head"), two, flip(two, "head"), mid_kept, mid_got, kept, got],
    )
    dilated_grad = jnp.transpose(dilated_grad, (1, 0, 2))
    return (input_grad.reshape(samples, positions, channels), dilated_grad, point_grad)


def solution(mesh):
    placed = (
        P("sample", "seq", None),
        P(None, None, "head"),
        P(None, "head"),
        P("sample", "head"),
        P("sample", "seq", "head"),
    )
    return jax.shard_map(
        body,
        mesh=mesh,
        in_specs=placed,
        out_specs=(
            P("sample", "seq", None),
            P(("seq", "sample"), None, "head"),
            P(("seq", "sample"), "head"),
        ),
        check_vma=False,
    )
```

```python
import jax
import jax.numpy as jnp
from jax import lax
from jax.experimental import pallas as pl
from jax.experimental.pallas import tpu as pltpu
from jax.sharding import PartitionSpec as P

DILATION_STEP = 1024
BF16 = jnp.bfloat16
F32 = jnp.float32
VMEM = 24 * 2**20
LITTLE = pl.CostEstimate(flops=1, bytes_accessed=1, transcendentals=0)


def gelu_value(value):
    inner = 0.7978845608 * (value + 0.044715 * value * value * value)
    return 0.5 * value * (1.0 + jnp.tanh(inner))


def gelu_slope(value):
    inner = 0.7978845608 * (value + 0.044715 * value * value * value)
    tangent = jnp.tanh(inner)
    return 0.5 * (1.0 + tangent) + 0.5 * value * (1.0 - tangent * tangent) * 0.7978845608 * (
        1.0 + 3.0 * 0.044715 * value * value
    )


def dot(left, right, contract):
    return lax.dot_general(left, right, (contract, ((), ())), preferred_element_type=F32)


def flip(value, axis, step=1):
    count = lax.axis_size(axis)
    return lax.ppermute(value, axis, [(i, i ^ step) for i in range(count)])


def own_first(value, axis_at, bit):
    return (
        lax.dynamic_index_in_dim(value, bit, axis_at, keepdims=False),
        lax.dynamic_index_in_dim(value, 1 - bit, axis_at, keepdims=False),
    )


def in_order(own, other, bit, axis):
    first = jnp.where(bit == 0, own, other)
    second = jnp.where(bit == 0, other, own)
    return jnp.concatenate([first, second], axis=axis)


def bits_of(count):
    return count.bit_length() - 1


def general(features, dilated_weight, point_weight, track_weight, track_cotangent):
    samples, positions, channels = features.shape
    rows = samples * positions
    half = rows // 2
    width = dilated_weight.shape[2]
    n_seq, n_sample = lax.axis_size("seq"), lax.axis_size("sample")
    seq, head, sample = lax.axis_index("seq"), lax.axis_index("head"), lax.axis_index("sample")
    dist = DILATION_STEP // positions
    one_sided = n_seq == 2 * dist
    low = seq < dist
    taps = jnp.transpose(dilated_weight, (1, 0, 2))

    if one_sided:
        outer_weights = [lax.dynamic_index_in_dim(taps, jnp.where(low, 0, 2), 0, keepdims=False)]
        pairs = [(i, (i + dist) % n_seq) for i in range(n_seq)]
        forward, backward = [pairs], [pairs]
    else:
        outer_weights = [taps[0], taps[2]]
        up = [(i, i + dist) for i in range(n_seq - dist)]
        down = [(i + dist, i) for i in range(n_seq - dist)]
        forward, backward = [up, down], [down, up]
    count = len(outer_weights)

    whole_track = lax.all_gather(track_weight, "sample", axis=0, tiled=True)
    piece = channels // n_sample
    own_piece = lax.dynamic_slice_in_dim(point_weight, sample * piece, piece, 0)
    other_point = lax.all_gather(flip(own_piece, "head"), "sample", axis=0, tiled=True)

    feat = features.reshape(rows, channels)
    feat_wide = feat.astype(F32)
    activated = gelu_value(feat_wide).astype(BF16)
    sent = [dot(activated, weight, ((1,), (0,))).astype(BF16) for weight in outer_weights]
    arrived = [lax.ppermute(term, "seq", pairs) for term, pairs in zip(sent, forward)]
    middle = dot(activated, taps[1], ((1,), (0,)))
    for term in arrived:
        middle = middle + term.astype(F32)
    middle_b = middle.astype(BF16)
    other_middle = flip(middle_b, "head")
    hidden = gelu_value(middle).astype(BF16)
    other_hidden = gelu_value(other_middle.astype(F32)).astype(BF16)
    block_out = (
        feat_wide
        + dot(hidden, point_weight, ((1,), (1,)))
        + dot(other_hidden, other_point, ((1,), (1,)))
    ).astype(BF16)

    def rows_of(value, which):
        return lax.dynamic_slice_in_dim(value, which * half, half, 0)

    cotangent = track_cotangent.reshape(rows, whole_track.shape[1])

    def track_part(which):
        scores = dot(rows_of(block_out, which), whole_track, ((1,), (0,)))
        grad = (rows_of(cotangent, which).astype(F32) * jax.nn.sigmoid(scores)).astype(BF16)
        return dot(grad, whole_track, ((1,), (1,)))

    theirs = flip(track_part(1 - head).astype(BF16), "head")
    out_grad = track_part(head) + theirs.astype(F32)
    out_grad_b = out_grad.astype(BF16)
    other_out_grad = flip(out_grad_b, "head")

    grad_own = (
        dot(out_grad_b, point_weight, ((1,), (0,))) * gelu_slope(rows_of(middle, head))
    ).astype(BF16)
    grad_other = (
        dot(out_grad_b, other_point, ((1,), (0,)))
        * gelu_slope(rows_of(other_middle, head).astype(F32))
    ).astype(BF16)
    middle_grad = in_order(grad_own, flip(grad_other, "head"), head, 0)
    moved = []
    for pairs in backward:
        straight = lax.ppermute(grad_own, "seq", pairs)
        crossed = lax.ppermute(
            grad_other,
            ("seq", "head"),
            [(2 * i + k, 2 * j + 1 - k) for i, j in pairs for k in range(2)],
        )
        moved.append(in_order(straight, crossed, head, 0))

    act_part = dot(middle_grad, taps[1], ((1,), (1,)))
    for field, weight in zip(moved, outer_weights):
        act_part = act_part + dot(field, weight, ((1,), (1,)))
    act_theirs = flip(rows_of(act_part, 1 - head).astype(BF16), "head")
    act_grad = rows_of(act_part, head) + act_theirs.astype(F32)
    input_half = (out_grad + act_grad * gelu_slope(rows_of(feat_wide, head))).astype(BF16)
    input_grad = in_order(input_half, flip(input_half, "head"), head, 0)

    seq_bits = bits_of(n_seq)
    block = channels // (n_seq * n_sample)
    shape = (2,) * seq_bits + (n_sample, block)

    def halve(value, left, bit, keep_last=False):
        at = left.index(bit)
        if bit < 0:
            mine, give = own_first(value, at, sample)
            got = flip(give.astype(BF16), "sample")
        else:
            mine, give = own_first(value, at, (seq >> bit) & 1)
            got = flip(give.astype(BF16), "seq", 1 << bit)
        rest = [b for b in left if b != bit]
        return (mine, got, rest) if keep_last else (mine.astype(F32) + got.astype(F32), rest)

    def reduced(value, order, apart=False):
        left = list(range(seq_bits - 1, -1, -1)) + [-1]
        value = value.reshape(shape + value.shape[1:])
        for bit in order[:-1]:
            value, left = halve(value, left, bit)
            value = value.astype(BF16)
        mine, got, _ = halve(value, left, order[-1], True)
        if apart:
            return mine.astype(F32), got.astype(F32)
        return mine.astype(F32) + got.astype(F32)

    order_a = [-1] + list(range(seq_bits))
    order_b = [-1] + list(range(1, seq_bits - 1)) + [0, seq_bits - 1]
    whole_out_grad = in_order(out_grad_b, other_out_grad, head, 0)
    point_grad = reduced(dot(whole_out_grad, hidden, ((0,), (0,))), order_a)
    mid_tap = reduced(dot(activated, middle_grad, ((0,), (0,))), order_b)
    if one_sided:
        mine, got = reduced(dot(activated, moved[0], ((0,), (0,))), order_a, True)
        outer = [jnp.where(low, mine, got), jnp.where(low, got, mine)]
    else:
        outer = [reduced(dot(activated, field, ((0,), (0,))), order_a) for field in moved]
    dilated_grad = jnp.transpose(jnp.stack([outer[0], mid_tap, outer[1]]), (1, 0, 2))
    return (input_grad.reshape(samples, positions, channels), dilated_grad, point_grad)


def wide(ref):
    return ref[...].astype(F32)


def kernel_call(kernel, outs, ins, after=(), scratch=(), spaces={}):
    place, arrays = ins[0], list(ins[1:])
    in_specs = [pl.BlockSpec(memory_space=pltpu.SMEM)]
    in_specs += [
        pl.BlockSpec(memory_space=spaces.get(k + 1, pltpu.VMEM)) for k in range(len(arrays))
    ]
    number = len(arrays) + 1
    for value in after:
        arrays.append(value)
        in_specs.append(pl.BlockSpec(memory_space=pl.ANY))

    def run(*refs):
        given = refs[:number]
        kernel(*given, *refs[len(in_specs):])

    return pl.pallas_call(
        run,
        out_shape=[jax.ShapeDtypeStruct(s, d) for s, d in outs],
        in_specs=in_specs,
        out_specs=[pl.BlockSpec(memory_space=pltpu.VMEM)] * len(outs),
        scratch_shapes=list(scratch),
        compiler_params=pltpu.CompilerParams(vmem_limit_bytes=VMEM),
        cost_estimate=LITTLE,
        name=kernel.__name__,
    )(place, *arrays)


def in_hbm(value):
    return pltpu.with_memory_space_constraint(value, pltpu.HBM)


NN = ((1,), (0,))
NT = ((1,), (1,))
HEAD, SAMPLE, TOP, MID, LOWEST = 1, 2, 3, 4, 5


def outer_term(place, feat, taps, acted, term, rows, weight, sems):
    steps = sems.shape[1]
    depth = rows.shape[1] // steps
    parts = [pl.ds(k * depth, depth) for k in range(steps)]
    feats = [
        pltpu.make_async_copy(feat.at[:, part], rows.at[:, part], sems.at[0, k])
        for k, part in enumerate(parts)
    ]
    weights = [
        pltpu.make_async_copy(taps.at[place[0], part], weight.at[part], sems.at[1, k])
        for k, part in enumerate(parts)
    ]
    for pair in zip(feats, weights):
        for copy in pair:
            copy.start()
    total = None
    for copy, coming, part in zip(feats, weights, parts):
        copy.wait()
        act = gelu_value(rows[:, part].astype(F32)).astype(BF16)
        acted[:, part] = act
        coming.wait()
        value = dot(act, weight[part, :], NN)
        total = value if total is None else total + value
    term[...] = total.astype(BF16)


def piece_of(place, point, piece, sem):
    number = piece.shape[0]
    own = pl.ds(pl.multiple_of(place[SAMPLE] * number, number), number)
    copy = pltpu.make_async_copy(point.at[own], piece, sem)
    copy.start()
    copy.wait()


def middle_term(place, acted, weight, middle, kept, given):
    act = acted[...]
    middle[...] = dot(act, weight[1], NN)
    part_channels(place, act.T, kept, given)


def part_channels(place, turned, kept, given):
    groups, block, rows = kept.shape
    split = turned.reshape(groups, 2, block, rows)
    first = place[SAMPLE] == 0
    kept[...] = jnp.where(first, split[:, 0], split[:, 1])
    given[...] = jnp.where(first, split[:, 1], split[:, 0])


def add_terms(place, middle, arrived, total, sent):
    value = middle[...] + wide(arrived)
    total[...] = value
    sent[...] = value.astype(BF16)


def own_hidden(place, middle, feat, point, near, hidden, block, slope, slope_feat, *pieces):
    value = middle[...]
    hid = gelu_value(value).astype(BF16)
    hidden[...] = hid
    rows = wide(feat)
    block[...] = rows + dot(hid, point[...], NT)
    slope[...] = gelu_slope(value)
    slope_feat[...] = gelu_slope(rows)
    first = 0
    for piece in pieces:
        piece[...] = near[first : first + piece.shape[0]]
        first += piece.shape[0]


def tracks(place, block, other_middle, near, far, cotangent, point, *rest):
    *pieces, part, other_hidden, grad_kept, grad_given, block_b, grads, points = rest
    sample = place[SAMPLE]
    piece = block_b.shape[2]
    width = other_middle.shape[1]
    ahead = 0
    for other in pieces:
        number = other.shape[0]
        which, row = (sample, ahead) if ahead < piece else (1 - sample, ahead - piece)
        points[which, row : row + number, width:] = other[...]
        ahead += number
    hid = gelu_value(wide(other_middle)).astype(BF16)
    other_hidden[...] = hid
    for which in range(2):
        columns = slice(which * piece, (which + 1) * piece)
        points[which, :, :width] = point[columns, :]
        value = block[:, columns] + dot(hid, points[which, :, width:], NT)
        block_b[which] = value.astype(BF16)
    number = near.shape[1]
    tile = width if number % width == 0 else number
    for start in range(0, number, tile):
        columns = slice(start, start + tile)
        scores = dot(block_b[sample], near[:, columns], NN)
        scores += dot(block_b[1 - sample], far[:, columns], NN)
        grads[:, columns] = (wide(cotangent.at[:, columns]) * jax.nn.sigmoid(scores)).astype(BF16)
    both = 0.0
    for which, weight in ((sample, near), (1 - sample, far)):
        columns = pl.ds(pl.multiple_of(which * piece, piece), piece)
        value = dot(grads[...], weight[...], NT).astype(BF16)
        part[:, columns] = value
        both += dot(value, points[which], NN)
    grad_kept[...] = both[:, :width]
    grad_given[...] = both[:, width:].astype(BF16)


def turn_parts(place, part, far_middle, kept, far_hidden, *rest):
    *pieces, given = rest
    far_hidden[...] = gelu_value(wide(far_middle)).astype(BF16)
    part_channels(place, part[...].T, kept, given)
    first = 0
    for piece in pieces:
        piece[...] = given[first : first + piece.shape[0]]
        first += piece.shape[0]


def other_points(place, outs, other_hidden, far_other, *rest):
    *pieces, share, other_outs = rest
    joined(pieces, other_outs)
    groups, block, rows = outs.shape
    value = dot(outs[...].reshape(groups * block, rows), other_hidden[...], NN)
    value += dot(other_outs[...].reshape(groups * block, rows), far_other[...], NN)
    share[...] = value.astype(BF16).reshape(share.shape)


def middle_grads(place, kept, got, slope, share, middle_grad, give):
    middle_grad[...] = ((kept[...] + wide(got)) * slope[...]).astype(BF16)
    give[...] = share[...]


def joined(pieces, whole):
    first = 0
    for piece in pieces:
        whole[first : first + piece.shape[0]] = piece[...]
        first += piece.shape[0]


def each_chip(place, keep, along, across, both, values):
    mid, lowest = place[MID], place[LOWEST]
    for i, j, out in (
        (1 - mid, 1 - lowest, both),
        (1 - mid, lowest, along),
        (mid, 1 - lowest, across),
        (mid, lowest, keep),
    ):

        def left(ref):
            groups, at = ref.shape[0], 2 * i + j
            return jnp.concatenate([ref[at], ref[groups // 2 + at]], axis=0)

        for k, value in enumerate(values(left)):
            width = value.shape[1]
            shape = (2, out.shape[1], width)
            out[:, :, k * width : (k + 1) * width] = value.astype(out.dtype).reshape(shape)


def middle_products(place, acts, other_acts, field, *rest):
    *pieces, keep, across, along, both, other = rest
    joined(pieces, other)

    def values(left):
        return (dot(left(acts), field[...], NN) + dot(left(other_acts), other[...], NN),)

    each_chip(place, keep, along, across, both, values)


def late_products(
    place, acts, other_acts, moved, outs, other_outs, hidden, far_hidden, shares, first, second,
    keep, across, along, both, other_moved,
):
    joined((first, second), other_moved)

    def values(left):
        point = dot(left(outs), hidden[...], NN) + dot(left(other_outs), far_hidden[...], NN)
        return (
            dot(left(acts), moved[...], NN) + dot(left(other_acts), other_moved[...], NN),
            point + left(shares).astype(F32),
        )

    each_chip(place, keep, along, across, both, values)


def act_part(first):
    def act_rows(place, middle_grad, moved, weight, part, slope, give):
        rows = slice(first, first + give.shape[0])
        value = dot(middle_grad[rows, :], weight[1], NT)
        value += dot(moved[rows, :], weight[place[0]], NT)
        give[...] = (part[rows, :].astype(F32) + value * slope[rows, :]).astype(BF16)

    return act_rows


def over_chips(at, kept, *arrived):
    total = kept[at]
    for part in arrived:
        total += part[at].astype(F32)
    return total


def chips_sum(place, *refs):
    *parts, keep, give = refs
    top = place[TOP]
    keep[...] = over_chips(top, *parts)
    give[...] = over_chips(1 - top, *parts).astype(BF16)


def finish(
    place, one, one_got, two, two_got, mid_kept, mid_got, kept, got, dilated, point, result
):
    width = point.shape[1]
    dilated[1] = mid_kept[...] + wide(mid_got)
    dilated[place[0]] = kept[:, :width]
    dilated[2 - place[0]] = got[:, :width].astype(F32)
    point[...] = kept[:, width:] + got[:, width:].astype(F32)
    first = 0
    for own, theirs in ((one, one_got), (two, two_got)):
        rows = slice(first, first + own.shape[0])
        result[rows, :] = (wide(own) + wide(theirs)).astype(BF16)
        first += own.shape[0]


def body(features, dilated_weight, point_weight, track_weight, track_cotangent):
    samples, positions, channels = features.shape
    n_seq, n_sample, n_head = (lax.axis_size(a) for a in ("seq", "sample", "head"))
    dist = DILATION_STEP // positions
    if not (n_seq == 2 * dist and bits_of(n_seq) == 3 and n_sample == 2 and n_head == 2 and samples == 1):
        return general(features, dilated_weight, point_weight, track_weight, track_cotangent)
    rows = positions
    half = rows // 2
    width = dilated_weight.shape[2]
    tracks_here = track_weight.shape[1]
    piece = channels // n_sample
    block = channels // (n_seq * n_sample)
    seq, head, sample = lax.axis_index("seq"), lax.axis_index("head"), lax.axis_index("sample")
    place = jnp.stack(
        [jnp.where(seq < dist, 0, 2), head, sample, (seq >> 2) & 1, (seq >> 1) & 1, seq & 1]
    ).astype(jnp.int32)
    taps = jnp.transpose(dilated_weight, (1, 0, 2))
    feat = features.reshape(rows, channels)
    cotangent = track_cotangent.reshape(rows, tracks_here)
    pairs = [(i, (i + dist) % n_seq) for i in range(n_seq)]

    (own_piece,) = kernel_call(
        piece_of,
        [((piece, width), BF16)],
        [place, in_hbm(point_weight)],
        scratch=[pltpu.SemaphoreType.DMA],
        spaces={1: pltpu.HBM},
    )
    near = flip(own_piece, "head")
    far_track = flip(track_weight, "sample")
    acted, term = kernel_call(
        outer_term,
        [((rows, channels), BF16), ((rows, width), BF16)],
        [place, in_hbm(feat), in_hbm(taps)],
        [own_piece],
        scratch=[
            pltpu.VMEM((rows, channels), BF16),
            pltpu.VMEM((channels, width), BF16),
            pltpu.SemaphoreType.DMA((2, 3)),
        ],
        spaces={1: pltpu.HBM, 2: pltpu.HBM},
    )
    arrived = lax.ppermute(term, "seq", pairs)
    groups = n_seq

    turned = ((groups, block, rows), BF16)
    middle, acts, acts_given = kernel_call(
        middle_term,
        [((rows, width), F32), turned, turned],
        [place, acted, taps],
    )
    middle, middle_b = kernel_call(
        add_terms, [((rows, width), F32), ((rows, width), BF16)], [place, middle, arrived], [acts]
    )
    other_middle = flip(middle_b, "head")
    cut = piece // 3
    other_acts = flip(acts_given, "sample")
    hidden, block_part, slope, slope_feat, *pieces = kernel_call(
        own_hidden,
        [
            ((rows, width), BF16),
            ((rows, channels), F32),
            ((rows, width), F32),
            ((rows, channels), F32),
        ]
        + [((cut, width), BF16)] * (piece // cut),
        [place, middle, feat, point_weight, near],
    )
    points = [near] + [flip(part, "sample") for part in pieces]
    part, other_hidden, grad_kept, grad_given = kernel_call(
        tracks,
        [((rows, channels), BF16), ((rows, width), BF16), ((rows, width), F32), ((rows, width), BF16)],
        [
            place, block_part, other_middle, track_weight, far_track, cotangent, point_weight,
            *points,
        ],
        scratch=[
            pltpu.VMEM((n_sample, rows, piece), BF16),
            pltpu.VMEM((rows, tracks_here), BF16),
            pltpu.VMEM((n_sample, piece, n_head * width), BF16),
        ],
    )
    grad_got = flip(grad_given, "head")
    far_hidden = flip(hidden, "sample")

    def traded(kernel, columns, ins, after=(), scratch=()):
        shape = (2, block, columns)
        keep, *gives = kernel_call(
            kernel, [(shape, F32)] + [(shape, BF16)] * 3, [place, *ins], after, scratch
        )
        return keep, *[flip(value, "seq", step) for value, step in zip(gives, (1, 2, 3))]

    third = -(-groups // 3)
    outs, far_other, *outs_given = kernel_call(
        turn_parts,
        [turned, ((rows, width), BF16)]
        + [((min(third, groups - k), block, rows), BF16) for k in range(0, groups, third)],
        [place, part, flip(other_middle, "sample")],
        [far_hidden],
        scratch=[pltpu.VMEM((groups, block, rows), BF16)],
    )
    shares = ((groups, block, width), BF16)
    share, other_outs = kernel_call(
        other_points,
        [shares, turned],
        [place, outs, other_hidden, far_other] + [flip(piece, "sample") for piece in outs_given],
    )
    middle_grad, share = kernel_call(
        middle_grads,
        [((rows, width), BF16), shares],
        [place, grad_kept, grad_got, slope, share],
    )
    moved = lax.ppermute(middle_grad, "seq", pairs)
    share_got = flip(share, "head")
    cuts = [k * rows // 4 for k in range(5)]
    early = traded(
        middle_products,
        width,
        [acts, other_acts, middle_grad]
        + [flip(middle_grad[i:j], "sample") for i, j in zip(cuts[:-1], cuts[1:])],
        scratch=[pltpu.VMEM((rows, width), BF16)],
    )

    def halved(terms, columns, after=()):
        kept, give = kernel_call(
            chips_sum, [((block, columns), F32), ((block, columns), BF16)], [place, *terms], after
        )
        return kept, flip(give, "seq", n_seq // 2)

    mid_kept, mid_got = halved(early, width)
    late = traded(
        late_products,
        2 * width,
        [acts, other_acts, moved, outs, other_outs, hidden, far_hidden, share_got]
        + [flip(moved[k : k + half], "sample") for k in (0, half)],
        [mid_kept],
        scratch=[pltpu.VMEM((rows, width), BF16)],
    )
    ins = [place, middle_grad, moved, taps, part, slope_feat]
    (one,) = kernel_call(act_part(0), [((half, channels), BF16)], ins, [late[0]])
    (two,) = kernel_call(act_part(half), [((half, channels), BF16)], ins, [one])
    kept, got = halved(late, 2 * width, [two, mid_got])
    dilated_grad, point_grad, input_grad = kernel_call(
        finish,
        [((3, block, width), F32), ((block, width), F32), ((rows, channels), BF16)],
        [place, one, flip(one, "head"), two, flip(two, "head"), mid_kept, mid_got, kept, got],
    )
    dilated_grad = jnp.transpose(dilated_grad, (1, 0, 2))
    return (input_grad.reshape(samples, positions, channels), dilated_grad, point_grad)


def solution(mesh):
    placed = (
        P("sample", "seq", None),
        P(None, None, "head"),
        P(None, "head"),
        P("sample", "head"),
        P("sample", "seq", "head"),
    )
    return jax.shard_map(
        body,
        mesh=mesh,
        in_specs=placed,
        out_specs=(
            P("sample", "seq", None),
            P(("seq", "sample"), None, "head"),
            P(("seq", "sample"), "head"),
        ),
        check_vma=False,
    )
```

```python
import jax
import jax.numpy as jnp
from jax import lax
from jax.experimental import pallas as pl
from jax.experimental.pallas import tpu as pltpu
from jax.sharding import PartitionSpec as P

DILATION_STEP = 1024
BF16 = jnp.bfloat16
F32 = jnp.float32
VMEM = 24 * 2**20
LITTLE = pl.CostEstimate(flops=1, bytes_accessed=1, transcendentals=0)


def gelu_value(value):
    inner = 0.7978845608 * (value + 0.044715 * value * value * value)
    return 0.5 * value * (1.0 + jnp.tanh(inner))


def gelu_slope(value):
    inner = 0.7978845608 * (value + 0.044715 * value * value * value)
    tangent = jnp.tanh(inner)
    return 0.5 * (1.0 + tangent) + 0.5 * value * (1.0 - tangent * tangent) * 0.7978845608 * (
        1.0 + 3.0 * 0.044715 * value * value
    )


def dot(left, right, contract):
    return lax.dot_general(left, right, (contract, ((), ())), preferred_element_type=F32)


def flip(value, axis, step=1):
    count = lax.axis_size(axis)
    return lax.ppermute(value, axis, [(i, i ^ step) for i in range(count)])


def own_first(value, axis_at, bit):
    return (
        lax.dynamic_index_in_dim(value, bit, axis_at, keepdims=False),
        lax.dynamic_index_in_dim(value, 1 - bit, axis_at, keepdims=False),
    )


def in_order(own, other, bit, axis):
    first = jnp.where(bit == 0, own, other)
    second = jnp.where(bit == 0, other, own)
    return jnp.concatenate([first, second], axis=axis)


def bits_of(count):
    return count.bit_length() - 1


def general(features, dilated_weight, point_weight, track_weight, track_cotangent):
    samples, positions, channels = features.shape
    rows = samples * positions
    half = rows // 2
    width = dilated_weight.shape[2]
    n_seq, n_sample = lax.axis_size("seq"), lax.axis_size("sample")
    seq, head, sample = lax.axis_index("seq"), lax.axis_index("head"), lax.axis_index("sample")
    dist = DILATION_STEP // positions
    one_sided = n_seq == 2 * dist
    low = seq < dist
    taps = jnp.transpose(dilated_weight, (1, 0, 2))

    if one_sided:
        outer_weights = [lax.dynamic_index_in_dim(taps, jnp.where(low, 0, 2), 0, keepdims=False)]
        pairs = [(i, (i + dist) % n_seq) for i in range(n_seq)]
        forward, backward = [pairs], [pairs]
    else:
        outer_weights = [taps[0], taps[2]]
        up = [(i, i + dist) for i in range(n_seq - dist)]
        down = [(i + dist, i) for i in range(n_seq - dist)]
        forward, backward = [up, down], [down, up]
    count = len(outer_weights)

    whole_track = lax.all_gather(track_weight, "sample", axis=0, tiled=True)
    piece = channels // n_sample
    own_piece = lax.dynamic_slice_in_dim(point_weight, sample * piece, piece, 0)
    other_point = lax.all_gather(flip(own_piece, "head"), "sample", axis=0, tiled=True)

    feat = features.reshape(rows, channels)
    feat_wide = feat.astype(F32)
    activated = gelu_value(feat_wide).astype(BF16)
    sent = [dot(activated, weight, ((1,), (0,))).astype(BF16) for weight in outer_weights]
    arrived = [lax.ppermute(term, "seq", pairs) for term, pairs in zip(sent, forward)]
    middle = dot(activated, taps[1], ((1,), (0,)))
    for term in arrived:
        middle = middle + term.astype(F32)
    middle_b = middle.astype(BF16)
    other_middle = flip(middle_b, "head")
    hidden = gelu_value(middle).astype(BF16)
    other_hidden = gelu_value(other_middle.astype(F32)).astype(BF16)
    block_out = (
        feat_wide
        + dot(hidden, point_weight, ((1,), (1,)))
        + dot(other_hidden, other_point, ((1,), (1,)))
    ).astype(BF16)

    def rows_of(value, which):
        return lax.dynamic_slice_in_dim(value, which * half, half, 0)

    cotangent = track_cotangent.reshape(rows, whole_track.shape[1])

    def track_part(which):
        scores = dot(rows_of(block_out, which), whole_track, ((1,), (0,)))
        grad = (rows_of(cotangent, which).astype(F32) * jax.nn.sigmoid(scores)).astype(BF16)
        return dot(grad, whole_track, ((1,), (1,)))

    theirs = flip(track_part(1 - head).astype(BF16), "head")
    out_grad = track_part(head) + theirs.astype(F32)
    out_grad_b = out_grad.astype(BF16)
    other_out_grad = flip(out_grad_b, "head")

    grad_own = (
        dot(out_grad_b, point_weight, ((1,), (0,))) * gelu_slope(rows_of(middle, head))
    ).astype(BF16)
    grad_other = (
        dot(out_grad_b, other_point, ((1,), (0,)))
        * gelu_slope(rows_of(other_middle, head).astype(F32))
    ).astype(BF16)
    middle_grad = in_order(grad_own, flip(grad_other, "head"), head, 0)
    moved = []
    for pairs in backward:
        straight = lax.ppermute(grad_own, "seq", pairs)
        crossed = lax.ppermute(
            grad_other,
            ("seq", "head"),
            [(2 * i + k, 2 * j + 1 - k) for i, j in pairs for k in range(2)],
        )
        moved.append(in_order(straight, crossed, head, 0))

    act_part = dot(middle_grad, taps[1], ((1,), (1,)))
    for field, weight in zip(moved, outer_weights):
        act_part = act_part + dot(field, weight, ((1,), (1,)))
    act_theirs = flip(rows_of(act_part, 1 - head).astype(BF16), "head")
    act_grad = rows_of(act_part, head) + act_theirs.astype(F32)
    input_half = (out_grad + act_grad * gelu_slope(rows_of(feat_wide, head))).astype(BF16)
    input_grad = in_order(input_half, flip(input_half, "head"), head, 0)

    seq_bits = bits_of(n_seq)
    block = channels // (n_seq * n_sample)
    shape = (2,) * seq_bits + (n_sample, block)

    def halve(value, left, bit, keep_last=False):
        at = left.index(bit)
        if bit < 0:
            mine, give = own_first(value, at, sample)
            got = flip(give.astype(BF16), "sample")
        else:
            mine, give = own_first(value, at, (seq >> bit) & 1)
            got = flip(give.astype(BF16), "seq", 1 << bit)
        rest = [b for b in left if b != bit]
        return (mine, got, rest) if keep_last else (mine.astype(F32) + got.astype(F32), rest)

    def reduced(value, order, apart=False):
        left = list(range(seq_bits - 1, -1, -1)) + [-1]
        value = value.reshape(shape + value.shape[1:])
        for bit in order[:-1]:
            value, left = halve(value, left, bit)
            value = value.astype(BF16)
        mine, got, _ = halve(value, left, order[-1], True)
        if apart:
            return mine.astype(F32), got.astype(F32)
        return mine.astype(F32) + got.astype(F32)

    order_a = [-1] + list(range(seq_bits))
    order_b = [-1] + list(range(1, seq_bits - 1)) + [0, seq_bits - 1]
    whole_out_grad = in_order(out_grad_b, other_out_grad, head, 0)
    point_grad = reduced(dot(whole_out_grad, hidden, ((0,), (0,))), order_a)
    mid_tap = reduced(dot(activated, middle_grad, ((0,), (0,))), order_b)
    if one_sided:
        mine, got = reduced(dot(activated, moved[0], ((0,), (0,))), order_a, True)
        outer = [jnp.where(low, mine, got), jnp.where(low, got, mine)]
    else:
        outer = [reduced(dot(activated, field, ((0,), (0,))), order_a) for field in moved]
    dilated_grad = jnp.transpose(jnp.stack([outer[0], mid_tap, outer[1]]), (1, 0, 2))
    return (input_grad.reshape(samples, positions, channels), dilated_grad, point_grad)


def wide(ref):
    return ref[...].astype(F32)


def kernel_call(kernel, outs, ins, after=(), scratch=(), spaces={}):
    place, arrays = ins[0], list(ins[1:])
    in_specs = [pl.BlockSpec(memory_space=pltpu.SMEM)]
    in_specs += [
        pl.BlockSpec(memory_space=spaces.get(k + 1, pltpu.VMEM)) for k in range(len(arrays))
    ]
    number = len(arrays) + 1
    for value in after:
        arrays.append(value)
        in_specs.append(pl.BlockSpec(memory_space=pl.ANY))

    def run(*refs):
        given = refs[:number]
        kernel(*given, *refs[len(in_specs):])

    return pl.pallas_call(
        run,
        out_shape=[jax.ShapeDtypeStruct(s, d) for s, d in outs],
        in_specs=in_specs,
        out_specs=[pl.BlockSpec(memory_space=pltpu.VMEM)] * len(outs),
        scratch_shapes=list(scratch),
        compiler_params=pltpu.CompilerParams(vmem_limit_bytes=VMEM),
        cost_estimate=LITTLE,
        name=kernel.__name__,
    )(place, *arrays)


def in_hbm(value):
    return pltpu.with_memory_space_constraint(value, pltpu.HBM)


NN = ((1,), (0,))
NT = ((1,), (1,))
HEAD, SAMPLE, TOP, MID, LOWEST = 1, 2, 3, 4, 5


def outer_term(place, feat, taps, acted, term, rows, weight, sems):
    steps = sems.shape[1]
    depth = rows.shape[1] // steps
    parts = [pl.ds(k * depth, depth) for k in range(steps)]
    feats = [
        pltpu.make_async_copy(feat.at[:, part], rows.at[:, part], sems.at[0, k])
        for k, part in enumerate(parts)
    ]
    weights = [
        pltpu.make_async_copy(taps.at[place[0], part], weight.at[part], sems.at[1, k])
        for k, part in enumerate(parts)
    ]
    for pair in zip(feats, weights):
        for copy in pair:
            copy.start()
    total = None
    for copy, coming, part in zip(feats, weights, parts):
        copy.wait()
        act = gelu_value(rows[:, part].astype(F32)).astype(BF16)
        acted[:, part] = act
        coming.wait()
        value = dot(act, weight[part, :], NN)
        total = value if total is None else total + value
    term[...] = total.astype(BF16)


def piece_of(place, point, piece, sem):
    number = piece.shape[0]
    own = pl.ds(pl.multiple_of(place[SAMPLE] * number, number), number)
    copy = pltpu.make_async_copy(point.at[own], piece, sem)
    copy.start()
    copy.wait()


def middle_term(place, acted, weight, middle, kept, given):
    act = acted[...]
    middle[...] = dot(act, weight[1], NN)
    part_channels(place, act.T, kept, given)


def part_channels(place, turned, kept, given):
    groups, block, rows = kept.shape
    split = turned.reshape(groups, 2, block, rows)
    first = place[SAMPLE] == 0
    kept[...] = jnp.where(first, split[:, 0], split[:, 1])
    given[...] = jnp.where(first, split[:, 1], split[:, 0])


def add_terms(place, middle, arrived, total, sent):
    value = middle[...] + wide(arrived)
    total[...] = value
    sent[...] = value.astype(BF16)


def own_hidden(place, middle, feat, point, near, hidden, block, slope, slope_feat, *pieces):
    value = middle[...]
    hid = gelu_value(value).astype(BF16)
    hidden[...] = hid
    rows = wide(feat)
    block[...] = rows + dot(hid, point[...], NT)
    slope[...] = gelu_slope(value)
    slope_feat[...] = gelu_slope(rows)
    first = 0
    for piece in pieces:
        piece[...] = near[first : first + piece.shape[0]]
        first += piece.shape[0]


def tracks(place, block, other_middle, near, far, cotangent, point, *rest):
    *pieces, part, other_hidden, grad_kept, grad_given, block_b, grads, points = rest
    sample = place[SAMPLE]
    piece = block_b.shape[2]
    width = other_middle.shape[1]
    ahead = 0
    for other in pieces:
        number = other.shape[0]
        which, row = (sample, ahead) if ahead < piece else (1 - sample, ahead - piece)
        points[which, row : row + number, width:] = other[...]
        ahead += number
    hid = gelu_value(wide(other_middle)).astype(BF16)
    other_hidden[...] = hid
    for which in range(2):
        columns = slice(which * piece, (which + 1) * piece)
        points[which, :, :width] = point[columns, :]
        value = block[:, columns] + dot(hid, points[which, :, width:], NT)
        block_b[which] = value.astype(BF16)
    number = near.shape[1]
    tile = width if number % width == 0 else number
    for start in range(0, number, tile):
        columns = slice(start, start + tile)
        scores = dot(block_b[sample], near[:, columns], NN)
        scores += dot(block_b[1 - sample], far[:, columns], NN)
        grads[:, columns] = (wide(cotangent.at[:, columns]) * jax.nn.sigmoid(scores)).astype(BF16)
    both = 0.0
    for which, weight in ((sample, near), (1 - sample, far)):
        columns = pl.ds(pl.multiple_of(which * piece, piece), piece)
        value = dot(grads[...], weight[...], NT).astype(BF16)
        part[:, columns] = value
        both += dot(value, points[which], NN)
    grad_kept[...] = both[:, :width]
    grad_given[...] = both[:, width:].astype(BF16)


def turn_parts(place, part, far_middle, kept, far_hidden, *rest):
    *pieces, given = rest
    far_hidden[...] = gelu_value(wide(far_middle)).astype(BF16)
    part_channels(place, part[...].T, kept, given)
    first = 0
    for piece in pieces:
        piece[...] = given[first : first + piece.shape[0]]
        first += piece.shape[0]


def other_points(place, outs, other_hidden, far_other, *rest):
    *pieces, share, other_outs = rest
    joined(pieces, other_outs)
    groups, block, rows = outs.shape
    value = dot(outs[...].reshape(groups * block, rows), other_hidden[...], NN)
    value += dot(other_outs[...].reshape(groups * block, rows), far_other[...], NN)
    share[...] = value.astype(BF16).reshape(share.shape)


def middle_grads(place, kept, got, slope, share, middle_grad, give):
    middle_grad[...] = ((kept[...] + wide(got)) * slope[...]).astype(BF16)
    give[...] = share[...]


def joined(pieces, whole):
    first = 0
    for piece in pieces:
        whole[first : first + piece.shape[0]] = piece[...]
        first += piece.shape[0]


def each_chip(place, keep, along, across, both, values):
    mid, lowest = place[MID], place[LOWEST]
    for i, j, out in (
        (1 - mid, 1 - lowest, both),
        (1 - mid, lowest, along),
        (mid, 1 - lowest, across),
        (mid, lowest, keep),
    ):

        def left(ref):
            groups, at = ref.shape[0], 2 * i + j
            return jnp.concatenate([ref[at], ref[groups // 2 + at]], axis=0)

        for k, value in enumerate(values(left)):
            width = value.shape[1]
            shape = (2, out.shape[1], width)
            out[:, :, k * width : (k + 1) * width] = value.astype(out.dtype).reshape(shape)


def middle_products(place, acts, other_acts, field, *rest):
    *pieces, keep, both, across, along, other = rest
    joined(pieces, other)

    def values(left):
        return (dot(left(acts), field[...], NN) + dot(left(other_acts), other[...], NN),)

    each_chip(place, keep, along, across, both, values)


def late_products(
    place, acts, other_acts, moved, outs, other_outs, hidden, far_hidden, shares, first, second,
    keep, both, across, along, other_moved,
):
    joined((first, second), other_moved)

    def values(left):
        point = dot(left(outs), hidden[...], NN) + dot(left(other_outs), far_hidden[...], NN)
        return (
            dot(left(acts), moved[...], NN) + dot(left(other_acts), other_moved[...], NN),
            point + left(shares).astype(F32),
        )

    each_chip(place, keep, along, across, both, values)


def act_part(place, middle_grad, moved, weight, part, slope, *halves):
    value = dot(middle_grad[...], weight[1], NT) + dot(moved[...], weight[place[0]], NT)
    value = wide(part) + value * slope[...]
    first = 0
    for out in halves:
        out[...] = value[first : first + out.shape[0]].astype(BF16)
        first += out.shape[0]


def over_chips(at, kept, *arrived):
    total = kept[at]
    for part in arrived:
        total += part[at].astype(F32)
    return total


def chips_sum(place, *refs):
    *parts, keep, give = refs
    top = place[TOP]
    keep[...] = over_chips(top, *parts)
    give[...] = over_chips(1 - top, *parts).astype(BF16)


def finish(
    place, one, one_got, two, two_got, mid_kept, mid_got, kept, got, dilated, point, result
):
    width = point.shape[1]
    dilated[1] = mid_kept[...] + wide(mid_got)
    dilated[place[0]] = kept[:, :width]
    dilated[2 - place[0]] = got[:, :width].astype(F32)
    point[...] = kept[:, width:] + got[:, width:].astype(F32)
    first = 0
    for own, theirs in ((one, one_got), (two, two_got)):
        rows = slice(first, first + own.shape[0])
        result[rows, :] = (wide(own) + wide(theirs)).astype(BF16)
        first += own.shape[0]


def body(features, dilated_weight, point_weight, track_weight, track_cotangent):
    samples, positions, channels = features.shape
    n_seq, n_sample, n_head = (lax.axis_size(a) for a in ("seq", "sample", "head"))
    dist = DILATION_STEP // positions
    if not (n_seq == 2 * dist and bits_of(n_seq) == 3 and n_sample == 2 and n_head == 2 and samples == 1):
        return general(features, dilated_weight, point_weight, track_weight, track_cotangent)
    rows = positions
    half = rows // 2
    width = dilated_weight.shape[2]
    tracks_here = track_weight.shape[1]
    piece = channels // n_sample
    block = channels // (n_seq * n_sample)
    seq, head, sample = lax.axis_index("seq"), lax.axis_index("head"), lax.axis_index("sample")
    place = jnp.stack(
        [jnp.where(seq < dist, 0, 2), head, sample, (seq >> 2) & 1, (seq >> 1) & 1, seq & 1]
    ).astype(jnp.int32)
    taps = jnp.transpose(dilated_weight, (1, 0, 2))
    feat = features.reshape(rows, channels)
    cotangent = track_cotangent.reshape(rows, tracks_here)
    pairs = [(i, (i + dist) % n_seq) for i in range(n_seq)]

    (own_piece,) = kernel_call(
        piece_of,
        [((piece, width), BF16)],
        [place, in_hbm(point_weight)],
        scratch=[pltpu.SemaphoreType.DMA],
        spaces={1: pltpu.HBM},
    )
    near = flip(own_piece, "head")
    far_track = flip(track_weight, "sample")
    acted, term = kernel_call(
        outer_term,
        [((rows, channels), BF16), ((rows, width), BF16)],
        [place, in_hbm(feat), in_hbm(taps)],
        [own_piece],
        scratch=[
            pltpu.VMEM((rows, channels), BF16),
            pltpu.VMEM((channels, width), BF16),
            pltpu.SemaphoreType.DMA((2, 3)),
        ],
        spaces={1: pltpu.HBM, 2: pltpu.HBM},
    )
    arrived = lax.ppermute(term, "seq", pairs)
    groups = n_seq

    turned = ((groups, block, rows), BF16)
    middle, acts, acts_given = kernel_call(
        middle_term,
        [((rows, width), F32), turned, turned],
        [place, acted, taps],
    )
    middle, middle_b = kernel_call(
        add_terms, [((rows, width), F32), ((rows, width), BF16)], [place, middle, arrived], [acts]
    )
    other_middle = flip(middle_b, "head")
    cut = piece // 3
    other_acts = flip(acts_given, "sample")
    hidden, block_part, slope, slope_feat, *pieces = kernel_call(
        own_hidden,
        [
            ((rows, width), BF16),
            ((rows, channels), F32),
            ((rows, width), F32),
            ((rows, channels), F32),
        ]
        + [((cut, width), BF16)] * (piece // cut),
        [place, middle, feat, point_weight, near],
    )
    points = [near] + [flip(part, "sample") for part in pieces]
    part, other_hidden, grad_kept, grad_given = kernel_call(
        tracks,
        [((rows, channels), BF16), ((rows, width), BF16), ((rows, width), F32), ((rows, width), BF16)],
        [
            place, block_part, other_middle, track_weight, far_track, cotangent, point_weight,
            *points,
        ],
        scratch=[
            pltpu.VMEM((n_sample, rows, piece), BF16),
            pltpu.VMEM((rows, tracks_here), BF16),
            pltpu.VMEM((n_sample, piece, n_head * width), BF16),
        ],
    )
    grad_got = flip(grad_given, "head")
    far_hidden = flip(hidden, "sample")

    def traded(kernel, columns, ins, after=(), scratch=()):
        shape = (2, block, columns)
        keep, *gives = kernel_call(
            kernel, [(shape, F32)] + [(shape, BF16)] * 3, [place, *ins], after, scratch
        )
        return keep, *[flip(value, "seq", step) for value, step in zip(gives, (3, 1, 2))]

    third = -(-groups // 3)
    outs, far_other, *outs_given = kernel_call(
        turn_parts,
        [turned, ((rows, width), BF16)]
        + [((min(third, groups - k), block, rows), BF16) for k in range(0, groups, third)],
        [place, part, flip(other_middle, "sample")],
        [far_hidden],
        scratch=[pltpu.VMEM((groups, block, rows), BF16)],
    )
    shares = ((groups, block, width), BF16)
    share, other_outs = kernel_call(
        other_points,
        [shares, turned],
        [place, outs, other_hidden, far_other] + [flip(piece, "sample") for piece in outs_given],
    )
    middle_grad, share = kernel_call(
        middle_grads,
        [((rows, width), BF16), shares],
        [place, grad_kept, grad_got, slope, share],
    )
    moved = lax.ppermute(middle_grad, "seq", pairs)
    share_got = flip(share, "head")
    cuts = [k * rows // 4 for k in range(5)]
    early = traded(
        middle_products,
        width,
        [acts, other_acts, middle_grad]
        + [flip(middle_grad[i:j], "sample") for i, j in zip(cuts[:-1], cuts[1:])],
        scratch=[pltpu.VMEM((rows, width), BF16)],
    )

    def halved(terms, columns, after=()):
        kept, give = kernel_call(
            chips_sum, [((block, columns), F32), ((block, columns), BF16)], [place, *terms], after
        )
        return kept, flip(give, "seq", n_seq // 2)

    mid_kept, mid_got = halved(early, width)
    late = traded(
        late_products,
        2 * width,
        [acts, other_acts, moved, outs, other_outs, hidden, far_hidden, share_got]
        + [flip(moved[k : k + half], "sample") for k in (0, half)],
        [mid_kept],
        scratch=[pltpu.VMEM((rows, width), BF16)],
    )
    ins = [place, middle_grad, moved, taps, part, slope_feat]
    one, two = kernel_call(act_part, [((half, channels), BF16)] * 2, ins, [late[0]])
    kept, got = halved(late, 2 * width, [two, mid_got])
    dilated_grad, point_grad, input_grad = kernel_call(
        finish,
        [((3, block, width), F32), ((block, width), F32), ((rows, channels), BF16)],
        [place, one, flip(one, "head"), two, flip(two, "head"), mid_kept, mid_got, kept, got],
    )
    dilated_grad = jnp.transpose(dilated_grad, (1, 0, 2))
    return (input_grad.reshape(samples, positions, channels), dilated_grad, point_grad)


def solution(mesh):
    placed = (
        P("sample", "seq", None),
        P(None, None, "head"),
        P(None, "head"),
        P("sample", "head"),
        P("sample", "seq", "head"),
    )
    return jax.shard_map(
        body,
        mesh=mesh,
        in_specs=placed,
        out_specs=(
            P("sample", "seq", None),
            P(("seq", "sample"), None, "head"),
            P(("seq", "sample"), "head"),
        ),
        check_vma=False,
    )
```

```python
import jax
import jax.numpy as jnp
from jax import lax
from jax.experimental import pallas as pl
from jax.experimental.pallas import tpu as pltpu
from jax.sharding import PartitionSpec as P

DILATION_STEP = 1024
BF16 = jnp.bfloat16
F32 = jnp.float32
VMEM = 24 * 2**20
LITTLE = pl.CostEstimate(flops=1, bytes_accessed=1, transcendentals=0)


def gelu_value(value):
    inner = 0.7978845608 * (value + 0.044715 * value * value * value)
    return 0.5 * value * (1.0 + jnp.tanh(inner))


def gelu_slope(value):
    inner = 0.7978845608 * (value + 0.044715 * value * value * value)
    tangent = jnp.tanh(inner)
    return 0.5 * (1.0 + tangent) + 0.5 * value * (1.0 - tangent * tangent) * 0.7978845608 * (
        1.0 + 3.0 * 0.044715 * value * value
    )


def dot(left, right, contract):
    return lax.dot_general(left, right, (contract, ((), ())), preferred_element_type=F32)


def flip(value, axis, step=1):
    count = lax.axis_size(axis)
    return lax.ppermute(value, axis, [(i, i ^ step) for i in range(count)])


def own_first(value, axis_at, bit):
    return (
        lax.dynamic_index_in_dim(value, bit, axis_at, keepdims=False),
        lax.dynamic_index_in_dim(value, 1 - bit, axis_at, keepdims=False),
    )


def in_order(own, other, bit, axis):
    first = jnp.where(bit == 0, own, other)
    second = jnp.where(bit == 0, other, own)
    return jnp.concatenate([first, second], axis=axis)


def bits_of(count):
    return count.bit_length() - 1


def general(features, dilated_weight, point_weight, track_weight, track_cotangent):
    samples, positions, channels = features.shape
    rows = samples * positions
    half = rows // 2
    width = dilated_weight.shape[2]
    n_seq, n_sample = lax.axis_size("seq"), lax.axis_size("sample")
    seq, head, sample = lax.axis_index("seq"), lax.axis_index("head"), lax.axis_index("sample")
    dist = DILATION_STEP // positions
    one_sided = n_seq == 2 * dist
    low = seq < dist
    taps = jnp.transpose(dilated_weight, (1, 0, 2))

    if one_sided:
        outer_weights = [lax.dynamic_index_in_dim(taps, jnp.where(low, 0, 2), 0, keepdims=False)]
        pairs = [(i, (i + dist) % n_seq) for i in range(n_seq)]
        forward, backward = [pairs], [pairs]
    else:
        outer_weights = [taps[0], taps[2]]
        up = [(i, i + dist) for i in range(n_seq - dist)]
        down = [(i + dist, i) for i in range(n_seq - dist)]
        forward, backward = [up, down], [down, up]
    count = len(outer_weights)

    whole_track = lax.all_gather(track_weight, "sample", axis=0, tiled=True)
    piece = channels // n_sample
    own_piece = lax.dynamic_slice_in_dim(point_weight, sample * piece, piece, 0)
    other_point = lax.all_gather(flip(own_piece, "head"), "sample", axis=0, tiled=True)

    feat = features.reshape(rows, channels)
    feat_wide = feat.astype(F32)
    activated = gelu_value(feat_wide).astype(BF16)
    sent = [dot(activated, weight, ((1,), (0,))).astype(BF16) for weight in outer_weights]
    arrived = [lax.ppermute(term, "seq", pairs) for term, pairs in zip(sent, forward)]
    middle = dot(activated, taps[1], ((1,), (0,)))
    for term in arrived:
        middle = middle + term.astype(F32)
    middle_b = middle.astype(BF16)
    other_middle = flip(middle_b, "head")
    hidden = gelu_value(middle).astype(BF16)
    other_hidden = gelu_value(other_middle.astype(F32)).astype(BF16)
    block_out = (
        feat_wide
        + dot(hidden, point_weight, ((1,), (1,)))
        + dot(other_hidden, other_point, ((1,), (1,)))
    ).astype(BF16)

    def rows_of(value, which):
        return lax.dynamic_slice_in_dim(value, which * half, half, 0)

    cotangent = track_cotangent.reshape(rows, whole_track.shape[1])

    def track_part(which):
        scores = dot(rows_of(block_out, which), whole_track, ((1,), (0,)))
        grad = (rows_of(cotangent, which).astype(F32) * jax.nn.sigmoid(scores)).astype(BF16)
        return dot(grad, whole_track, ((1,), (1,)))

    theirs = flip(track_part(1 - head).astype(BF16), "head")
    out_grad = track_part(head) + theirs.astype(F32)
    out_grad_b = out_grad.astype(BF16)
    other_out_grad = flip(out_grad_b, "head")

    grad_own = (
        dot(out_grad_b, point_weight, ((1,), (0,))) * gelu_slope(rows_of(middle, head))
    ).astype(BF16)
    grad_other = (
        dot(out_grad_b, other_point, ((1,), (0,)))
        * gelu_slope(rows_of(other_middle, head).astype(F32))
    ).astype(BF16)
    middle_grad = in_order(grad_own, flip(grad_other, "head"), head, 0)
    moved = []
    for pairs in backward:
        straight = lax.ppermute(grad_own, "seq", pairs)
        crossed = lax.ppermute(
            grad_other,
            ("seq", "head"),
            [(2 * i + k, 2 * j + 1 - k) for i, j in pairs for k in range(2)],
        )
        moved.append(in_order(straight, crossed, head, 0))

    act_part = dot(middle_grad, taps[1], ((1,), (1,)))
    for field, weight in zip(moved, outer_weights):
        act_part = act_part + dot(field, weight, ((1,), (1,)))
    act_theirs = flip(rows_of(act_part, 1 - head).astype(BF16), "head")
    act_grad = rows_of(act_part, head) + act_theirs.astype(F32)
    input_half = (out_grad + act_grad * gelu_slope(rows_of(feat_wide, head))).astype(BF16)
    input_grad = in_order(input_half, flip(input_half, "head"), head, 0)

    seq_bits = bits_of(n_seq)
    block = channels // (n_seq * n_sample)
    shape = (2,) * seq_bits + (n_sample, block)

    def halve(value, left, bit, keep_last=False):
        at = left.index(bit)
        if bit < 0:
            mine, give = own_first(value, at, sample)
            got = flip(give.astype(BF16), "sample")
        else:
            mine, give = own_first(value, at, (seq >> bit) & 1)
            got = flip(give.astype(BF16), "seq", 1 << bit)
        rest = [b for b in left if b != bit]
        return (mine, got, rest) if keep_last else (mine.astype(F32) + got.astype(F32), rest)

    def reduced(value, order, apart=False):
        left = list(range(seq_bits - 1, -1, -1)) + [-1]
        value = value.reshape(shape + value.shape[1:])
        for bit in order[:-1]:
            value, left = halve(value, left, bit)
            value = value.astype(BF16)
        mine, got, _ = halve(value, left, order[-1], True)
        if apart:
            return mine.astype(F32), got.astype(F32)
        return mine.astype(F32) + got.astype(F32)

    order_a = [-1] + list(range(seq_bits))
    order_b = [-1] + list(range(1, seq_bits - 1)) + [0, seq_bits - 1]
    whole_out_grad = in_order(out_grad_b, other_out_grad, head, 0)
    point_grad = reduced(dot(whole_out_grad, hidden, ((0,), (0,))), order_a)
    mid_tap = reduced(dot(activated, middle_grad, ((0,), (0,))), order_b)
    if one_sided:
        mine, got = reduced(dot(activated, moved[0], ((0,), (0,))), order_a, True)
        outer = [jnp.where(low, mine, got), jnp.where(low, got, mine)]
    else:
        outer = [reduced(dot(activated, field, ((0,), (0,))), order_a) for field in moved]
    dilated_grad = jnp.transpose(jnp.stack([outer[0], mid_tap, outer[1]]), (1, 0, 2))
    return (input_grad.reshape(samples, positions, channels), dilated_grad, point_grad)


def wide(ref):
    return ref[...].astype(F32)


def kernel_call(kernel, outs, ins, after=(), scratch=(), spaces={}):
    place, arrays = ins[0], list(ins[1:])
    in_specs = [pl.BlockSpec(memory_space=pltpu.SMEM)]
    in_specs += [
        pl.BlockSpec(memory_space=spaces.get(k + 1, pltpu.VMEM)) for k in range(len(arrays))
    ]
    number = len(arrays) + 1
    for value in after:
        arrays.append(value)
        in_specs.append(pl.BlockSpec(memory_space=pl.ANY))

    def run(*refs):
        given = refs[:number]
        kernel(*given, *refs[len(in_specs):])

    return pl.pallas_call(
        run,
        out_shape=[jax.ShapeDtypeStruct(s, d) for s, d in outs],
        in_specs=in_specs,
        out_specs=[pl.BlockSpec(memory_space=pltpu.VMEM)] * len(outs),
        scratch_shapes=list(scratch),
        compiler_params=pltpu.CompilerParams(vmem_limit_bytes=VMEM),
        cost_estimate=LITTLE,
        name=kernel.__name__,
    )(place, *arrays)


def in_hbm(value):
    return pltpu.with_memory_space_constraint(value, pltpu.HBM)


NN = ((1,), (0,))
NT = ((1,), (1,))
HEAD, SAMPLE, TOP, MID, LOWEST = 1, 2, 3, 4, 5


def outer_term(place, feat, taps, acted, term, rows, weight, sems):
    steps = sems.shape[1]
    depth = rows.shape[1] // steps
    parts = [pl.ds(k * depth, depth) for k in range(steps)]
    feats = [
        pltpu.make_async_copy(feat.at[:, part], rows.at[:, part], sems.at[0, k])
        for k, part in enumerate(parts)
    ]
    weights = [
        pltpu.make_async_copy(taps.at[place[0], part], weight.at[part], sems.at[1, k])
        for k, part in enumerate(parts)
    ]
    for pair in zip(feats, weights):
        for copy in pair:
            copy.start()
    total = None
    for copy, coming, part in zip(feats, weights, parts):
        copy.wait()
        act = gelu_value(rows[:, part].astype(F32)).astype(BF16)
        acted[:, part] = act
        coming.wait()
        value = dot(act, weight[part, :], NN)
        total = value if total is None else total + value
    term[...] = total.astype(BF16)


def middle_term(place, acted, weight, middle, kept, given):
    act = acted[...]
    middle[...] = dot(act, weight[1], NN)
    part_channels(place, act.T, kept, given)


def part_channels(place, turned, kept, given):
    groups, block, rows = kept.shape
    split = turned.reshape(groups, 2, block, rows)
    first = place[SAMPLE] == 0
    kept[...] = jnp.where(first, split[:, 0], split[:, 1])
    given[...] = jnp.where(first, split[:, 1], split[:, 0])


def add_terms(place, middle, arrived, total, sent):
    value = middle[...] + wide(arrived)
    total[...] = value
    sent[...] = value.astype(BF16)


def own_hidden(place, middle, feat, point, near, hidden, block, slope, slope_feat, *pieces):
    value = middle[...]
    hid = gelu_value(value).astype(BF16)
    hidden[...] = hid
    rows = wide(feat)
    block[...] = rows + dot(hid, point[...], NT)
    slope[...] = gelu_slope(value)
    slope_feat[...] = gelu_slope(rows)
    first = 0
    for piece in pieces:
        piece[...] = near[first : first + piece.shape[0]]
        first += piece.shape[0]


def tracks(place, block, other_middle, near, far, cotangent, point, *rest):
    *pieces, part, other_hidden, grad_kept, grad_given, block_b, grads, points = rest
    sample = place[SAMPLE]
    piece = block_b.shape[2]
    width = other_middle.shape[1]
    ahead = 0
    for other in pieces:
        number = other.shape[0]
        which, row = (sample, ahead) if ahead < piece else (1 - sample, ahead - piece)
        points[which, row : row + number, width:] = other[...]
        ahead += number
    hid = gelu_value(wide(other_middle)).astype(BF16)
    other_hidden[...] = hid
    for which in range(2):
        columns = slice(which * piece, (which + 1) * piece)
        points[which, :, :width] = point[columns, :]
        value = block[:, columns] + dot(hid, points[which, :, width:], NT)
        block_b[which] = value.astype(BF16)
    number = near.shape[1]
    tile = width if number % width == 0 else number
    for start in range(0, number, tile):
        columns = slice(start, start + tile)
        scores = dot(block_b[sample], near[:, columns], NN)
        scores += dot(block_b[1 - sample], far[:, columns], NN)
        grads[:, columns] = (wide(cotangent.at[:, columns]) * jax.nn.sigmoid(scores)).astype(BF16)
    both = 0.0
    for which, weight in ((sample, near), (1 - sample, far)):
        columns = pl.ds(pl.multiple_of(which * piece, piece), piece)
        value = dot(grads[...], weight[...], NT).astype(BF16)
        part[:, columns] = value
        both += dot(value, points[which], NN)
    grad_kept[...] = both[:, :width]
    grad_given[...] = both[:, width:].astype(BF16)


def turn_parts(place, part, far_middle, kept, far_hidden, *rest):
    *pieces, given = rest
    far_hidden[...] = gelu_value(wide(far_middle)).astype(BF16)
    part_channels(place, part[...].T, kept, given)
    first = 0
    for piece in pieces:
        piece[...] = given[first : first + piece.shape[0]]
        first += piece.shape[0]


def other_points(place, outs, other_hidden, far_other, *rest):
    *pieces, share, other_outs = rest
    joined(pieces, other_outs)
    groups, block, rows = outs.shape
    value = dot(outs[...].reshape(groups * block, rows), other_hidden[...], NN)
    value += dot(other_outs[...].reshape(groups * block, rows), far_other[...], NN)
    share[...] = value.astype(BF16).reshape(share.shape)


def middle_grads(place, kept, got, slope, share, middle_grad, give):
    middle_grad[...] = ((kept[...] + wide(got)) * slope[...]).astype(BF16)
    give[...] = share[...]


def joined(pieces, whole):
    first = 0
    for piece in pieces:
        whole[first : first + piece.shape[0]] = piece[...]
        first += piece.shape[0]


def each_chip(place, keep, along, across, both, values):
    mid, lowest = place[MID], place[LOWEST]
    for i, j, out in (
        (1 - mid, 1 - lowest, both),
        (1 - mid, lowest, along),
        (mid, 1 - lowest, across),
        (mid, lowest, keep),
    ):

        def left(ref):
            groups, at = ref.shape[0], 2 * i + j
            return jnp.concatenate([ref[at], ref[groups // 2 + at]], axis=0)

        for k, value in enumerate(values(left)):
            width = value.shape[1]
            shape = (2, out.shape[1], width)
            out[:, :, k * width : (k + 1) * width] = value.astype(out.dtype).reshape(shape)


def middle_products(place, acts, other_acts, field, *rest):
    *pieces, keep, both, across, along, other = rest
    joined(pieces, other)

    def values(left):
        return (dot(left(acts), field[...], NN) + dot(left(other_acts), other[...], NN),)

    each_chip(place, keep, along, across, both, values)


def late_products(
    place, acts, other_acts, moved, outs, other_outs, hidden, far_hidden, shares, first, second,
    keep, both, across, along, other_moved,
):
    joined((first, second), other_moved)

    def values(left):
        point = dot(left(outs), hidden[...], NN) + dot(left(other_outs), far_hidden[...], NN)
        return (
            dot(left(acts), moved[...], NN) + dot(left(other_acts), other_moved[...], NN),
            point + left(shares).astype(F32),
        )

    each_chip(place, keep, along, across, both, values)


def act_part(place, middle_grad, moved, weight, part, slope, *halves):
    value = dot(middle_grad[...], weight[1], NT) + dot(moved[...], weight[place[0]], NT)
    value = wide(part) + value * slope[...]
    first = 0
    for out in halves:
        out[...] = value[first : first + out.shape[0]].astype(BF16)
        first += out.shape[0]


def over_chips(at, kept, *arrived):
    total = kept[at]
    for part in arrived:
        total += part[at].astype(F32)
    return total


def chips_sum(place, *refs):
    *parts, keep, give = refs
    top = place[TOP]
    keep[...] = over_chips(top, *parts)
    give[...] = over_chips(1 - top, *parts).astype(BF16)


def finish(
    place, one, one_got, two, two_got, mid_kept, mid_got, kept, got, dilated, point, result
):
    width = point.shape[1]
    dilated[1] = mid_kept[...] + wide(mid_got)
    dilated[place[0]] = kept[:, :width]
    dilated[2 - place[0]] = got[:, :width].astype(F32)
    point[...] = kept[:, width:] + got[:, width:].astype(F32)
    first = 0
    for own, theirs in ((one, one_got), (two, two_got)):
        rows = slice(first, first + own.shape[0])
        result[rows, :] = (wide(own) + wide(theirs)).astype(BF16)
        first += own.shape[0]


def body(features, dilated_weight, point_weight, track_weight, track_cotangent):
    samples, positions, channels = features.shape
    n_seq, n_sample, n_head = (lax.axis_size(a) for a in ("seq", "sample", "head"))
    dist = DILATION_STEP // positions
    if not (n_seq == 2 * dist and bits_of(n_seq) == 3 and n_sample == 2 and n_head == 2 and samples == 1):
        return general(features, dilated_weight, point_weight, track_weight, track_cotangent)
    rows = positions
    half = rows // 2
    width = dilated_weight.shape[2]
    tracks_here = track_weight.shape[1]
    piece = channels // n_sample
    block = channels // (n_seq * n_sample)
    seq, head, sample = lax.axis_index("seq"), lax.axis_index("head"), lax.axis_index("sample")
    place = jnp.stack(
        [jnp.where(seq < dist, 0, 2), head, sample, (seq >> 2) & 1, (seq >> 1) & 1, seq & 1]
    ).astype(jnp.int32)
    taps = jnp.transpose(dilated_weight, (1, 0, 2))
    feat = features.reshape(rows, channels)
    cotangent = track_cotangent.reshape(rows, tracks_here)
    pairs = [(i, (i + dist) % n_seq) for i in range(n_seq)]

    own_piece = lax.dynamic_slice_in_dim(point_weight, sample * piece, piece, 0)
    near = flip(own_piece, "head")
    far_track = flip(track_weight, "sample")
    acted, term = kernel_call(
        outer_term,
        [((rows, channels), BF16), ((rows, width), BF16)],
        [place, in_hbm(feat), in_hbm(taps)],
        [own_piece],
        scratch=[
            pltpu.VMEM((rows, channels), BF16),
            pltpu.VMEM((channels, width), BF16),
            pltpu.SemaphoreType.DMA((2, 6)),
        ],
        spaces={1: pltpu.HBM, 2: pltpu.HBM},
    )
    arrived = lax.ppermute(term, "seq", pairs)
    groups = n_seq

    turned = ((groups, block, rows), BF16)
    middle, acts, acts_given = kernel_call(
        middle_term,
        [((rows, width), F32), turned, turned],
        [place, acted, taps],
    )
    middle, middle_b = kernel_call(
        add_terms, [((rows, width), F32), ((rows, width), BF16)], [place, middle, arrived], [acts]
    )
    other_middle = flip(middle_b, "head")
    cut = piece // 3
    other_acts = flip(acts_given, "sample")
    hidden, block_part, slope, slope_feat, *pieces = kernel_call(
        own_hidden,
        [
            ((rows, width), BF16),
            ((rows, channels), F32),
            ((rows, width), F32),
            ((rows, channels), F32),
        ]
        + [((cut, width), BF16)] * (piece // cut),
        [place, middle, feat, point_weight, near],
    )
    points = [near] + [flip(part, "sample") for part in pieces]
    part, other_hidden, grad_kept, grad_given = kernel_call(
        tracks,
        [((rows, channels), BF16), ((rows, width), BF16), ((rows, width), F32), ((rows, width), BF16)],
        [
            place, block_part, other_middle, track_weight, far_track, cotangent, point_weight,
            *points,
        ],
        scratch=[
            pltpu.VMEM((n_sample, rows, piece), BF16),
            pltpu.VMEM((rows, tracks_here), BF16),
            pltpu.VMEM((n_sample, piece, n_head * width), BF16),
        ],
    )
    grad_got = flip(grad_given, "head")
    far_hidden = flip(hidden, "sample")

    def traded(kernel, columns, ins, after=(), scratch=()):
        shape = (2, block, columns)
        keep, *gives = kernel_call(
            kernel, [(shape, F32)] + [(shape, BF16)] * 3, [place, *ins], after, scratch
        )
        return keep, *[flip(value, "seq", step) for value, step in zip(gives, (3, 1, 2))]

    third = -(-groups // 3)
    outs, far_other, *outs_given = kernel_call(
        turn_parts,
        [turned, ((rows, width), BF16)]
        + [((min(third, groups - k), block, rows), BF16) for k in range(0, groups, third)],
        [place, part, flip(other_middle, "sample")],
        [far_hidden],
        scratch=[pltpu.VMEM((groups, block, rows), BF16)],
    )
    shares = ((groups, block, width), BF16)
    share, other_outs = kernel_call(
        other_points,
        [shares, turned],
        [place, outs, other_hidden, far_other] + [flip(piece, "sample") for piece in outs_given],
    )
    middle_grad, share = kernel_call(
        middle_grads,
        [((rows, width), BF16), shares],
        [place, grad_kept, grad_got, slope, share],
    )
    moved = lax.ppermute(middle_grad, "seq", pairs)
    share_got = flip(share, "head")
    cuts = [k * rows // 4 for k in range(5)]
    early = traded(
        middle_products,
        width,
        [acts, other_acts, middle_grad]
        + [flip(middle_grad[i:j], "sample") for i, j in zip(cuts[:-1], cuts[1:])],
        scratch=[pltpu.VMEM((rows, width), BF16)],
    )

    def halved(terms, columns, after=()):
        kept, give = kernel_call(
            chips_sum, [((block, columns), F32), ((block, columns), BF16)], [place, *terms], after
        )
        return kept, flip(give, "seq", n_seq // 2)

    mid_kept, mid_got = halved(early, width)
    late = traded(
        late_products,
        2 * width,
        [acts, other_acts, moved, outs, other_outs, hidden, far_hidden, share_got]
        + [flip(moved[k : k + half], "sample") for k in (0, half)],
        [mid_kept],
        scratch=[pltpu.VMEM((rows, width), BF16)],
    )
    ins = [place, middle_grad, moved, taps, part, slope_feat]
    one, two = kernel_call(act_part, [((half, channels), BF16)] * 2, ins, [late[0]])
    kept, got = halved(late, 2 * width, [two, mid_got])
    dilated_grad, point_grad, input_grad = kernel_call(
        finish,
        [((3, block, width), F32), ((block, width), F32), ((rows, channels), BF16)],
        [place, one, flip(one, "head"), two, flip(two, "head"), mid_kept, mid_got, kept, got],
    )
    dilated_grad = jnp.transpose(dilated_grad, (1, 0, 2))
    return (input_grad.reshape(samples, positions, channels), dilated_grad, point_grad)


def solution(mesh):
    placed = (
        P("sample", "seq", None),
        P(None, None, "head"),
        P(None, "head"),
        P("sample", "head"),
        P("sample", "seq", "head"),
    )
    return jax.shard_map(
        body,
        mesh=mesh,
        in_specs=placed,
        out_specs=(
            P("sample", "seq", None),
            P(("seq", "sample"), None, "head"),
            P(("seq", "sample"), "head"),
        ),
        check_vma=False,
    )
```

```python
import jax
import jax.numpy as jnp
from jax import lax
from jax.experimental import pallas as pl
from jax.experimental.pallas import tpu as pltpu
from jax.sharding import PartitionSpec as P

DILATION_STEP = 1024
BF16 = jnp.bfloat16
F32 = jnp.float32
VMEM = 24 * 2**20
LITTLE = pl.CostEstimate(flops=1, bytes_accessed=1, transcendentals=0)


def gelu_value(value):
    inner = 0.7978845608 * (value + 0.044715 * value * value * value)
    return 0.5 * value * (1.0 + jnp.tanh(inner))


def gelu_slope(value):
    inner = 0.7978845608 * (value + 0.044715 * value * value * value)
    tangent = jnp.tanh(inner)
    return 0.5 * (1.0 + tangent) + 0.5 * value * (1.0 - tangent * tangent) * 0.7978845608 * (
        1.0 + 3.0 * 0.044715 * value * value
    )


def dot(left, right, contract):
    return lax.dot_general(left, right, (contract, ((), ())), preferred_element_type=F32)


def flip(value, axis, step=1):
    count = lax.axis_size(axis)
    return lax.ppermute(value, axis, [(i, i ^ step) for i in range(count)])


def own_first(value, axis_at, bit):
    return (
        lax.dynamic_index_in_dim(value, bit, axis_at, keepdims=False),
        lax.dynamic_index_in_dim(value, 1 - bit, axis_at, keepdims=False),
    )


def in_order(own, other, bit, axis):
    first = jnp.where(bit == 0, own, other)
    second = jnp.where(bit == 0, other, own)
    return jnp.concatenate([first, second], axis=axis)


def bits_of(count):
    return count.bit_length() - 1


def general(features, dilated_weight, point_weight, track_weight, track_cotangent):
    samples, positions, channels = features.shape
    rows = samples * positions
    half = rows // 2
    width = dilated_weight.shape[2]
    n_seq, n_sample = lax.axis_size("seq"), lax.axis_size("sample")
    seq, head, sample = lax.axis_index("seq"), lax.axis_index("head"), lax.axis_index("sample")
    dist = DILATION_STEP // positions
    one_sided = n_seq == 2 * dist
    low = seq < dist
    taps = jnp.transpose(dilated_weight, (1, 0, 2))

    if one_sided:
        outer_weights = [lax.dynamic_index_in_dim(taps, jnp.where(low, 0, 2), 0, keepdims=False)]
        pairs = [(i, (i + dist) % n_seq) for i in range(n_seq)]
        forward, backward = [pairs], [pairs]
    else:
        outer_weights = [taps[0], taps[2]]
        up = [(i, i + dist) for i in range(n_seq - dist)]
        down = [(i + dist, i) for i in range(n_seq - dist)]
        forward, backward = [up, down], [down, up]
    count = len(outer_weights)

    whole_track = lax.all_gather(track_weight, "sample", axis=0, tiled=True)
    piece = channels // n_sample
    own_piece = lax.dynamic_slice_in_dim(point_weight, sample * piece, piece, 0)
    other_point = lax.all_gather(flip(own_piece, "head"), "sample", axis=0, tiled=True)

    feat = features.reshape(rows, channels)
    feat_wide = feat.astype(F32)
    activated = gelu_value(feat_wide).astype(BF16)
    sent = [dot(activated, weight, ((1,), (0,))).astype(BF16) for weight in outer_weights]
    arrived = [lax.ppermute(term, "seq", pairs) for term, pairs in zip(sent, forward)]
    middle = dot(activated, taps[1], ((1,), (0,)))
    for term in arrived:
        middle = middle + term.astype(F32)
    middle_b = middle.astype(BF16)
    other_middle = flip(middle_b, "head")
    hidden = gelu_value(middle).astype(BF16)
    other_hidden = gelu_value(other_middle.astype(F32)).astype(BF16)
    block_out = (
        feat_wide
        + dot(hidden, point_weight, ((1,), (1,)))
        + dot(other_hidden, other_point, ((1,), (1,)))
    ).astype(BF16)

    def rows_of(value, which):
        return lax.dynamic_slice_in_dim(value, which * half, half, 0)

    cotangent = track_cotangent.reshape(rows, whole_track.shape[1])

    def track_part(which):
        scores = dot(rows_of(block_out, which), whole_track, ((1,), (0,)))
        grad = (rows_of(cotangent, which).astype(F32) * jax.nn.sigmoid(scores)).astype(BF16)
        return dot(grad, whole_track, ((1,), (1,)))

    theirs = flip(track_part(1 - head).astype(BF16), "head")
    out_grad = track_part(head) + theirs.astype(F32)
    out_grad_b = out_grad.astype(BF16)
    other_out_grad = flip(out_grad_b, "head")

    grad_own = (
        dot(out_grad_b, point_weight, ((1,), (0,))) * gelu_slope(rows_of(middle, head))
    ).astype(BF16)
    grad_other = (
        dot(out_grad_b, other_point, ((1,), (0,)))
        * gelu_slope(rows_of(other_middle, head).astype(F32))
    ).astype(BF16)
    middle_grad = in_order(grad_own, flip(grad_other, "head"), head, 0)
    moved = []
    for pairs in backward:
        straight = lax.ppermute(grad_own, "seq", pairs)
        crossed = lax.ppermute(
            grad_other,
            ("seq", "head"),
            [(2 * i + k, 2 * j + 1 - k) for i, j in pairs for k in range(2)],
        )
        moved.append(in_order(straight, crossed, head, 0))

    act_part = dot(middle_grad, taps[1], ((1,), (1,)))
    for field, weight in zip(moved, outer_weights):
        act_part = act_part + dot(field, weight, ((1,), (1,)))
    act_theirs = flip(rows_of(act_part, 1 - head).astype(BF16), "head")
    act_grad = rows_of(act_part, head) + act_theirs.astype(F32)
    input_half = (out_grad + act_grad * gelu_slope(rows_of(feat_wide, head))).astype(BF16)
    input_grad = in_order(input_half, flip(input_half, "head"), head, 0)

    seq_bits = bits_of(n_seq)
    block = channels // (n_seq * n_sample)
    shape = (2,) * seq_bits + (n_sample, block)

    def halve(value, left, bit, keep_last=False):
        at = left.index(bit)
        if bit < 0:
            mine, give = own_first(value, at, sample)
            got = flip(give.astype(BF16), "sample")
        else:
            mine, give = own_first(value, at, (seq >> bit) & 1)
            got = flip(give.astype(BF16), "seq", 1 << bit)
        rest = [b for b in left if b != bit]
        return (mine, got, rest) if keep_last else (mine.astype(F32) + got.astype(F32), rest)

    def reduced(value, order, apart=False):
        left = list(range(seq_bits - 1, -1, -1)) + [-1]
        value = value.reshape(shape + value.shape[1:])
        for bit in order[:-1]:
            value, left = halve(value, left, bit)
            value = value.astype(BF16)
        mine, got, _ = halve(value, left, order[-1], True)
        if apart:
            return mine.astype(F32), got.astype(F32)
        return mine.astype(F32) + got.astype(F32)

    order_a = [-1] + list(range(seq_bits))
    order_b = [-1] + list(range(1, seq_bits - 1)) + [0, seq_bits - 1]
    whole_out_grad = in_order(out_grad_b, other_out_grad, head, 0)
    point_grad = reduced(dot(whole_out_grad, hidden, ((0,), (0,))), order_a)
    mid_tap = reduced(dot(activated, middle_grad, ((0,), (0,))), order_b)
    if one_sided:
        mine, got = reduced(dot(activated, moved[0], ((0,), (0,))), order_a, True)
        outer = [jnp.where(low, mine, got), jnp.where(low, got, mine)]
    else:
        outer = [reduced(dot(activated, field, ((0,), (0,))), order_a) for field in moved]
    dilated_grad = jnp.transpose(jnp.stack([outer[0], mid_tap, outer[1]]), (1, 0, 2))
    return (input_grad.reshape(samples, positions, channels), dilated_grad, point_grad)


def wide(ref):
    return ref[...].astype(F32)


def kernel_call(kernel, outs, ins, after=(), scratch=(), spaces={}):
    place, arrays = ins[0], list(ins[1:])
    in_specs = [pl.BlockSpec(memory_space=pltpu.SMEM)]
    in_specs += [
        pl.BlockSpec(memory_space=spaces.get(k + 1, pltpu.VMEM)) for k in range(len(arrays))
    ]
    number = len(arrays) + 1
    for value in after:
        arrays.append(value)
        in_specs.append(pl.BlockSpec(memory_space=pl.ANY))

    def run(*refs):
        given = refs[:number]
        kernel(*given, *refs[len(in_specs):])

    return pl.pallas_call(
        run,
        out_shape=[jax.ShapeDtypeStruct(s, d) for s, d in outs],
        in_specs=in_specs,
        out_specs=[pl.BlockSpec(memory_space=pltpu.VMEM)] * len(outs),
        scratch_shapes=list(scratch),
        compiler_params=pltpu.CompilerParams(vmem_limit_bytes=VMEM),
        cost_estimate=LITTLE,
        name=kernel.__name__,
    )(place, *arrays)


def in_hbm(value):
    return pltpu.with_memory_space_constraint(value, pltpu.HBM)


NN = ((1,), (0,))
NT = ((1,), (1,))
HEAD, SAMPLE, TOP, MID, LOWEST = 1, 2, 3, 4, 5


def outer_term(place, feat, taps, acted, term, rows, weight, sems):
    steps = sems.shape[1]
    depth = rows.shape[1] // steps
    parts = [pl.ds(k * depth, depth) for k in range(steps)]
    feats = [
        pltpu.make_async_copy(feat.at[:, part], rows.at[:, part], sems.at[0, k])
        for k, part in enumerate(parts)
    ]
    weights = [
        pltpu.make_async_copy(taps.at[place[0], part], weight.at[part], sems.at[1, k])
        for k, part in enumerate(parts)
    ]
    for pair in zip(feats, weights):
        for copy in pair:
            copy.start()
    total = None
    for copy, coming, part in zip(feats, weights, parts):
        copy.wait()
        act = gelu_value(rows[:, part].astype(F32)).astype(BF16)
        acted[:, part] = act
        coming.wait()
        value = dot(act, weight[part, :], NN)
        total = value if total is None else total + value
    term[...] = total.astype(BF16)


def middle_term(place, acted, weight, middle, kept, given):
    act = acted[...]
    middle[...] = dot(act, weight[1], NN)
    part_channels(place, act.T, kept, given)


def part_channels(place, turned, kept, given):
    groups, block, rows = kept.shape
    split = turned.reshape(groups, 2, block, rows)
    first = place[SAMPLE] == 0
    kept[...] = jnp.where(first, split[:, 0], split[:, 1])
    given[...] = jnp.where(first, split[:, 1], split[:, 0])


def add_terms(place, middle, arrived, total, sent):
    value = middle[...] + wide(arrived)
    total[...] = value
    sent[...] = value.astype(BF16)


def own_hidden(place, middle, feat, point, near, hidden, block, slope, slope_feat, *pieces):
    value = middle[...]
    hid = gelu_value(value).astype(BF16)
    hidden[...] = hid
    rows = wide(feat)
    block[...] = rows + dot(hid, point[...], NT)
    slope[...] = gelu_slope(value)
    slope_feat[...] = gelu_slope(rows)
    first = 0
    for piece in pieces:
        piece[...] = near[first : first + piece.shape[0]]
        first += piece.shape[0]


def tracks(place, block, other_middle, near, far, cotangent, point, *rest):
    *pieces, part, other_hidden, grad_kept, grad_given, block_b, grads, points = rest
    sample = place[SAMPLE]
    piece = block_b.shape[2]
    width = other_middle.shape[1]
    ahead = 0
    for other in pieces:
        number = other.shape[0]
        which, row = (sample, ahead) if ahead < piece else (1 - sample, ahead - piece)
        points[which, row : row + number, width:] = other[...]
        ahead += number
    hid = gelu_value(wide(other_middle)).astype(BF16)
    other_hidden[...] = hid
    for which in range(2):
        columns = slice(which * piece, (which + 1) * piece)
        points[which, :, :width] = point[columns, :]
        value = block[:, columns] + dot(hid, points[which, :, width:], NT)
        block_b[which] = value.astype(BF16)
    number = near.shape[1]
    tile = width if number % width == 0 else number
    for start in range(0, number, tile):
        columns = slice(start, start + tile)
        scores = dot(block_b[sample], near[:, columns], NN)
        scores += dot(block_b[1 - sample], far[:, columns], NN)
        grads[:, columns] = (wide(cotangent.at[:, columns]) * jax.nn.sigmoid(scores)).astype(BF16)
    both = 0.0
    for which, weight in ((sample, near), (1 - sample, far)):
        columns = pl.ds(pl.multiple_of(which * piece, piece), piece)
        value = dot(grads[...], weight[...], NT).astype(BF16)
        part[:, columns] = value
        both += dot(value, points[which], NN)
    grad_kept[...] = both[:, :width]
    grad_given[...] = both[:, width:].astype(BF16)


def turn_parts(place, part, far_middle, kept, far_hidden, *rest):
    *pieces, given = rest
    far_hidden[...] = gelu_value(wide(far_middle)).astype(BF16)
    part_channels(place, part[...].T, kept, given)
    first = 0
    for piece in pieces:
        piece[...] = given[first : first + piece.shape[0]]
        first += piece.shape[0]


def other_points(place, outs, other_hidden, far_other, *rest):
    *pieces, share, other_outs = rest
    joined(pieces, other_outs)
    groups, block, rows = outs.shape
    value = dot(outs[...].reshape(groups * block, rows), other_hidden[...], NN)
    value += dot(other_outs[...].reshape(groups * block, rows), far_other[...], NN)
    share[...] = value.astype(BF16).reshape(share.shape)


def middle_grads(place, kept, got, slope, share, middle_grad, give):
    middle_grad[...] = ((kept[...] + wide(got)) * slope[...]).astype(BF16)
    give[...] = share[...]


def joined(pieces, whole):
    first = 0
    for piece in pieces:
        whole[first : first + piece.shape[0]] = piece[...]
        first += piece.shape[0]


def each_chip(place, keep, along, across, both, values):
    mid, lowest = place[MID], place[LOWEST]
    for i, j, out in (
        (1 - mid, 1 - lowest, both),
        (1 - mid, lowest, along),
        (mid, 1 - lowest, across),
        (mid, lowest, keep),
    ):

        def left(ref):
            groups, at = ref.shape[0], 2 * i + j
            return jnp.concatenate([ref[at], ref[groups // 2 + at]], axis=0)

        for k, value in enumerate(values(left)):
            width = value.shape[1]
            shape = (2, out.shape[1], width)
            out[:, :, k * width : (k + 1) * width] = value.astype(out.dtype).reshape(shape)


def middle_products(place, acts, other_acts, field, *rest):
    *pieces, keep, both, across, along, other = rest
    joined(pieces, other)

    def values(left):
        return (dot(left(acts), field[...], NN) + dot(left(other_acts), other[...], NN),)

    each_chip(place, keep, along, across, both, values)


def late_products(
    place, acts, other_acts, moved, outs, other_outs, hidden, far_hidden, shares, first, second,
    keep, both, across, along, other_moved,
):
    joined((first, second), other_moved)

    def values(left):
        point = dot(left(outs), hidden[...], NN) + dot(left(other_outs), far_hidden[...], NN)
        return (
            dot(left(acts), moved[...], NN) + dot(left(other_acts), other_moved[...], NN),
            point + left(shares).astype(F32),
        )

    each_chip(place, keep, along, across, both, values)


def act_part(place, middle_grad, moved, weight, part, slope, *halves):
    value = dot(middle_grad[...], weight[1], NT) + dot(moved[...], weight[place[0]], NT)
    value = wide(part) + value * slope[...]
    first = 0
    for out in halves:
        out[...] = value[first : first + out.shape[0]].astype(BF16)
        first += out.shape[0]


def over_chips(at, kept, *arrived):
    total = kept[at]
    for part in arrived:
        total += part[at].astype(F32)
    return total


def chips_sum(place, *refs):
    *parts, keep, give = refs
    top = place[TOP]
    keep[...] = over_chips(top, *parts)
    give[...] = over_chips(1 - top, *parts).astype(BF16)


def finish(
    place, one, one_got, two, two_got, mid_kept, mid_got, kept, got, dilated, point, result
):
    width = point.shape[1]
    dilated[1] = mid_kept[...] + wide(mid_got)
    dilated[place[0]] = kept[:, :width]
    dilated[2 - place[0]] = got[:, :width].astype(F32)
    point[...] = kept[:, width:] + got[:, width:].astype(F32)
    first = 0
    for own, theirs in ((one, one_got), (two, two_got)):
        rows = slice(first, first + own.shape[0])
        result[rows, :] = (wide(own) + wide(theirs)).astype(BF16)
        first += own.shape[0]


def body(features, dilated_weight, point_weight, track_weight, track_cotangent):
    samples, positions, channels = features.shape
    n_seq, n_sample, n_head = (lax.axis_size(a) for a in ("seq", "sample", "head"))
    dist = DILATION_STEP // positions
    if not (n_seq == 2 * dist and bits_of(n_seq) == 3 and n_sample == 2 and n_head == 2 and samples == 1):
        return general(features, dilated_weight, point_weight, track_weight, track_cotangent)
    rows = positions
    half = rows // 2
    width = dilated_weight.shape[2]
    tracks_here = track_weight.shape[1]
    piece = channels // n_sample
    block = channels // (n_seq * n_sample)
    seq, head, sample = lax.axis_index("seq"), lax.axis_index("head"), lax.axis_index("sample")
    place = jnp.stack(
        [jnp.where(seq < dist, 0, 2), head, sample, (seq >> 2) & 1, (seq >> 1) & 1, seq & 1]
    ).astype(jnp.int32)
    taps = jnp.transpose(dilated_weight, (1, 0, 2))
    feat = features.reshape(rows, channels)
    cotangent = track_cotangent.reshape(rows, tracks_here)
    pairs = [(i, (i + dist) % n_seq) for i in range(n_seq)]

    own_piece = lax.dynamic_slice_in_dim(point_weight, sample * piece, piece, 0)
    near = flip(own_piece, "head")
    far_track = flip(track_weight, "sample")
    acted, term = kernel_call(
        outer_term,
        [((rows, channels), BF16), ((rows, width), BF16)],
        [place, in_hbm(feat), in_hbm(taps)],
        [own_piece],
        scratch=[
            pltpu.VMEM((rows, channels), BF16),
            pltpu.VMEM((channels, width), BF16),
            pltpu.SemaphoreType.DMA((2, 3)),
        ],
        spaces={1: pltpu.HBM, 2: pltpu.HBM},
    )
    arrived = lax.ppermute(term, "seq", pairs)
    groups = n_seq

    turned = ((groups, block, rows), BF16)
    middle, acts, acts_given = kernel_call(
        middle_term,
        [((rows, width), F32), turned, turned],
        [place, acted, taps],
    )
    middle, middle_b = kernel_call(
        add_terms, [((rows, width), F32), ((rows, width), BF16)], [place, middle, arrived], [acts]
    )
    other_middle = flip(middle_b, "head")
    cut = piece // 3
    other_acts = flip(acts_given, "sample")
    hidden, block_part, slope, slope_feat, *pieces = kernel_call(
        own_hidden,
        [
            ((rows, width), BF16),
            ((rows, channels), F32),
            ((rows, width), F32),
            ((rows, channels), F32),
        ]
        + [((cut, width), BF16)] * (piece // cut),
        [place, middle, feat, point_weight, near],
    )
    points = [near] + [flip(part, "sample") for part in pieces]
    part, other_hidden, grad_kept, grad_given = kernel_call(
        tracks,
        [((rows, channels), BF16), ((rows, width), BF16), ((rows, width), F32), ((rows, width), BF16)],
        [
            place, block_part, other_middle, track_weight, far_track, cotangent, point_weight,
            *points,
        ],
        scratch=[
            pltpu.VMEM((n_sample, rows, piece), BF16),
            pltpu.VMEM((rows, tracks_here), BF16),
            pltpu.VMEM((n_sample, piece, n_head * width), BF16),
        ],
    )
    grad_got = flip(grad_given, "head")
    far_hidden = flip(hidden, "sample")

    def traded(kernel, columns, ins, after=(), scratch=()):
        shape = (2, block, columns)
        keep, *gives = kernel_call(
            kernel, [(shape, F32)] + [(shape, BF16)] * 3, [place, *ins], after, scratch
        )
        return keep, *[flip(value, "seq", step) for value, step in zip(gives, (3, 1, 2))]

    third = -(-groups // 3)
    outs, far_other, *outs_given = kernel_call(
        turn_parts,
        [turned, ((rows, width), BF16)]
        + [((min(third, groups - k), block, rows), BF16) for k in range(0, groups, third)],
        [place, part, flip(other_middle, "sample")],
        [far_hidden],
        scratch=[pltpu.VMEM((groups, block, rows), BF16)],
    )
    shares = ((groups, block, width), BF16)
    share, other_outs = kernel_call(
        other_points,
        [shares, turned],
        [place, outs, other_hidden, far_other] + [flip(piece, "sample") for piece in outs_given],
    )
    middle_grad, share = kernel_call(
        middle_grads,
        [((rows, width), BF16), shares],
        [place, grad_kept, grad_got, slope, share],
    )
    moved = lax.ppermute(middle_grad, "seq", pairs)
    share_got = flip(share, "head")
    cuts = [k * rows // 4 for k in range(5)]
    early = traded(
        middle_products,
        width,
        [acts, other_acts, middle_grad]
        + [flip(middle_grad[i:j], "sample") for i, j in zip(cuts[:-1], cuts[1:])],
        scratch=[pltpu.VMEM((rows, width), BF16)],
    )

    def halved(terms, columns, after=()):
        kept, give = kernel_call(
            chips_sum, [((block, columns), F32), ((block, columns), BF16)], [place, *terms], after
        )
        return kept, flip(give, "seq", n_seq // 2)

    mid_kept, mid_got = halved(early, width)
    late = traded(
        late_products,
        2 * width,
        [acts, other_acts, moved, outs, other_outs, hidden, far_hidden, share_got]
        + [flip(moved[k : k + half], "sample") for k in (0, half)],
        [mid_kept],
        scratch=[pltpu.VMEM((rows, width), BF16)],
    )
    ins = [place, middle_grad, moved, taps, part, slope_feat]
    one, two = kernel_call(act_part, [((half, channels), BF16)] * 2, ins, [late[0]])
    kept, got = halved(late, 2 * width, [two, mid_got])
    dilated_grad, point_grad, input_grad = kernel_call(
        finish,
        [((3, block, width), F32), ((block, width), F32), ((rows, channels), BF16)],
        [place, one, flip(one, "head"), two, flip(two, "head"), mid_kept, mid_got, kept, got],
    )
    dilated_grad = jnp.transpose(dilated_grad, (1, 0, 2))
    return (input_grad.reshape(samples, positions, channels), dilated_grad, point_grad)


def solution(mesh):
    placed = (
        P("sample", "seq", None),
        P(None, None, "head"),
        P(None, "head"),
        P("sample", "head"),
        P("sample", "seq", "head"),
    )
    return jax.shard_map(
        body,
        mesh=mesh,
        in_specs=placed,
        out_specs=(
            P("sample", "seq", None),
            P(("seq", "sample"), None, "head"),
            P(("seq", "sample"), "head"),
        ),
        check_vma=False,
    )
```

```python
import jax
import jax.numpy as jnp
from jax import lax
from jax.experimental import pallas as pl
from jax.experimental.pallas import tpu as pltpu
from jax.sharding import PartitionSpec as P

DILATION_STEP = 1024
BF16 = jnp.bfloat16
F32 = jnp.float32
VMEM = 24 * 2**20
LITTLE = pl.CostEstimate(flops=1, bytes_accessed=1, transcendentals=0)


def gelu_value(value):
    inner = 0.7978845608 * (value + 0.044715 * value * value * value)
    return 0.5 * value * (1.0 + jnp.tanh(inner))


def gelu_slope(value):
    inner = 0.7978845608 * (value + 0.044715 * value * value * value)
    tangent = jnp.tanh(inner)
    return 0.5 * (1.0 + tangent) + 0.5 * value * (1.0 - tangent * tangent) * 0.7978845608 * (
        1.0 + 3.0 * 0.044715 * value * value
    )


def dot(left, right, contract):
    return lax.dot_general(left, right, (contract, ((), ())), preferred_element_type=F32)


def flip(value, axis, step=1):
    count = lax.axis_size(axis)
    return lax.ppermute(value, axis, [(i, i ^ step) for i in range(count)])


def own_first(value, axis_at, bit):
    return (
        lax.dynamic_index_in_dim(value, bit, axis_at, keepdims=False),
        lax.dynamic_index_in_dim(value, 1 - bit, axis_at, keepdims=False),
    )


def in_order(own, other, bit, axis):
    first = jnp.where(bit == 0, own, other)
    second = jnp.where(bit == 0, other, own)
    return jnp.concatenate([first, second], axis=axis)


def bits_of(count):
    return count.bit_length() - 1


def general(features, dilated_weight, point_weight, track_weight, track_cotangent):
    samples, positions, channels = features.shape
    rows = samples * positions
    half = rows // 2
    width = dilated_weight.shape[2]
    n_seq, n_sample = lax.axis_size("seq"), lax.axis_size("sample")
    seq, head, sample = lax.axis_index("seq"), lax.axis_index("head"), lax.axis_index("sample")
    dist = DILATION_STEP // positions
    one_sided = n_seq == 2 * dist
    low = seq < dist
    taps = jnp.transpose(dilated_weight, (1, 0, 2))

    if one_sided:
        outer_weights = [lax.dynamic_index_in_dim(taps, jnp.where(low, 0, 2), 0, keepdims=False)]
        pairs = [(i, (i + dist) % n_seq) for i in range(n_seq)]
        forward, backward = [pairs], [pairs]
    else:
        outer_weights = [taps[0], taps[2]]
        up = [(i, i + dist) for i in range(n_seq - dist)]
        down = [(i + dist, i) for i in range(n_seq - dist)]
        forward, backward = [up, down], [down, up]
    count = len(outer_weights)

    whole_track = lax.all_gather(track_weight, "sample", axis=0, tiled=True)
    piece = channels // n_sample
    own_piece = lax.dynamic_slice_in_dim(point_weight, sample * piece, piece, 0)
    other_point = lax.all_gather(flip(own_piece, "head"), "sample", axis=0, tiled=True)

    feat = features.reshape(rows, channels)
    feat_wide = feat.astype(F32)
    activated = gelu_value(feat_wide).astype(BF16)
    sent = [dot(activated, weight, ((1,), (0,))).astype(BF16) for weight in outer_weights]
    arrived = [lax.ppermute(term, "seq", pairs) for term, pairs in zip(sent, forward)]
    middle = dot(activated, taps[1], ((1,), (0,)))
    for term in arrived:
        middle = middle + term.astype(F32)
    middle_b = middle.astype(BF16)
    other_middle = flip(middle_b, "head")
    hidden = gelu_value(middle).astype(BF16)
    other_hidden = gelu_value(other_middle.astype(F32)).astype(BF16)
    block_out = (
        feat_wide
        + dot(hidden, point_weight, ((1,), (1,)))
        + dot(other_hidden, other_point, ((1,), (1,)))
    ).astype(BF16)

    def rows_of(value, which):
        return lax.dynamic_slice_in_dim(value, which * half, half, 0)

    cotangent = track_cotangent.reshape(rows, whole_track.shape[1])

    def track_part(which):
        scores = dot(rows_of(block_out, which), whole_track, ((1,), (0,)))
        grad = (rows_of(cotangent, which).astype(F32) * jax.nn.sigmoid(scores)).astype(BF16)
        return dot(grad, whole_track, ((1,), (1,)))

    theirs = flip(track_part(1 - head).astype(BF16), "head")
    out_grad = track_part(head) + theirs.astype(F32)
    out_grad_b = out_grad.astype(BF16)
    other_out_grad = flip(out_grad_b, "head")

    grad_own = (
        dot(out_grad_b, point_weight, ((1,), (0,))) * gelu_slope(rows_of(middle, head))
    ).astype(BF16)
    grad_other = (
        dot(out_grad_b, other_point, ((1,), (0,)))
        * gelu_slope(rows_of(other_middle, head).astype(F32))
    ).astype(BF16)
    middle_grad = in_order(grad_own, flip(grad_other, "head"), head, 0)
    moved = []
    for pairs in backward:
        straight = lax.ppermute(grad_own, "seq", pairs)
        crossed = lax.ppermute(
            grad_other,
            ("seq", "head"),
            [(2 * i + k, 2 * j + 1 - k) for i, j in pairs for k in range(2)],
        )
        moved.append(in_order(straight, crossed, head, 0))

    act_part = dot(middle_grad, taps[1], ((1,), (1,)))
    for field, weight in zip(moved, outer_weights):
        act_part = act_part + dot(field, weight, ((1,), (1,)))
    act_theirs = flip(rows_of(act_part, 1 - head).astype(BF16), "head")
    act_grad = rows_of(act_part, head) + act_theirs.astype(F32)
    input_half = (out_grad + act_grad * gelu_slope(rows_of(feat_wide, head))).astype(BF16)
    input_grad = in_order(input_half, flip(input_half, "head"), head, 0)

    seq_bits = bits_of(n_seq)
    block = channels // (n_seq * n_sample)
    shape = (2,) * seq_bits + (n_sample, block)

    def halve(value, left, bit, keep_last=False):
        at = left.index(bit)
        if bit < 0:
            mine, give = own_first(value, at, sample)
            got = flip(give.astype(BF16), "sample")
        else:
            mine, give = own_first(value, at, (seq >> bit) & 1)
            got = flip(give.astype(BF16), "seq", 1 << bit)
        rest = [b for b in left if b != bit]
        return (mine, got, rest) if keep_last else (mine.astype(F32) + got.astype(F32), rest)

    def reduced(value, order, apart=False):
        left = list(range(seq_bits - 1, -1, -1)) + [-1]
        value = value.reshape(shape + value.shape[1:])
        for bit in order[:-1]:
            value, left = halve(value, left, bit)
            value = value.astype(BF16)
        mine, got, _ = halve(value, left, order[-1], True)
        if apart:
            return mine.astype(F32), got.astype(F32)
        return mine.astype(F32) + got.astype(F32)

    order_a = [-1] + list(range(seq_bits))
    order_b = [-1] + list(range(1, seq_bits - 1)) + [0, seq_bits - 1]
    whole_out_grad = in_order(out_grad_b, other_out_grad, head, 0)
    point_grad = reduced(dot(whole_out_grad, hidden, ((0,), (0,))), order_a)
    mid_tap = reduced(dot(activated, middle_grad, ((0,), (0,))), order_b)
    if one_sided:
        mine, got = reduced(dot(activated, moved[0], ((0,), (0,))), order_a, True)
        outer = [jnp.where(low, mine, got), jnp.where(low, got, mine)]
    else:
        outer = [reduced(dot(activated, field, ((0,), (0,))), order_a) for field in moved]
    dilated_grad = jnp.transpose(jnp.stack([outer[0], mid_tap, outer[1]]), (1, 0, 2))
    return (input_grad.reshape(samples, positions, channels), dilated_grad, point_grad)


def wide(ref):
    return ref[...].astype(F32)


def kernel_call(kernel, outs, ins, after=(), scratch=(), spaces={}):
    place, arrays = ins[0], list(ins[1:])
    in_specs = [pl.BlockSpec(memory_space=pltpu.SMEM)]
    in_specs += [
        pl.BlockSpec(memory_space=spaces.get(k + 1, pltpu.VMEM)) for k in range(len(arrays))
    ]
    number = len(arrays) + 1
    for value in after:
        arrays.append(value)
        in_specs.append(pl.BlockSpec(memory_space=pl.ANY))

    def run(*refs):
        given = refs[:number]
        kernel(*given, *refs[len(in_specs):])

    return pl.pallas_call(
        run,
        out_shape=[jax.ShapeDtypeStruct(s, d) for s, d in outs],
        in_specs=in_specs,
        out_specs=[pl.BlockSpec(memory_space=pltpu.VMEM)] * len(outs),
        scratch_shapes=list(scratch),
        compiler_params=pltpu.CompilerParams(vmem_limit_bytes=VMEM),
        cost_estimate=LITTLE,
        name=kernel.__name__,
    )(place, *arrays)


def in_hbm(value):
    return pltpu.with_memory_space_constraint(value, pltpu.HBM)


NN = ((1,), (0,))
NT = ((1,), (1,))
HEAD, SAMPLE, TOP, MID, LOWEST = 1, 2, 3, 4, 5


def outer_term(place, feat, taps, acted, term, rows, weight, sems):
    steps = sems.shape[1]
    depth = rows.shape[1] // steps
    parts = [pl.ds(k * depth, depth) for k in range(steps)]
    feats = [
        pltpu.make_async_copy(feat.at[:, part], rows.at[:, part], sems.at[0, k])
        for k, part in enumerate(parts)
    ]
    weights = [
        pltpu.make_async_copy(taps.at[place[0], part], weight.at[part], sems.at[1, k])
        for k, part in enumerate(parts)
    ]
    for pair in zip(feats, weights):
        for copy in pair:
            copy.start()
    total = None
    for copy, coming, part in zip(feats, weights, parts):
        copy.wait()
        act = gelu_value(rows[:, part].astype(F32)).astype(BF16)
        acted[:, part] = act
        coming.wait()
        value = dot(act, weight[part, :], NN)
        total = value if total is None else total + value
    term[...] = total.astype(BF16)


def middle_term(place, acted, weight, middle, kept, given):
    act = acted[...]
    middle[...] = dot(act, weight[1], NN)
    part_channels(place, act.T, kept, given)


def part_channels(place, turned, kept, given):
    groups, block, rows = kept.shape
    split = turned.reshape(groups, 2, block, rows)
    first = place[SAMPLE] == 0
    kept[...] = jnp.where(first, split[:, 0], split[:, 1])
    given[...] = jnp.where(first, split[:, 1], split[:, 0])


def add_terms(place, middle, arrived, total, sent):
    value = middle[...] + wide(arrived)
    total[...] = value
    sent[...] = value.astype(BF16)


def own_hidden(place, middle, feat, point, near, hidden, block, slope, slope_feat, *pieces):
    value = middle[...]
    hid = gelu_value(value).astype(BF16)
    hidden[...] = hid
    rows = wide(feat)
    block[...] = rows + dot(hid, point[...], NT)
    slope[...] = gelu_slope(value)
    slope_feat[...] = gelu_slope(rows)
    first = 0
    for piece in pieces:
        piece[...] = near[first : first + piece.shape[0]]
        first += piece.shape[0]


def tracks(place, block, other_middle, near, far, cotangent, point, *rest):
    *pieces, part, other_hidden, grad_kept, grad_given, block_b, grads, points = rest
    sample = place[SAMPLE]
    piece = block_b.shape[2]
    width = other_middle.shape[1]
    ahead = 0
    for other in pieces:
        number = other.shape[0]
        which, row = (sample, ahead) if ahead < piece else (1 - sample, ahead - piece)
        points[which, row : row + number, width:] = other[...]
        ahead += number
    hid = gelu_value(wide(other_middle)).astype(BF16)
    other_hidden[...] = hid
    for which in range(2):
        columns = slice(which * piece, (which + 1) * piece)
        points[which, :, :width] = point[columns, :]
        value = block[:, columns] + dot(hid, points[which, :, width:], NT)
        block_b[which] = value.astype(BF16)
    number = near.shape[1]
    tile = width if number % width == 0 else number
    for start in range(0, number, tile):
        columns = slice(start, start + tile)
        scores = dot(block_b[sample], near[:, columns], NN)
        scores += dot(block_b[1 - sample], far[:, columns], NN)
        grads[:, columns] = (wide(cotangent.at[:, columns]) * jax.nn.sigmoid(scores)).astype(BF16)
    both = 0.0
    for which, weight in ((sample, near), (1 - sample, far)):
        columns = pl.ds(pl.multiple_of(which * piece, piece), piece)
        value = dot(grads[...], weight[...], NT).astype(BF16)
        part[:, columns] = value
        both += dot(value, points[which], NN)
    grad_kept[...] = both[:, :width]
    grad_given[...] = both[:, width:].astype(BF16)


def turn_parts(place, part, far_middle, kept, far_hidden, *rest):
    *pieces, given = rest
    far_hidden[...] = gelu_value(wide(far_middle)).astype(BF16)
    part_channels(place, part[...].T, kept, given)
    first = 0
    for piece in pieces:
        piece[...] = given[first : first + piece.shape[0]]
        first += piece.shape[0]


def other_points(place, outs, other_hidden, far_other, *rest):
    *pieces, share, other_outs = rest
    joined(pieces, other_outs)
    groups, block, rows = outs.shape
    value = dot(outs[...].reshape(groups * block, rows), other_hidden[...], NN)
    value += dot(other_outs[...].reshape(groups * block, rows), far_other[...], NN)
    share[...] = value.astype(BF16).reshape(share.shape)


def middle_grads(place, kept, got, slope, share, middle_grad, give):
    middle_grad[...] = ((kept[...] + wide(got)) * slope[...]).astype(BF16)
    give[...] = share[...]


def joined(pieces, whole):
    first = 0
    for piece in pieces:
        whole[first : first + piece.shape[0]] = piece[...]
        first += piece.shape[0]


def each_chip(place, keep, along, across, both, values):
    mid, lowest = place[MID], place[LOWEST]
    for i, j, out in (
        (1 - mid, 1 - lowest, both),
        (1 - mid, lowest, along),
        (mid, 1 - lowest, across),
        (mid, lowest, keep),
    ):

        def left(ref):
            groups, at = ref.shape[0], 2 * i + j
            return jnp.concatenate([ref[at], ref[groups // 2 + at]], axis=0)

        for k, value in enumerate(values(left)):
            width = value.shape[1]
            shape = (2, out.shape[1], width)
            out[:, :, k * width : (k + 1) * width] = value.astype(out.dtype).reshape(shape)


def middle_products(place, acts, other_acts, field, *rest):
    *pieces, keep, both, across, along, other = rest
    joined(pieces, other)

    def values(left):
        return (dot(left(acts), field[...], NN) + dot(left(other_acts), other[...], NN),)

    each_chip(place, keep, along, across, both, values)


def late_products(
    place, acts, other_acts, moved, outs, other_outs, hidden, far_hidden, shares, first, second,
    keep, both, across, along, other_moved,
):
    joined((first, second), other_moved)

    def values(left):
        point = dot(left(outs), hidden[...], NN) + dot(left(other_outs), far_hidden[...], NN)
        return (
            dot(left(acts), moved[...], NN) + dot(left(other_acts), other_moved[...], NN),
            point + left(shares).astype(F32),
        )

    each_chip(place, keep, along, across, both, values)


def act_part(place, middle_grad, moved, weight, part, slope, *halves):
    value = dot(middle_grad[...], weight[1], NT) + dot(moved[...], weight[place[0]], NT)
    value = wide(part) + value * slope[...]
    first = 0
    for out in halves:
        out[...] = value[first : first + out.shape[0]].astype(BF16)
        first += out.shape[0]


def over_chips(at, kept, *arrived):
    total = kept[at]
    for part in arrived:
        total += part[at].astype(F32)
    return total


def chips_sum(place, *refs):
    *parts, keep, give = refs
    top = place[TOP]
    keep[...] = over_chips(top, *parts)
    give[...] = over_chips(1 - top, *parts).astype(BF16)


def finish(
    place, one, one_got, two, two_got, mid_kept, mid_got, kept, got, dilated, point, result
):
    width = point.shape[1]
    dilated[1] = mid_kept[...] + wide(mid_got)
    dilated[place[0]] = kept[:, :width]
    dilated[2 - place[0]] = got[:, :width].astype(F32)
    point[...] = kept[:, width:] + got[:, width:].astype(F32)
    first = 0
    for own, theirs in ((one, one_got), (two, two_got)):
        rows = slice(first, first + own.shape[0])
        result[rows, :] = (wide(own) + wide(theirs)).astype(BF16)
        first += own.shape[0]


def body(features, dilated_weight, point_weight, track_weight, track_cotangent):
    samples, positions, channels = features.shape
    n_seq, n_sample, n_head = (lax.axis_size(a) for a in ("seq", "sample", "head"))
    dist = DILATION_STEP // positions
    if not (n_seq == 2 * dist and bits_of(n_seq) == 3 and n_sample == 2 and n_head == 2 and samples == 1):
        return general(features, dilated_weight, point_weight, track_weight, track_cotangent)
    rows = positions
    half = rows // 2
    width = dilated_weight.shape[2]
    tracks_here = track_weight.shape[1]
    piece = channels // n_sample
    block = channels // (n_seq * n_sample)
    seq, head, sample = lax.axis_index("seq"), lax.axis_index("head"), lax.axis_index("sample")
    place = jnp.stack(
        [jnp.where(seq < dist, 0, 2), head, sample, (seq >> 2) & 1, (seq >> 1) & 1, seq & 1]
    ).astype(jnp.int32)
    taps = jnp.transpose(dilated_weight, (1, 0, 2))
    feat = features.reshape(rows, channels)
    cotangent = track_cotangent.reshape(rows, tracks_here)
    pairs = [(i, (i + dist) % n_seq) for i in range(n_seq)]

    own_piece = lax.dynamic_slice_in_dim(point_weight, sample * piece, piece, 0)
    near = flip(own_piece, "head")
    far_track = flip(track_weight, "sample")
    acted, term = kernel_call(
        outer_term,
        [((rows, channels), BF16), ((rows, width), BF16)],
        [place, in_hbm(feat), in_hbm(taps)],
        [own_piece],
        scratch=[
            pltpu.VMEM((rows, channels), BF16),
            pltpu.VMEM((channels, width), BF16),
            pltpu.SemaphoreType.DMA((2, 2)),
        ],
        spaces={1: pltpu.HBM, 2: pltpu.HBM},
    )
    arrived = lax.ppermute(term, "seq", pairs)
    groups = n_seq

    turned = ((groups, block, rows), BF16)
    middle, acts, acts_given = kernel_call(
        middle_term,
        [((rows, width), F32), turned, turned],
        [place, acted, taps],
    )
    middle, middle_b = kernel_call(
        add_terms, [((rows, width), F32), ((rows, width), BF16)], [place, middle, arrived], [acts]
    )
    other_middle = flip(middle_b, "head")
    cut = piece // 3
    other_acts = flip(acts_given, "sample")
    hidden, block_part, slope, slope_feat, *pieces = kernel_call(
        own_hidden,
        [
            ((rows, width), BF16),
            ((rows, channels), F32),
            ((rows, width), F32),
            ((rows, channels), F32),
        ]
        + [((cut, width), BF16)] * (piece // cut),
        [place, middle, feat, point_weight, near],
    )
    points = [near] + [flip(part, "sample") for part in pieces]
    part, other_hidden, grad_kept, grad_given = kernel_call(
        tracks,
        [((rows, channels), BF16), ((rows, width), BF16), ((rows, width), F32), ((rows, width), BF16)],
        [
            place, block_part, other_middle, track_weight, far_track, cotangent, point_weight,
            *points,
        ],
        scratch=[
            pltpu.VMEM((n_sample, rows, piece), BF16),
            pltpu.VMEM((rows, tracks_here), BF16),
            pltpu.VMEM((n_sample, piece, n_head * width), BF16),
        ],
    )
    grad_got = flip(grad_given, "head")
    far_hidden = flip(hidden, "sample")

    def traded(kernel, columns, ins, after=(), scratch=()):
        shape = (2, block, columns)
        keep, *gives = kernel_call(
            kernel, [(shape, F32)] + [(shape, BF16)] * 3, [place, *ins], after, scratch
        )
        return keep, *[flip(value, "seq", step) for value, step in zip(gives, (3, 1, 2))]

    third = -(-groups // 3)
    outs, far_other, *outs_given = kernel_call(
        turn_parts,
        [turned, ((rows, width), BF16)]
        + [((min(third, groups - k), block, rows), BF16) for k in range(0, groups, third)],
        [place, part, flip(other_middle, "sample")],
        [far_hidden],
        scratch=[pltpu.VMEM((groups, block, rows), BF16)],
    )
    shares = ((groups, block, width), BF16)
    share, other_outs = kernel_call(
        other_points,
        [shares, turned],
        [place, outs, other_hidden, far_other] + [flip(piece, "sample") for piece in outs_given],
    )
    middle_grad, share = kernel_call(
        middle_grads,
        [((rows, width), BF16), shares],
        [place, grad_kept, grad_got, slope, share],
    )
    moved = lax.ppermute(middle_grad, "seq", pairs)
    share_got = flip(share, "head")
    cuts = [k * rows // 4 for k in range(5)]
    early = traded(
        middle_products,
        width,
        [acts, other_acts, middle_grad]
        + [flip(middle_grad[i:j], "sample") for i, j in zip(cuts[:-1], cuts[1:])],
        scratch=[pltpu.VMEM((rows, width), BF16)],
    )

    def halved(terms, columns, after=()):
        kept, give = kernel_call(
            chips_sum, [((block, columns), F32), ((block, columns), BF16)], [place, *terms], after
        )
        return kept, flip(give, "seq", n_seq // 2)

    mid_kept, mid_got = halved(early, width)
    late = traded(
        late_products,
        2 * width,
        [acts, other_acts, moved, outs, other_outs, hidden, far_hidden, share_got]
        + [flip(moved[k : k + half], "sample") for k in (0, half)],
        [mid_kept],
        scratch=[pltpu.VMEM((rows, width), BF16)],
    )
    ins = [place, middle_grad, moved, taps, part, slope_feat]
    one, two = kernel_call(act_part, [((half, channels), BF16)] * 2, ins, [late[0]])
    kept, got = halved(late, 2 * width, [two, mid_got])
    dilated_grad, point_grad, input_grad = kernel_call(
        finish,
        [((3, block, width), F32), ((block, width), F32), ((rows, channels), BF16)],
        [place, one, flip(one, "head"), two, flip(two, "head"), mid_kept, mid_got, kept, got],
    )
    dilated_grad = jnp.transpose(dilated_grad, (1, 0, 2))
    return (input_grad.reshape(samples, positions, channels), dilated_grad, point_grad)


def solution(mesh):
    placed = (
        P("sample", "seq", None),
        P(None, None, "head"),
        P(None, "head"),
        P("sample", "head"),
        P("sample", "seq", "head"),
    )
    return jax.shard_map(
        body,
        mesh=mesh,
        in_specs=placed,
        out_specs=(
            P("sample", "seq", None),
            P(("seq", "sample"), None, "head"),
            P(("seq", "sample"), "head"),
        ),
        check_vma=False,
    )
```
